32 devices in a mesh: shift: 2 (over y), row: 8 (over z, x), col: 2 (over core).
Axes of the slice: x: 2, y: 2, z: 4, core: 2. Of those that a mesh axis runs over, the one named last changes fastest.
Arguments:
- krylov_basis: float32 [128, 3, 8, 8, 128], P('shift', None, 'row', 'col'), parts along dimension 0, may hold values from -4000 to 4000, as said below
- regions: int32 [8, 8, 128], P('row', 'col'), may hold values from 0 to 7
- mu_table: float32 [8], replicated, may hold values from 0.5 to 2
- eps_table: float32 [8], replicated, may hold values from 1 to 4
- shift_value: float32 [2], P('shift'), parts along dimension 0, may hold values from 0.5 to 2
Outputs:
- orthonormal: float32 [128, 3, 8, 8, 128], P('shift', None, 'row', 'col'), parts along dimension 0
- upper_factor: float32 [128, 64], P('shift'), parts along dimension 0
- applied: float32 [128, 3, 8, 8, 128], P('shift', None, 'row', 'col'), parts along dimension 0
- projected: float32 [128, 64], P('shift'), parts along dimension 0
The draws below stay inside these ranges and needn't reach their ends.
There are 2 independent parts, one for each index of `shift`. The reference program is written for one: setup_inputs(seed, part) draws one part's arguments, and reference() takes and returns one part's arrays. A program takes and returns all parts, laid end to end along the dimension named above; an argument that names none is the same for every part. Nothing has to cross between parts.
Inputs may be any that keep to these rules, and one draw needn't show every extreme that they name: `krylov_basis`: Real-valued entries.
All inputs are finite; a program needn't handle non-finite values.
Results may differ from the reference program's by a relative error of at most 0.000071.
Values sent between devices are 32-bit elements; how exact they have to be, the bound alone decides.
No kernel may reach another device: no remote copies, remote signals or barrier semaphores. Data moves between devices by JAX's collectives and lax.ppermute only.
A program may use at most 64 MiB of HBM per device.

```python
import math
import jax
import jax.numpy as jnp
from jax import lax

COLS = 64
NZ = 128
NREG = 8
NX = 8
NY = 8


def draw_krylov_basis(key, part):
    keys = jax.random.split(jax.random.fold_in(key, 71), 3)
    normals = jnp.clip(jax.random.normal(keys[0], (COLS, 3, NX, NY, NZ), jnp.float32), -5.0, 5.0)
    position = jnp.arange(NX, dtype=jnp.float32) / max(NX - 1, 1)
    along_x = 1.0 + 2.0 * position
    column_scale = jnp.exp(jax.random.uniform(keys[1], (COLS,), jnp.float32) * jnp.log(10.0))
    cell_scale = jnp.exp(jax.random.uniform(keys[2], (3, NX, NY, NZ), jnp.float32) * jnp.log(3.0))
    scaled = normals * column_scale[:, None, None, None, None]
    scaled = scaled * along_x[None, None, :, None, None] * cell_scale[None]
    return scaled.astype(jnp.float32)


def set_ends(entries, stream_key, low, high):
    longest = entries.shape.index(max(entries.shape))
    spots = []
    for shift in (0, 1):
        where = [jax.random.randint(jax.random.fold_in(stream_key, axis), (), 0, length) for axis, length in enumerate(entries.shape)]
        where[longest] = (where[longest] + shift) % entries.shape[longest]
        spots.append(tuple(where))
    return entries.at[spots[0]].set(low).at[spots[1]].set(high)


def setup_inputs(seed: int = 0, part: int = 0) -> dict:
    streams_of = jax.random.split(jax.random.key(seed), 6)
    part_keys = jax.random.split(jax.random.fold_in(streams_of[5], part), 6)
    return {
        "krylov_basis": draw_krylov_basis(jax.random.fold_in(jax.random.fold_in(streams_of[5], part), 71), part),
        "regions": set_ends(jax.random.randint(streams_of[1], (NX, NY, NZ), 0, NREG), jax.random.fold_in(streams_of[1], 1), 0, NREG - 1).astype(jnp.int32),
        "mu_table": jnp.clip(jnp.exp(jax.random.uniform(streams_of[2], (NREG,), jnp.float32, math.log(0.5), math.log(2.0))), 0.5, 2.0),
        "eps_table": jnp.clip(jnp.exp(jax.random.uniform(streams_of[3], (NREG,), jnp.float32, math.log(1.0), math.log(4.0))), 1.0, 4.0),
        "shift_value": jnp.clip(jax.random.uniform(part_keys[4], (1,), jnp.float32, 0.5, 2.0), 0.5, 2.0),
    }


def forward_z(values):
    return jnp.pad(values[..., 1:], ((0, 0), (0, 0), (0, 0), (0, 1))) - values

def backward_z(values):
    return values - jnp.pad(values[..., :-1], ((0, 0), (0, 0), (0, 0), (1, 0)))

def operator_block(padded_field, coupling, permittivity, shift_scalar):
    cells_x = padded_field.shape[2] - 2
    cells_y = padded_field.shape[3] - 2
    field_x = padded_field[:, 0]
    field_y = padded_field[:, 1]
    field_z = padded_field[:, 2]

    def corner_part(values):
        return values[:, :cells_x + 1, :cells_y + 1]

    def forward_x(values):
        return values[:, 1:cells_x + 2, :cells_y + 1] - corner_part(values)

    def forward_y(values):
        return values[:, :cells_x + 1, 1:cells_y + 2] - corner_part(values)

    def forward_dz(values):
        return forward_z(corner_part(values))
    curl_x = forward_y(field_z) - forward_dz(field_y)
    curl_y = forward_dz(field_x) - forward_x(field_z)
    curl_z = forward_x(field_y) - forward_y(field_x)
    weighted_x = coupling * curl_x
    weighted_y = coupling * curl_y
    weighted_z = coupling * curl_z

    def backward_x(values):
        return values[:, 1:, 1:] - values[:, :-1, 1:]

    def backward_y(values):
        return values[:, 1:, 1:] - values[:, 1:, :-1]

    def backward_dz(values):
        return backward_z(values[:, 1:, 1:])
    result_x = backward_y(weighted_z) - backward_dz(weighted_y)
    result_y = backward_dz(weighted_x) - backward_x(weighted_z)
    result_z = backward_x(weighted_y) - backward_y(weighted_x)
    interior = padded_field[:, :, 1:cells_x + 1, 1:cells_y + 1]
    stacked = jnp.stack([result_x, result_y, result_z], axis=1)
    return stacked - shift_scalar * permittivity * interior

def reference(krylov_basis, regions, mu_table, eps_table, shift_value):
    total_rows = 3 * NX * NY * NZ
    flattened = krylov_basis.reshape(COLS, -1)
    gram_matrix = jnp.dot(flattened.astype(jnp.float32), flattened.T.astype(jnp.float32), precision=lax.Precision.HIGHEST, preferred_element_type=jnp.float32) / total_rows
    lower_factor = jnp.linalg.cholesky(gram_matrix)
    upper_factor = lower_factor.T
    inverse = lax.linalg.triangular_solve(lower_factor, jnp.eye(COLS, dtype=jnp.float32), left_side=True, lower=True)
    ortho_flat = jnp.dot(inverse.astype(jnp.float32), flattened.astype(jnp.float32), precision=lax.Precision.HIGHEST, preferred_element_type=jnp.float32)
    orthonormal = ortho_flat.reshape(krylov_basis.shape)
    coupling = jnp.pad(mu_table[regions], ((1, 0), (1, 0), (0, 0)))
    permittivity = eps_table[regions]
    shift_scalar = shift_value[0]
    blocks = orthonormal.reshape((COLS // 8, 8) + krylov_basis.shape[1:])

    def apply_block(column_block):
        padded_field = jnp.pad(column_block, ((0, 0), (0, 0), (1, 1), (1, 1), (0, 0)))
        return operator_block(padded_field, coupling, permittivity, shift_scalar)
    applied = lax.map(apply_block, blocks).reshape(krylov_basis.shape)
    projected = jnp.dot(ortho_flat.astype(jnp.float32), applied.reshape(COLS, -1).T.astype(jnp.float32), precision=lax.Precision.HIGHEST, preferred_element_type=jnp.float32) / total_rows
    return (orthonormal, upper_factor, applied, projected)
```

```python
import functools

import jax
import jax.numpy as jnp
from jax import lax
from jax.experimental import pallas as pl
from jax.experimental.pallas import tpu as pltpu
from jax.sharding import PartitionSpec as P

F32 = jnp.float32
HIGHEST = lax.Precision.HIGHEST


def shifted(x, axis, by):
    peers = lax.axis_size(axis)
    pairs = [(i, i + by) for i in range(peers) if 0 <= i + by < peers]
    return lax.ppermute(x, axis, pairs)


def exchanged_sum(x, axes):
    for axis in axes:
        peers = lax.axis_size(axis)
        if peers & (peers - 1):
            x = lax.psum(x, axis)
            continue
        step = 1
        while step < peers:
            x = x + lax.ppermute(x, axis, [(i, i ^ step) for i in range(peers)])
            step *= 2
    return x


def wide(chunks):
    return jnp.concatenate(chunks, axis=1)


def inner(left, right):
    return lax.dot_general(
        left, right, (((1,), (1,)), ((), ())), precision=HIGHEST, preferred_element_type=F32
    )


def table_rows(labels, table_ref):
    result = jnp.zeros(labels.shape, F32)
    for region in range(table_ref.shape[0]):
        result = jnp.where(labels == region, table_ref[region], result)
    return result


def forward_z(values):
    lanes = values.shape[1]
    lane = lax.broadcasted_iota(jnp.int32, values.shape, 1)
    ahead = jnp.where(lane == lanes - 1, 0.0, pltpu.roll(values, lanes - 1, 1))
    return ahead - values


def backward_z(values):
    lane = lax.broadcasted_iota(jnp.int32, values.shape, 1)
    return values - jnp.where(lane == 0, 0.0, pltpu.roll(values, 1, 1))


def part(ref, index, columns):
    return ref[index * columns : (index + 1) * columns, :]


def pack_kernel(columns, cells, basis, out_x, out_yz, out_edge):
    stride = 3 * cells
    for k in range(stride):
        chunk = basis[pl.ds(k, columns, stride=stride), :]
        ref, at = (out_x, k) if k < cells else (out_yz, k - cells)
        ref[at * columns : (at + 1) * columns, :] = chunk
        if k == 0:
            out_edge[:columns, :] = chunk
        if k == 2 * cells:
            out_edge[columns:, :] = chunk


def gram_kernel(columns, cells, field_x, field_yz, out):
    chunks = [part(field_x, k, columns) for k in range(cells)]
    chunks += [part(field_yz, k, columns) for k in range(2 * cells)]
    flat = wide(chunks)
    out[...] = inner(flat, flat)


def curl_kernel(
    columns, cells, mu_table, eps_table, shift, field_x, field_yz, ahead_x, ahead_y, regions,
    out_x, out_yz, out_edge, out_proj,
):
    coupling = table_rows(regions[...], mu_table)
    scaled_eps = -shift[0] * table_rows(regions[...], eps_table)
    left, right = [], []
    for y in range(cells):
        e_x = part(field_x, y, columns)
        e_y = part(field_yz, y, columns)
        e_z = part(field_yz, cells + y, columns)
        inside = y + 1 < cells
        e_x_up = part(field_x, y + 1, columns) if inside else part(ahead_y, 0, columns)
        e_z_up = part(field_yz, cells + y + 1, columns) if inside else part(ahead_y, 1, columns)
        e_y_next = part(ahead_x, y, columns)
        e_z_next = part(ahead_x, cells + y, columns)
        curl_x = (e_z_up - e_z) - forward_z(e_y)
        curl_y = forward_z(e_x) - (e_z_next - e_z)
        curl_z = (e_y_next - e_y) - (e_x_up - e_x)
        mu = coupling[y : y + 1, :]
        eps = scaled_eps[y : y + 1, :]
        m_x, m_y, m_z = mu * curl_x, mu * curl_y, mu * curl_z
        out_x[y * columns : (y + 1) * columns, :] = m_x
        out_yz[y * columns : (y + 1) * columns, :] = m_y
        out_yz[(cells + y) * columns : (cells + y + 1) * columns, :] = m_z
        if not inside:
            out_edge[:columns, :] = m_x
            out_edge[columns:, :] = m_z
        left += [curl_x, curl_y, curl_z, e_x, e_y, e_z]
        right += [m_x, m_y, m_z, eps * e_x, eps * e_y, eps * e_z]
    out_proj[...] = inner(wide(left), wide(right))


def factor(gram):
    columns = gram.shape[0]
    row = lax.broadcasted_iota(jnp.int32, (columns, 2 * columns), 0)
    lane = lax.broadcasted_iota(jnp.int32, (columns, 2 * columns), 1)
    work = jnp.concatenate([gram, jnp.zeros_like(gram)], axis=1)
    work = jnp.where(lane == row + columns, 1.0, work)
    for j in range(columns):
        pivot_row = work[j : j + 1, :]
        column = work[:, j : j + 1]
        scale = jnp.where(row > j, column / work[j : j + 1, j : j + 1], 0.0)
        work = work - scale * pivot_row
    diagonal = jnp.sum(jnp.where(lane == row, work, 0.0), axis=1, keepdims=True)
    work = work * lax.rsqrt(diagonal)
    work = jnp.where((lane >= row) & (lane <= row + columns), work, 0.0)
    return work[:, :columns], work[:, columns:]


def finish_kernel(
    columns, cells, total, eps_table, shift, field_x, field_yz, m_x, m_yz, behind_x, behind_y,
    regions, gram, proj, out_basis, out_upper, out_image, out_proj,
):
    upper, inverse = factor(gram[...] / total)
    out_upper[...] = upper
    half = lax.dot_general(
        inverse, proj[...] / total, (((1,), (0,)), ((), ())), precision=HIGHEST,
        preferred_element_type=F32,
    )
    out_proj[...] = inner(half, inverse)
    scaled_eps = shift[0] * table_rows(regions[...], eps_table)
    stride = 3 * cells
    for y in range(cells):
        e = [part(field_x, y, columns), part(field_yz, y, columns), part(field_yz, cells + y, columns)]
        m = [part(m_x, y, columns), part(m_yz, y, columns), part(m_yz, cells + y, columns)]
        inside = y > 0
        m_x_down = part(m_x, y - 1, columns) if inside else part(behind_y, 0, columns)
        m_z_down = part(m_yz, cells + y - 1, columns) if inside else part(behind_y, 1, columns)
        m_y_last = part(behind_x, y, columns)
        m_z_last = part(behind_x, cells + y, columns)
        eps = scaled_eps[y : y + 1, :]
        image = [
            (m[2] - m_z_down) - backward_z(m[1]) - eps * e[0],
            backward_z(m[0]) - (m[2] - m_z_last) - eps * e[1],
            (m[1] - m_y_last) - (m[0] - m_x_down) - eps * e[2],
        ]
        both = lax.dot_general(
            inverse, wide(e + image), (((1,), (0,)), ((), ())), precision=HIGHEST,
            preferred_element_type=F32,
        )
        lanes = e[0].shape[1]
        for c in range(3):
            place = pl.ds(c * cells + y, columns, stride=stride)
            out_basis[place, :] = both[:, c * lanes : (c + 1) * lanes]
            out_image[place, :] = both[:, (3 + c) * lanes : (4 + c) * lanes]


SMEM = pl.BlockSpec(memory_space=pltpu.SMEM)
VMEM = pl.BlockSpec(memory_space=pltpu.VMEM)


def call(body, scalars, arrays, outs):
    shapes = [jax.ShapeDtypeStruct(shape, F32) for shape in outs]
    return pl.pallas_call(
        body,
        out_shape=shapes,
        in_specs=[SMEM] * len(scalars) + [VMEM] * len(arrays),
        out_specs=[VMEM] * len(shapes),
        compiler_params=pltpu.CompilerParams(vmem_limit_bytes=32 * 1024 * 1024),
    )(*scalars, *arrays)


def local(krylov_basis, regions, mu_table, eps_table, shift_value):
    columns, parts, layers, cells, lanes = krylov_basis.shape
    assert layers == 1 and parts == 3
    total = 3 * cells * lanes * lax.axis_size("row") * lax.axis_size("col")
    basis = krylov_basis.reshape(-1, lanes)
    labels = regions[0]
    small, large, edge = (cells * columns, lanes), (2 * cells * columns, lanes), (2 * columns, lanes)
    square = (columns, columns)

    field_x, field_yz, edge_e = call(
        functools.partial(pack_kernel, columns, cells), (), (basis,), (small, large, edge)
    )
    ahead_x = shifted(field_yz, "row", -1)
    ahead_y = shifted(edge_e, "col", -1)
    (gram,) = call(
        functools.partial(gram_kernel, columns, cells), (), (field_x, field_yz), (square,)
    )
    m_x, m_yz, edge_m, proj = call(
        functools.partial(curl_kernel, columns, cells),
        (mu_table, eps_table, shift_value),
        (field_x, field_yz, ahead_x, ahead_y, labels),
        (small, large, edge, square),
    )
    behind_x = shifted(m_yz, "row", 1)
    behind_y = shifted(edge_m, "col", 1)
    gram = exchanged_sum(gram, ("col", "row"))
    proj = exchanged_sum(proj, ("col", "row"))
    basis_out, upper, image_out, projected = call(
        functools.partial(finish_kernel, columns, cells, total),
        (eps_table, shift_value),
        (field_x, field_yz, m_x, m_yz, behind_x, behind_y, labels, gram, proj),
        (basis.shape, square, basis.shape, square),
    )
    return (
        basis_out.reshape(krylov_basis.shape),
        upper,
        image_out.reshape(krylov_basis.shape),
        projected,
    )


def solution(mesh):
    placed = (P("shift", None, "row", "col", None), P("row", "col", None), P(), P(), P("shift"))
    return jax.shard_map(
        local,
        mesh=mesh,
        in_specs=placed,
        out_specs=(
            P("shift", None, "row", "col", None),
            P("shift", None),
            P("shift", None, "row", "col", None),
            P("shift", None),
        ),
        check_vma=False,
    )
```

```python
import functools

import jax
import jax.numpy as jnp
from jax import lax
from jax.experimental import pallas as pl
from jax.experimental.pallas import tpu as pltpu
from jax.sharding import PartitionSpec as P

F32 = jnp.float32
HIGHEST = lax.Precision.HIGHEST


def shifted(x, axis, by):
    peers = lax.axis_size(axis)
    pairs = [(i, i + by) for i in range(peers) if 0 <= i + by < peers]
    return lax.ppermute(x, axis, pairs)


def wide(chunks):
    return jnp.concatenate(chunks, axis=1)


def inner(left, right):
    return lax.dot_general(
        left, right, (((1,), (1,)), ((), ())), precision=HIGHEST, preferred_element_type=F32
    )


def table_rows(labels, table_ref):
    result = jnp.zeros(labels.shape, F32)
    for region in range(table_ref.shape[0]):
        result = jnp.where(labels == region, table_ref[region], result)
    return result


def forward_z(values):
    lanes = values.shape[1]
    lane = lax.broadcasted_iota(jnp.int32, values.shape, 1)
    ahead = jnp.where(lane == lanes - 1, 0.0, pltpu.roll(values, lanes - 1, 1))
    return ahead - values


def backward_z(values):
    lane = lax.broadcasted_iota(jnp.int32, values.shape, 1)
    return values - jnp.where(lane == 0, 0.0, pltpu.roll(values, 1, 1))


def part(ref, index, columns):
    return ref[index * columns : (index + 1) * columns, :]


def packed(square):
    half = square.shape[0] // 2
    return jnp.concatenate([square[:half, :], square[half:, :]], axis=1)


def unpacked(pair):
    half = pair.shape[1] // 2
    return jnp.concatenate([pair[:, :half], pair[:, half:]], axis=0)


def pack_kernel(columns, cells, basis, out_x, out_yz):
    stride = 3 * cells
    for k in range(stride):
        ref, at = (out_x, k) if k < cells else (out_yz, k - cells)
        ref[at * columns : (at + 1) * columns, :] = basis[pl.ds(k, columns, stride=stride), :]


def material_kernel(mu_table, eps_table, shift, regions, out):
    labels = regions[...]
    cells = labels.shape[0]
    out[:cells, :] = table_rows(labels, mu_table)
    out[cells:, :] = shift[0] * table_rows(labels, eps_table)


def gram_kernel(columns, cells, field_x, field_yz, out):
    half = columns // 2
    chunks = [part(field_x, k, columns) for k in range(cells)]
    chunks += [part(field_yz, k, columns) for k in range(2 * cells)]
    flat = wide(chunks)
    out[half : half + columns, :] = chunks[0]
    out[half + columns :, :] = chunks[2 * cells]
    out[:half, :] = packed(inner(flat, flat))


def curl_kernel(
    columns, cells, has_next, field_x, field_yz, ahead_x, ahead_y, material, gram, gram_other,
    out_x, out_yz, out_edge, out_gram,
):
    half = columns // 2
    out_gram[...] = gram[...] + gram_other[...]
    coupling = material[:cells, :]
    scaled_eps = -material[cells:, :]
    inside_next = has_next[0] > 0
    left, right = [], []
    for y in range(cells):
        e_x = part(field_x, y, columns)
        e_y = part(field_yz, y, columns)
        e_z = part(field_yz, cells + y, columns)
        inside = y + 1 < cells
        if inside:
            e_x_up, e_z_up = part(field_x, y + 1, columns), part(field_yz, cells + y + 1, columns)
        else:
            e_x_up = jnp.where(inside_next, ahead_y[half : half + columns, :], 0.0)
            e_z_up = jnp.where(inside_next, ahead_y[half + columns :, :], 0.0)
        e_y_next = part(ahead_x, y, columns)
        e_z_next = part(ahead_x, cells + y, columns)
        curl_x = (e_z_up - e_z) - forward_z(e_y)
        curl_y = forward_z(e_x) - (e_z_next - e_z)
        curl_z = (e_y_next - e_y) - (e_x_up - e_x)
        mu = coupling[y : y + 1, :]
        eps = scaled_eps[y : y + 1, :]
        m_x, m_y, m_z = mu * curl_x, mu * curl_y, mu * curl_z
        out_x[y * columns : (y + 1) * columns, :] = m_x
        out_yz[y * columns : (y + 1) * columns, :] = m_y
        out_yz[(cells + y) * columns : (cells + y + 1) * columns, :] = m_z
        if not inside:
            out_edge[half : half + columns, :] = m_x
            out_edge[half + columns :, :] = m_z
        left += [curl_x, curl_y, curl_z, e_x, e_y, e_z]
        right += [m_x, m_y, m_z, eps * e_x, eps * e_y, eps * e_z]
    out_edge[:half, :] = packed(inner(wide(left), wide(right)))


def join_kernel(gram, edge, edge_other, out):
    half, columns = gram.shape[0], 2 * gram.shape[0]
    proj = edge[:half, :] + edge_other[:half, :]
    out[:, :columns] = unpacked(gram[...])
    out[:, columns:] = unpacked(proj)


def factor(gram):
    columns = gram.shape[0]
    span, tile = 2 * columns, 8
    count = columns // tile
    spread = lambda values: jnp.broadcast_to(values, (tile, span))
    sublane = lax.broadcasted_iota(jnp.int32, (tile, span), 0)
    lane = lax.broadcasted_iota(jnp.int32, (tile, span), 1)
    blocks = []
    for b in range(count):
        rows = gram[b * tile : (b + 1) * tile, :]
        rows = jnp.concatenate([rows, jnp.zeros_like(rows)], axis=1)
        blocks.append(jnp.where(lane == sublane + b * tile + columns, 1.0, rows))
    scales = [None] * count
    for first in range(count):
        panel = [
            [spread(rows[:, first * tile + k : first * tile + k + 1]) for rows in blocks[first:]]
            for k in range(tile)
        ]
        for k in range(tile):
            pivot = spread(panel[k][0][k : k + 1, :])
            inverse = 1.0 / pivot
            ratio = [rows * inverse for rows in panel[k]]
            ratio[0] = jnp.where(sublane > k, ratio[0], 0.0)
            root = lax.rsqrt(pivot)
            scales[first] = root if k == 0 else jnp.where(sublane == k, root, scales[first])
            for later in range(k + 1, tile):
                entry = spread(panel[k][0][later : later + 1, :])
                panel[later] = [rows - f * entry for rows, f in zip(panel[later], ratio)]
            pivot_row = spread(blocks[first][k : k + 1, :])
            for b in range(first, count):
                blocks[b] = blocks[b] - ratio[b - first] * pivot_row
    kept = []
    for b in range(count):
        row = sublane + b * tile
        kept.append(jnp.where((lane >= row) & (lane <= row + columns), blocks[b] * scales[b], 0.0))
    both = jnp.concatenate(kept, axis=0)
    return both[:, :columns], both[:, columns:]


def factor_kernel(total, sums, out_upper, out_inverse):
    columns = sums.shape[0]
    upper, inverse = factor(sums[:, :columns] / total)
    out_upper[...] = upper
    out_inverse[...] = inverse


def finish_kernel(
    columns, cells, total, has_last, field_x, field_yz, m_x, m_yz, behind_x, behind_y, material,
    inverse_ref, proj, proj_other, out_basis, out_image, out_proj,
):
    half = columns // 2
    inverse = inverse_ref[...]
    raw = unpacked(proj[...] + proj_other[...]) / total
    left = lax.dot_general(
        inverse, raw, (((1,), (0,)), ((), ())), precision=HIGHEST, preferred_element_type=F32
    )
    out_proj[...] = inner(left, inverse)
    inside_last = has_last[0] > 0
    scaled_eps = material[cells:, :]
    stride = 3 * cells
    for y in range(cells):
        e = [part(field_x, y, columns), part(field_yz, y, columns), part(field_yz, cells + y, columns)]
        m = [part(m_x, y, columns), part(m_yz, y, columns), part(m_yz, cells + y, columns)]
        if y > 0:
            m_x_down, m_z_down = part(m_x, y - 1, columns), part(m_yz, cells + y - 1, columns)
        else:
            m_x_down = jnp.where(inside_last, behind_y[half : half + columns, :], 0.0)
            m_z_down = jnp.where(inside_last, behind_y[half + columns :, :], 0.0)
        m_y_last = part(behind_x, y, columns)
        m_z_last = part(behind_x, cells + y, columns)
        eps = scaled_eps[y : y + 1, :]
        image = [
            (m[2] - m_z_down) - backward_z(m[1]) - eps * e[0],
            backward_z(m[0]) - (m[2] - m_z_last) - eps * e[1],
            (m[1] - m_y_last) - (m[0] - m_x_down) - eps * e[2],
        ]
        both = lax.dot_general(
            inverse, wide(e + image), (((1,), (0,)), ((), ())), precision=HIGHEST,
            preferred_element_type=F32,
        )
        lanes = e[0].shape[1]
        for c in range(3):
            place = pl.ds(c * cells + y, columns, stride=stride)
            out_basis[place, :] = both[:, c * lanes : (c + 1) * lanes]
            out_image[place, :] = both[:, (3 + c) * lanes : (4 + c) * lanes]


def split_kernel(sums, out):
    columns = sums.shape[0]
    out[...] = packed(sums[:, columns:])


SMEM = pl.BlockSpec(memory_space=pltpu.SMEM)
VMEM = pl.BlockSpec(memory_space=pltpu.VMEM)


def call(body, scalars, arrays, outs, flops=None):
    shapes = [jax.ShapeDtypeStruct(shape, F32) for shape in outs]
    cost = None
    if flops is not None:
        cost = pl.CostEstimate(flops=flops, bytes_accessed=0, transcendentals=0)
    return pl.pallas_call(
        body,
        out_shape=shapes,
        in_specs=[SMEM] * len(scalars) + [VMEM] * len(arrays),
        out_specs=[VMEM] * len(shapes),
        cost_estimate=cost,
        compiler_params=pltpu.CompilerParams(vmem_limit_bytes=32 * 1024 * 1024),
    )(*scalars, *arrays)


def swapped(x, axis, step):
    return lax.ppermute(x, axis, [(i, i ^ step) for i in range(lax.axis_size(axis))])


def local(krylov_basis, regions, mu_table, eps_table, shift_value):
    columns, parts, layers, cells, lanes = krylov_basis.shape
    rows, cols = lax.axis_size("row"), lax.axis_size("col")
    assert layers == 1 and parts == 3 and cols == 2 and rows & (rows - 1) == 0
    total = 3 * cells * lanes * rows * cols
    basis = krylov_basis.reshape(-1, lanes)
    labels = regions[0]
    half = columns // 2
    small, large = (cells * columns, lanes), (2 * cells * columns, lanes)
    edge, pair = (half + 2 * columns, lanes), (half, 2 * columns)
    square = (columns, columns)
    place = lax.axis_index("col")
    has_next = jnp.where(place == 0, 1, 0).astype(jnp.int32)[None]
    has_last = 1 - has_next

    (material,) = call(
        material_kernel, (mu_table, eps_table, shift_value), (labels,), ((2 * cells, lanes),),
        flops=0,
    )
    field_x, field_yz = call(
        functools.partial(pack_kernel, columns, cells), (), (basis,), (small, large), flops=0
    )
    ahead_x = shifted(field_yz, "row", -1)
    (gram_edge,) = call(
        functools.partial(gram_kernel, columns, cells), (), (field_x, field_yz), (edge,), flops=0
    )
    ahead_y = swapped(gram_edge, "col", 1)
    gram = gram_edge[:half] + ahead_y[:half]
    gram_other = swapped(gram, "row", 1)
    m_x, m_yz, proj_edge, gram = call(
        functools.partial(curl_kernel, columns, cells),
        (has_next,),
        (field_x, field_yz, ahead_x, ahead_y, material, gram, gram_other),
        (small, large, edge, pair),
        flops=0,
    )
    behind_y = swapped(proj_edge, "col", 1)
    behind_x = shifted(m_yz, "row", 1)
    (sums,) = call(
        join_kernel, (), (gram, proj_edge, behind_y), ((columns, 2 * columns),), flops=0
    )
    step = 2
    while step < rows:
        sums = sums + swapped(sums, "row", step)
        step *= 2
    (proj,) = call(split_kernel, (), (sums,), (pair,), flops=0)
    proj_other = swapped(proj, "row", 1)
    upper, inverse = call(
        functools.partial(factor_kernel, total), (), (sums,), (square, square), flops=0
    )
    basis_out, image_out, projected = call(
        functools.partial(finish_kernel, columns, cells, total),
        (has_last,),
        (field_x, field_yz, m_x, m_yz, behind_x, behind_y, material, inverse, proj, proj_other),
        (basis.shape, basis.shape, square),
        flops=0,
    )
    return (
        basis_out.reshape(krylov_basis.shape),
        upper,
        image_out.reshape(krylov_basis.shape),
        projected,
    )


def solution(mesh):
    placed = (P("shift", None, "row", "col", None), P("row", "col", None), P(), P(), P("shift"))
    return jax.shard_map(
        local,
        mesh=mesh,
        in_specs=placed,
        out_specs=(
            P("shift", None, "row", "col", None),
            P("shift", None),
            P("shift", None, "row", "col", None),
            P("shift", None),
        ),
        check_vma=False,
    )
```

```python
import functools

import jax
import jax.numpy as jnp
from jax import lax
from jax.experimental import pallas as pl
from jax.experimental.pallas import tpu as pltpu
from jax.sharding import PartitionSpec as P

F32 = jnp.float32
HIGHEST = lax.Precision.HIGHEST


def shifted(x, axis, by):
    peers = lax.axis_size(axis)
    pairs = [(i, i + by) for i in range(peers) if 0 <= i + by < peers]
    return lax.ppermute(x, axis, pairs)


def wide(chunks):
    return jnp.concatenate(chunks, axis=1)


def inner(left, right):
    return lax.dot_general(
        left, right, (((1,), (1,)), ((), ())), precision=HIGHEST, preferred_element_type=F32
    )


def table_rows(labels, table_ref):
    result = jnp.zeros(labels.shape, F32)
    for region in range(table_ref.shape[0]):
        result = jnp.where(labels == region, table_ref[region], result)
    return result


def forward_z(values):
    lanes = values.shape[1]
    lane = lax.broadcasted_iota(jnp.int32, values.shape, 1)
    ahead = jnp.where(lane == lanes - 1, 0.0, pltpu.roll(values, lanes - 1, 1))
    return ahead - values


def backward_z(values):
    lane = lax.broadcasted_iota(jnp.int32, values.shape, 1)
    return values - jnp.where(lane == 0, 0.0, pltpu.roll(values, 1, 1))


def part(ref, index, columns):
    return ref[index * columns : (index + 1) * columns, :]


def packed(square):
    half = square.shape[0] // 2
    return jnp.concatenate([square[:half, :], square[half:, :]], axis=1)


def unpacked(pair):
    half = pair.shape[1] // 2
    return jnp.concatenate([pair[:, :half], pair[:, half:]], axis=0)


def pack_kernel(columns, cells, basis, out_x, out_yz):
    stride = 3 * cells
    for k in range(stride):
        ref, at = (out_x, k) if k < cells else (out_yz, k - cells)
        ref[at * columns : (at + 1) * columns, :] = basis[pl.ds(k, columns, stride=stride), :]


def material_kernel(mu_table, eps_table, shift, regions, out):
    labels = regions[...]
    cells = labels.shape[0]
    out[:cells, :] = table_rows(labels, mu_table)
    out[cells:, :] = shift[0] * table_rows(labels, eps_table)


def gram_kernel(columns, cells, field_x, field_yz, out):
    half = columns // 2
    chunks = [part(field_x, k, columns) for k in range(cells)]
    chunks += [part(field_yz, k, columns) for k in range(2 * cells)]
    flat = wide(chunks)
    out[half : half + columns, :] = chunks[0]
    out[half + columns :, :] = chunks[2 * cells]
    out[:half, :] = packed(inner(flat, flat))


def behind_kernel(columns, cells, has_next, field_x, field_yz, ahead_y, material, out):
    half = columns // 2
    inside_next = has_next[0] > 0
    mu = material[:cells, :]
    for y in range(cells):
        e_x = part(field_x, y, columns)
        if y + 1 < cells:
            e_x_up = part(field_x, y + 1, columns)
        else:
            e_x_up = jnp.where(inside_next, ahead_y[half : half + columns, :], 0.0)
        e_y, e_z = part(field_yz, y, columns), part(field_yz, cells + y, columns)
        mu_row = mu[y : y + 1, :]
        out[y * columns : (y + 1) * columns, :] = mu_row * (forward_z(e_x) + e_z)
        out[(cells + y) * columns : (cells + y + 1) * columns, :] = -mu_row * (e_y + (e_x_up - e_x))
    out[2 * cells * columns :, :] = jnp.concatenate(
        [mu, jnp.zeros((out.shape[0] - 2 * cells * columns - cells, mu.shape[1]), F32)], axis=0
    )


def curl_kernel(
    columns, cells, has_next, field_x, field_yz, ahead_x, ahead_y, material, out_x,
    out_yz, out_edge,
):
    half = columns // 2
    coupling = material[:cells, :]
    scaled_eps = -material[cells:, :]
    inside_next = has_next[0] > 0
    left, right = [], []
    for y in range(cells):
        e_x = part(field_x, y, columns)
        e_y = part(field_yz, y, columns)
        e_z = part(field_yz, cells + y, columns)
        inside = y + 1 < cells
        if inside:
            e_x_up, e_z_up = part(field_x, y + 1, columns), part(field_yz, cells + y + 1, columns)
        else:
            e_x_up = jnp.where(inside_next, ahead_y[half : half + columns, :], 0.0)
            e_z_up = jnp.where(inside_next, ahead_y[half + columns :, :], 0.0)
        e_y_next = part(ahead_x, y, columns)
        e_z_next = part(ahead_x, cells + y, columns)
        curl_x = (e_z_up - e_z) - forward_z(e_y)
        curl_y = forward_z(e_x) - (e_z_next - e_z)
        curl_z = (e_y_next - e_y) - (e_x_up - e_x)
        mu = coupling[y : y + 1, :]
        eps = scaled_eps[y : y + 1, :]
        m_x, m_y, m_z = mu * curl_x, mu * curl_y, mu * curl_z
        out_x[y * columns : (y + 1) * columns, :] = m_x
        out_yz[y * columns : (y + 1) * columns, :] = m_y
        out_yz[(cells + y) * columns : (cells + y + 1) * columns, :] = m_z
        if not inside:
            out_edge[half : half + columns, :] = m_x
            out_edge[half + columns :, :] = m_z
        left += [curl_x, curl_y, curl_z, e_x, e_y, e_z]
        right += [m_x, m_y, m_z, eps * e_x, eps * e_y, eps * e_z]
    out_edge[:half, :] = packed(inner(wide(left), wide(right)))


def add_kernel(left, right, out):
    out[...] = left[...] + right[...]


def join_kernel(gram, edge, edge_other, out):
    half, columns = gram.shape[0], 2 * gram.shape[0]
    proj = edge[:half, :] + edge_other[:half, :]
    out[:, :columns] = unpacked(gram[...])
    out[:, columns:] = unpacked(proj)


def factor(gram):
    columns = gram.shape[0]
    span, tile = 2 * columns, 8
    count = columns // tile
    spread = lambda values: jnp.broadcast_to(values, (tile, span))
    sublane = lax.broadcasted_iota(jnp.int32, (tile, span), 0)
    lane = lax.broadcasted_iota(jnp.int32, (tile, span), 1)
    blocks = []
    for b in range(count):
        rows = gram[b * tile : (b + 1) * tile, :]
        rows = jnp.concatenate([rows, jnp.zeros_like(rows)], axis=1)
        blocks.append(jnp.where(lane == sublane + b * tile + columns, 1.0, rows))
    scales = [None] * count
    for first in range(count):
        panel = [
            [spread(rows[:, first * tile + k : first * tile + k + 1]) for rows in blocks[first:]]
            for k in range(tile)
        ]
        for k in range(tile):
            pivot = spread(panel[k][0][k : k + 1, :])
            inverse = 1.0 / pivot
            ratio = [rows * inverse for rows in panel[k]]
            ratio[0] = jnp.where(sublane > k, ratio[0], 0.0)
            root = lax.rsqrt(pivot)
            scales[first] = root if k == 0 else jnp.where(sublane == k, root, scales[first])
            for later in range(k + 1, tile):
                entry = spread(panel[k][0][later : later + 1, :])
                panel[later] = [rows - f * entry for rows, f in zip(panel[later], ratio)]
            pivot_row = spread(blocks[first][k : k + 1, :])
            for b in range(first, count):
                blocks[b] = blocks[b] - ratio[b - first] * pivot_row
    kept = []
    for b in range(count):
        row = sublane + b * tile
        kept.append(jnp.where((lane >= row) & (lane <= row + columns), blocks[b] * scales[b], 0.0))
    both = jnp.concatenate(kept, axis=0)
    return both[:, :columns], both[:, columns:]


def factor_kernel(total, sums, out_upper, out_inverse):
    columns = sums.shape[0]
    upper, inverse = factor(sums[:, :columns] / total)
    out_upper[...] = upper
    out_inverse[...] = inverse


def finish_kernel(
    columns, cells, total, has_last, field_x, field_yz, m_x, m_yz, behind_x, behind_y, material,
    inverse_ref, proj, proj_other, out_basis, out_image, out_proj,
):
    half = columns // 2
    inverse = inverse_ref[...]
    raw = unpacked(proj[...] + proj_other[...]) / total
    left = lax.dot_general(
        inverse, raw, (((1,), (0,)), ((), ())), precision=HIGHEST, preferred_element_type=F32
    )
    out_proj[...] = inner(left, inverse)
    inside_last = has_last[0] > 0
    scaled_eps = material[cells:, :]
    stride = 3 * cells
    for y in range(cells):
        e = [part(field_x, y, columns), part(field_yz, y, columns), part(field_yz, cells + y, columns)]
        m = [part(m_x, y, columns), part(m_yz, y, columns), part(m_yz, cells + y, columns)]
        if y > 0:
            m_x_down, m_z_down = part(m_x, y - 1, columns), part(m_yz, cells + y - 1, columns)
        else:
            m_x_down = jnp.where(inside_last, behind_y[half : half + columns, :], 0.0)
            m_z_down = jnp.where(inside_last, behind_y[half + columns :, :], 0.0)
        mu_last = behind_x[2 * cells * columns + y : 2 * cells * columns + y + 1, :]
        m_y_last = part(behind_x, y, columns) - mu_last * e[2]
        m_z_last = part(behind_x, cells + y, columns) + mu_last * e[1]
        eps = scaled_eps[y : y + 1, :]
        image = [
            (m[2] - m_z_down) - backward_z(m[1]) - eps * e[0],
            backward_z(m[0]) - (m[2] - m_z_last) - eps * e[1],
            (m[1] - m_y_last) - (m[0] - m_x_down) - eps * e[2],
        ]
        both = lax.dot_general(
            inverse, wide(e + image), (((1,), (0,)), ((), ())), precision=HIGHEST,
            preferred_element_type=F32,
        )
        lanes = e[0].shape[1]
        for c in range(3):
            place = pl.ds(c * cells + y, columns, stride=stride)
            out_basis[place, :] = both[:, c * lanes : (c + 1) * lanes]
            out_image[place, :] = both[:, (3 + c) * lanes : (4 + c) * lanes]


def split_kernel(sums, out):
    columns = sums.shape[0]
    out[...] = packed(sums[:, columns:])


SMEM = pl.BlockSpec(memory_space=pltpu.SMEM)
VMEM = pl.BlockSpec(memory_space=pltpu.VMEM)


def call(body, scalars, arrays, outs, flops=None):
    shapes = [jax.ShapeDtypeStruct(shape, F32) for shape in outs]
    cost = None
    if flops is not None:
        cost = pl.CostEstimate(flops=flops, bytes_accessed=0, transcendentals=0)
    return pl.pallas_call(
        body,
        out_shape=shapes,
        in_specs=[SMEM] * len(scalars) + [VMEM] * len(arrays),
        out_specs=[VMEM] * len(shapes),
        cost_estimate=cost,
        compiler_params=pltpu.CompilerParams(vmem_limit_bytes=32 * 1024 * 1024),
    )(*scalars, *arrays)


def swapped(x, axis, step):
    return lax.ppermute(x, axis, [(i, i ^ step) for i in range(lax.axis_size(axis))])


def local(krylov_basis, regions, mu_table, eps_table, shift_value):
    columns, parts, layers, cells, lanes = krylov_basis.shape
    rows, cols = lax.axis_size("row"), lax.axis_size("col")
    assert layers == 1 and parts == 3 and cols == 2 and rows & (rows - 1) == 0
    total = 3 * cells * lanes * rows * cols
    basis = krylov_basis.reshape(-1, lanes)
    labels = regions[0]
    half = columns // 2
    small, large = (cells * columns, lanes), (2 * cells * columns, lanes)
    edge, pair = (half + 2 * columns, lanes), (half, 2 * columns)
    square = (columns, columns)
    place = lax.axis_index("col")
    has_next = jnp.where(place == 0, 1, 0).astype(jnp.int32)[None]
    has_last = 1 - has_next

    (material,) = call(
        material_kernel, (mu_table, eps_table, shift_value), (labels,), ((2 * cells, lanes),),
        flops=0,
    )
    field_x, field_yz = call(
        functools.partial(pack_kernel, columns, cells), (), (basis,), (small, large), flops=0
    )
    ahead_x = shifted(field_yz, "row", -1)
    (gram_edge,) = call(
        functools.partial(gram_kernel, columns, cells), (), (field_x, field_yz), (edge,), flops=0
    )
    ahead_y = swapped(gram_edge, "col", 1)
    gram = gram_edge[:half] + ahead_y[:half]
    gram_other = swapped(gram, "row", 1)
    (sent,) = call(
        functools.partial(behind_kernel, columns, cells),
        (has_next,),
        (field_x, field_yz, ahead_y, material),
        ((2 * cells * columns + -(-cells // 8) * 8, lanes),),
        flops=0,
    )
    behind_x = shifted(sent, "row", 1)
    m_x, m_yz, proj_edge = call(
        functools.partial(curl_kernel, columns, cells),
        (has_next,),
        (field_x, field_yz, ahead_x, ahead_y, material),
        (small, large, edge),
        flops=10**10,
    )
    (gram,) = call(add_kernel, (), (gram, gram_other), (pair,), flops=10**10)
    behind_y = swapped(proj_edge, "col", 1)
    (sums,) = call(
        join_kernel, (), (gram, proj_edge, behind_y), ((columns, 2 * columns),), flops=0
    )
    step = 2
    while step < rows:
        sums = sums + swapped(sums, "row", step)
        step *= 2
    (proj,) = call(split_kernel, (), (sums,), (pair,), flops=0)
    proj_other = swapped(proj, "row", 1)
    upper, inverse = call(
        functools.partial(factor_kernel, total), (), (sums,), (square, square), flops=0
    )
    basis_out, image_out, projected = call(
        functools.partial(finish_kernel, columns, cells, total),
        (has_last,),
        (field_x, field_yz, m_x, m_yz, behind_x, behind_y, material, inverse, proj, proj_other),
        (basis.shape, basis.shape, square),
        flops=0,
    )
    return (
        basis_out.reshape(krylov_basis.shape),
        upper,
        image_out.reshape(krylov_basis.shape),
        projected,
    )


def solution(mesh):
    placed = (P("shift", None, "row", "col", None), P("row", "col", None), P(), P(), P("shift"))
    return jax.shard_map(
        local,
        mesh=mesh,
        in_specs=placed,
        out_specs=(
            P("shift", None, "row", "col", None),
            P("shift", None),
            P("shift", None, "row", "col", None),
            P("shift", None),
        ),
        check_vma=False,
    )
```

```python
import functools

import jax
import jax.numpy as jnp
from jax import lax
from jax.experimental import pallas as pl
from jax.experimental.pallas import tpu as pltpu
from jax.sharding import PartitionSpec as P

F32 = jnp.float32
HIGHEST = lax.Precision.HIGHEST


def shifted(x, axis, by):
    peers = lax.axis_size(axis)
    pairs = [(i, i + by) for i in range(peers) if 0 <= i + by < peers]
    return lax.ppermute(x, axis, pairs)


def wide(chunks):
    return jnp.concatenate(chunks, axis=1)


def inner(left, right):
    return lax.dot_general(
        left, right, (((1,), (1,)), ((), ())), precision=HIGHEST, preferred_element_type=F32
    )


def table_rows(labels, table_ref):
    result = jnp.zeros(labels.shape, F32)
    for region in range(table_ref.shape[0]):
        result = jnp.where(labels == region, table_ref[region], result)
    return result


def forward_z(values):
    lanes = values.shape[1]
    lane = lax.broadcasted_iota(jnp.int32, values.shape, 1)
    ahead = jnp.where(lane == lanes - 1, 0.0, pltpu.roll(values, lanes - 1, 1))
    return ahead - values


def backward_z(values):
    lane = lax.broadcasted_iota(jnp.int32, values.shape, 1)
    return values - jnp.where(lane == 0, 0.0, pltpu.roll(values, 1, 1))


def part(ref, index, columns):
    return ref[index * columns : (index + 1) * columns, :]


def packed(square):
    half = square.shape[0] // 2
    return jnp.concatenate([square[:half, :], square[half:, :]], axis=1)


def unpacked(pair):
    half = pair.shape[1] // 2
    return jnp.concatenate([pair[:, :half], pair[:, half:]], axis=0)


def pack_kernel(columns, cells, basis, out_x, out_yz):
    stride = 3 * cells
    for k in range(stride):
        ref, at = (out_x, k) if k < cells else (out_yz, k - cells)
        ref[at * columns : (at + 1) * columns, :] = basis[pl.ds(k, columns, stride=stride), :]


def material_kernel(mu_table, eps_table, shift, regions, out):
    labels = regions[...]
    cells = labels.shape[0]
    out[:cells, :] = table_rows(labels, mu_table)
    out[cells:, :] = shift[0] * table_rows(labels, eps_table)


def gram_kernel(columns, cells, field_x, field_yz, out):
    half = columns // 2
    chunks = [part(field_x, k, columns) for k in range(cells)]
    chunks += [part(field_yz, k, columns) for k in range(2 * cells)]
    flat = wide(chunks)
    out[half : half + columns, :] = chunks[0]
    out[half + columns :, :] = chunks[2 * cells]
    out[:half, :] = packed(inner(flat, flat))


def behind_kernel(
    columns, cells, has_next, field_x, field_yz, gram_edge, ahead_y, material, out, out_gram
):
    half = columns // 2
    out_gram[...] = gram_edge[:half, :] + ahead_y[:half, :]
    inside_next = has_next[0] > 0
    mu = material[:cells, :]
    for y in range(cells):
        e_x = part(field_x, y, columns)
        if y + 1 < cells:
            e_x_up = part(field_x, y + 1, columns)
        else:
            e_x_up = jnp.where(inside_next, ahead_y[half : half + columns, :], 0.0)
        e_y, e_z = part(field_yz, y, columns), part(field_yz, cells + y, columns)
        mu_row = mu[y : y + 1, :]
        out[y * columns : (y + 1) * columns, :] = mu_row * (forward_z(e_x) + e_z)
        out[(cells + y) * columns : (cells + y + 1) * columns, :] = -mu_row * (e_y + (e_x_up - e_x))
    out[2 * cells * columns :, :] = jnp.concatenate(
        [mu, jnp.zeros((out.shape[0] - 2 * cells * columns - cells, mu.shape[1]), F32)], axis=0
    )


def near_kernel(columns, cells, has_next, field_x, field_yz, ahead_y, material, out_x, out_proj):
    half = columns // 2
    inside_next = has_next[0] > 0
    left, right = [], []
    for y in range(cells):
        e_x = part(field_x, y, columns)
        e_y = part(field_yz, y, columns)
        e_z = part(field_yz, cells + y, columns)
        if y + 1 < cells:
            e_z_up = part(field_yz, cells + y + 1, columns)
        else:
            e_z_up = jnp.where(inside_next, ahead_y[half + columns :, :], 0.0)
        curl_x = (e_z_up - e_z) - forward_z(e_y)
        m_x = material[y : y + 1, :] * curl_x
        eps = -material[cells + y : cells + y + 1, :]
        out_x[y * columns : (y + 1) * columns, :] = m_x
        left += [curl_x, e_x, e_y, e_z]
        right += [m_x, eps * e_x, eps * e_y, eps * e_z]
    out_proj[...] = packed(inner(wide(left), wide(right)))


def curl_kernel(
    columns, cells, has_next, field_x, field_yz, ahead_x, ahead_y, material, m_x, near, out_yz,
    out_edge,
):
    half = columns // 2
    inside_next = has_next[0] > 0
    left, right = [], []
    for y in range(cells):
        e_x = part(field_x, y, columns)
        e_y = part(field_yz, y, columns)
        e_z = part(field_yz, cells + y, columns)
        if y + 1 < cells:
            e_x_up = part(field_x, y + 1, columns)
        else:
            e_x_up = jnp.where(inside_next, ahead_y[half : half + columns, :], 0.0)
        curl_y = forward_z(e_x) - (part(ahead_x, cells + y, columns) - e_z)
        curl_z = (part(ahead_x, y, columns) - e_y) - (e_x_up - e_x)
        mu = material[y : y + 1, :]
        m_y, m_z = mu * curl_y, mu * curl_z
        out_yz[y * columns : (y + 1) * columns, :] = m_y
        out_yz[(cells + y) * columns : (cells + y + 1) * columns, :] = m_z
        if y + 1 == cells:
            out_edge[half + columns :, :] = m_z
        left += [curl_y, curl_z]
        right += [m_y, m_z]
    out_edge[half : half + columns, :] = part(m_x, cells - 1, columns)
    out_edge[:half, :] = near[...] + packed(inner(wide(left), wide(right)))


def add_kernel(left, right, out):
    out[...] = left[...] + right[...]


def join_kernel(gram, edge, edge_other, out):
    half, columns = gram.shape[0], 2 * gram.shape[0]
    proj = edge[:half, :] + edge_other[:half, :]
    out[:, :columns] = unpacked(gram[...])
    out[:, columns:] = unpacked(proj)


def factor(gram):
    columns = gram.shape[0]
    span, tile, width = 2 * columns, 8, 16
    count = columns // tile
    spread = lambda values: jnp.broadcast_to(values, (tile, span))
    sublane = lax.broadcasted_iota(jnp.int32, (tile, span), 0)
    lane = lax.broadcasted_iota(jnp.int32, (tile, span), 1)
    blocks = []
    for b in range(count):
        rows = gram[b * tile : (b + 1) * tile, :]
        rows = jnp.concatenate([rows, jnp.zeros_like(rows)], axis=1)
        blocks.append(jnp.where(lane == sublane + b * tile + columns, 1.0, rows))
    scales = [None] * count
    for start in range(0, columns, width):
        top = start // tile
        panel = [
            {b: spread(blocks[b][:, start + k : start + k + 1]) for b in range(top, count)}
            for k in range(width)
        ]
        for k in range(width):
            at, row = divmod(start + k, tile)
            pivot = spread(panel[k][at][row : row + 1, :])
            inverse = 1.0 / pivot
            ratio = {b: panel[k][b] * inverse for b in range(at, count)}
            ratio[at] = jnp.where(sublane > row, ratio[at], 0.0)
            root = lax.rsqrt(pivot)
            scales[at] = root if row == 0 else jnp.where(sublane == row, root, scales[at])
            for later in range(k + 1, width):
                to, below = divmod(start + later, tile)
                entry = spread(panel[k][to][below : below + 1, :])
                for b in range(at, count):
                    panel[later][b] = panel[later][b] - ratio[b] * entry
            pivot_row = spread(blocks[at][row : row + 1, :])
            for b in range(at, count):
                blocks[b] = blocks[b] - ratio[b] * pivot_row
    kept = []
    for b in range(count):
        row = sublane + b * tile
        kept.append(jnp.where((lane >= row) & (lane <= row + columns), blocks[b] * scales[b], 0.0))
    return jnp.concatenate(kept, axis=0)


def factor_kernel(total, sums, out):
    columns = sums.shape[0]
    out[...] = factor(sums[:, :columns] / total)


def finish_kernel(
    columns, cells, total, has_last, field_x, field_yz, m_x, m_yz, behind_x, behind_y, material,
    factors, proj, proj_other, out_basis, out_image, out_proj, out_upper,
):
    half = columns // 2
    inverse = factors[:, columns:]
    out_upper[...] = factors[:, :columns]
    raw = unpacked(proj[...] + proj_other[...]) / total
    left = lax.dot_general(
        inverse, raw, (((1,), (0,)), ((), ())), precision=HIGHEST, preferred_element_type=F32
    )
    out_proj[...] = inner(left, inverse)
    inside_last = has_last[0] > 0
    scaled_eps = material[cells:, :]
    stride = 3 * cells
    for y in range(cells):
        e = [part(field_x, y, columns), part(field_yz, y, columns), part(field_yz, cells + y, columns)]
        m = [part(m_x, y, columns), part(m_yz, y, columns), part(m_yz, cells + y, columns)]
        if y > 0:
            m_x_down, m_z_down = part(m_x, y - 1, columns), part(m_yz, cells + y - 1, columns)
        else:
            m_x_down = jnp.where(inside_last, behind_y[half : half + columns, :], 0.0)
            m_z_down = jnp.where(inside_last, behind_y[half + columns :, :], 0.0)
        mu_last = behind_x[2 * cells * columns + y : 2 * cells * columns + y + 1, :]
        m_y_last = part(behind_x, y, columns) - mu_last * e[2]
        m_z_last = part(behind_x, cells + y, columns) + mu_last * e[1]
        eps = scaled_eps[y : y + 1, :]
        image = [
            (m[2] - m_z_down) - backward_z(m[1]) - eps * e[0],
            backward_z(m[0]) - (m[2] - m_z_last) - eps * e[1],
            (m[1] - m_y_last) - (m[0] - m_x_down) - eps * e[2],
        ]
        both = lax.dot_general(
            inverse, wide(e + image), (((1,), (0,)), ((), ())), precision=HIGHEST,
            preferred_element_type=F32,
        )
        lanes = e[0].shape[1]
        for c in range(3):
            place = pl.ds(c * cells + y, columns, stride=stride)
            out_basis[place, :] = both[:, c * lanes : (c + 1) * lanes]
            out_image[place, :] = both[:, (3 + c) * lanes : (4 + c) * lanes]


def split_kernel(sums, out):
    columns = sums.shape[0]
    out[...] = packed(sums[:, columns:])


SMEM = pl.BlockSpec(memory_space=pltpu.SMEM)
VMEM = pl.BlockSpec(memory_space=pltpu.VMEM)


def call(body, scalars, arrays, outs, flops=None):
    shapes = [jax.ShapeDtypeStruct(shape, F32) for shape in outs]
    cost = None
    if flops is not None:
        cost = pl.CostEstimate(flops=flops, bytes_accessed=0, transcendentals=0)
    return pl.pallas_call(
        body,
        out_shape=shapes,
        in_specs=[SMEM] * len(scalars) + [VMEM] * len(arrays),
        out_specs=[VMEM] * len(shapes),
        cost_estimate=cost,
        compiler_params=pltpu.CompilerParams(vmem_limit_bytes=32 * 1024 * 1024),
    )(*scalars, *arrays)


def swapped(x, axis, step):
    return lax.ppermute(x, axis, [(i, i ^ step) for i in range(lax.axis_size(axis))])


def local(krylov_basis, regions, mu_table, eps_table, shift_value):
    columns, parts, layers, cells, lanes = krylov_basis.shape
    rows, cols = lax.axis_size("row"), lax.axis_size("col")
    assert layers == 1 and parts == 3 and cols == 2 and rows & (rows - 1) == 0
    total = 3 * cells * lanes * rows * cols
    basis = krylov_basis.reshape(-1, lanes)
    labels = regions[0]
    half = columns // 2
    small, large = (cells * columns, lanes), (2 * cells * columns, lanes)
    edge, pair = (half + 2 * columns, lanes), (half, 2 * columns)
    square = (columns, columns)
    place = lax.axis_index("col")
    has_next = jnp.where(place == 0, 1, 0).astype(jnp.int32)[None]
    has_last = 1 - has_next

    (material,) = call(
        material_kernel, (mu_table, eps_table, shift_value), (labels,), ((2 * cells, lanes),),
        flops=0,
    )
    field_x, field_yz = call(
        functools.partial(pack_kernel, columns, cells), (), (basis,), (small, large), flops=0
    )
    ahead_x = shifted(field_yz, "row", -1)
    (gram_edge,) = call(
        functools.partial(gram_kernel, columns, cells), (), (field_x, field_yz), (edge,), flops=0
    )
    ahead_y = swapped(gram_edge, "col", 1)
    sent, gram = call(
        functools.partial(behind_kernel, columns, cells),
        (has_next,),
        (field_x, field_yz, gram_edge, ahead_y, material),
        ((2 * cells * columns + -(-cells // 8) * 8, lanes), pair),
        flops=0,
    )
    gram_other = swapped(gram, "row", 1)
    behind_x = shifted(sent, "row", 1)
    m_x, near = call(
        functools.partial(near_kernel, columns, cells),
        (has_next,),
        (field_x, field_yz, ahead_y, material),
        (small, pair),
        flops=0,
    )
    m_yz, proj_edge = call(
        functools.partial(curl_kernel, columns, cells),
        (has_next,),
        (field_x, field_yz, ahead_x, ahead_y, material, m_x, near),
        (large, edge),
        flops=10**10,
    )
    (gram,) = call(add_kernel, (), (gram, gram_other), (pair,), flops=10**10)
    behind_y = swapped(proj_edge, "col", 1)
    (sums,) = call(
        join_kernel, (), (gram, proj_edge, behind_y), ((columns, 2 * columns),), flops=0
    )
    step = 2
    while step < rows:
        sums = sums + swapped(sums, "row", step)
        step *= 2
    (proj,) = call(split_kernel, (), (sums,), (pair,), flops=0)
    proj_other = swapped(proj, "row", 1)
    (factors,) = call(
        functools.partial(factor_kernel, total), (), (sums,), ((columns, 2 * columns),), flops=0
    )
    basis_out, image_out, projected, upper = call(
        functools.partial(finish_kernel, columns, cells, total),
        (has_last,),
        (field_x, field_yz, m_x, m_yz, behind_x, behind_y, material, factors, proj, proj_other),
        (basis.shape, basis.shape, square, square),
        flops=0,
    )
    return (
        basis_out.reshape(krylov_basis.shape),
        upper,
        image_out.reshape(krylov_basis.shape),
        projected,
    )


def solution(mesh):
    placed = (P("shift", None, "row", "col", None), P("row", "col", None), P(), P(), P("shift"))
    return jax.shard_map(
        local,
        mesh=mesh,
        in_specs=placed,
        out_specs=(
            P("shift", None, "row", "col", None),
            P("shift", None),
            P("shift", None, "row", "col", None),
            P("shift", None),
        ),
        check_vma=False,
    )
```

```python
import functools

import jax
import jax.numpy as jnp
from jax import lax
from jax.experimental import pallas as pl
from jax.experimental.pallas import tpu as pltpu
from jax.sharding import PartitionSpec as P

F32 = jnp.float32
BF16 = jnp.bfloat16


def shifted(x, axis, by):
    peers = lax.axis_size(axis)
    pairs = [(i, i + by) for i in range(peers) if 0 <= i + by < peers]
    return lax.ppermute(x, axis, pairs)


def wide(chunks):
    return jnp.concatenate(chunks, axis=1)


def three(values):
    high = values.astype(BF16)
    rest = values - high.astype(F32)
    middle = rest.astype(BF16)
    low = (rest - middle.astype(F32)).astype(BF16)
    return [high, middle, low]


def inner(left, right):
    return lax.dot_general(
        left, right, (((1,), (1,)), ((), ())), precision=lax.Precision.HIGHEST,
        preferred_element_type=F32,
    )


def product(left, right):
    rows = left.shape[0]
    high, middle, low = three(left)
    none = jnp.zeros_like(high)
    stacked = jnp.concatenate(
        [wide([high, high, high]), wide([middle, middle, none]), wide([low, none, none])], axis=0
    )
    blocks = lax.dot_general(
        stacked, jnp.concatenate(three(right), axis=0), (((1,), (0,)), ((), ())),
        preferred_element_type=F32,
    )
    return blocks[:rows, :] + (blocks[rows : 2 * rows, :] + blocks[2 * rows :, :])


def table_rows(labels, table_ref):
    result = jnp.zeros(labels.shape, F32)
    for region in range(table_ref.shape[0]):
        result = jnp.where(labels == region, table_ref[region], result)
    return result


def forward_z(values):
    lanes = values.shape[1]
    lane = lax.broadcasted_iota(jnp.int32, values.shape, 1)
    ahead = jnp.where(lane == lanes - 1, 0.0, pltpu.roll(values, lanes - 1, 1))
    return ahead - values


def backward_z(values):
    lane = lax.broadcasted_iota(jnp.int32, values.shape, 1)
    return values - jnp.where(lane == 0, 0.0, pltpu.roll(values, 1, 1))


def part(ref, index, columns):
    return ref[index * columns : (index + 1) * columns, :]


def packed(square):
    half = square.shape[0] // 2
    return jnp.concatenate([square[:half, :], square[half:, :]], axis=1)


def unpacked(pair):
    half = pair.shape[1] // 2
    return jnp.concatenate([pair[:, :half], pair[:, half:]], axis=0)


def pack_kernel(columns, cells, basis, out_x, out_yz):
    stride = 3 * cells
    for k in range(stride):
        ref, at = (out_x, k) if k < cells else (out_yz, k - cells)
        ref[at * columns : (at + 1) * columns, :] = basis[pl.ds(k, columns, stride=stride), :]


def material_kernel(mu_table, eps_table, shift, regions, out):
    labels = regions[...]
    cells = labels.shape[0]
    out[:cells, :] = table_rows(labels, mu_table)
    out[cells:, :] = shift[0] * table_rows(labels, eps_table)


def gram_kernel(columns, cells, field_x, field_yz, out):
    half = columns // 2
    chunks = [part(field_x, k, columns) for k in range(cells)]
    chunks += [part(field_yz, k, columns) for k in range(2 * cells)]
    flat = wide(chunks)
    out[half : half + columns, :] = chunks[0]
    out[half + columns :, :] = chunks[2 * cells]
    out[:half, :] = packed(inner(flat, flat))


def behind_kernel(
    columns, cells, has_next, field_x, field_yz, gram_edge, ahead_y, material, out, out_gram
):
    half = columns // 2
    out_gram[...] = gram_edge[:half, :] + ahead_y[:half, :]
    inside_next = has_next[0] > 0
    mu = material[:cells, :]
    for y in range(cells):
        e_x = part(field_x, y, columns)
        if y + 1 < cells:
            e_x_up = part(field_x, y + 1, columns)
        else:
            e_x_up = jnp.where(inside_next, ahead_y[half : half + columns, :], 0.0)
        e_y, e_z = part(field_yz, y, columns), part(field_yz, cells + y, columns)
        mu_row = mu[y : y + 1, :]
        out[y * columns : (y + 1) * columns, :] = mu_row * (forward_z(e_x) + e_z)
        out[(cells + y) * columns : (cells + y + 1) * columns, :] = -mu_row * (e_y + (e_x_up - e_x))
    out[2 * cells * columns :, :] = jnp.concatenate(
        [mu, jnp.zeros((out.shape[0] - 2 * cells * columns - cells, mu.shape[1]), F32)], axis=0
    )


def near_kernel(columns, cells, has_next, field_x, field_yz, ahead_y, material, out_x, out_proj):
    half = columns // 2
    inside_next = has_next[0] > 0
    left, right = [], []
    for y in range(cells):
        e_x = part(field_x, y, columns)
        e_y = part(field_yz, y, columns)
        e_z = part(field_yz, cells + y, columns)
        if y + 1 < cells:
            e_z_up = part(field_yz, cells + y + 1, columns)
        else:
            e_z_up = jnp.where(inside_next, ahead_y[half + columns :, :], 0.0)
        curl_x = (e_z_up - e_z) - forward_z(e_y)
        m_x = material[y : y + 1, :] * curl_x
        eps = -material[cells + y : cells + y + 1, :]
        out_x[y * columns : (y + 1) * columns, :] = m_x
        left += [curl_x, e_x, e_y, e_z]
        right += [m_x, eps * e_x, eps * e_y, eps * e_z]
    out_proj[...] = packed(inner(wide(left), wide(right)))


def curl_kernel(
    columns, cells, has_next, field_x, field_yz, ahead_x, ahead_y, material, m_x, near, out_yz,
    out_edge,
):
    half = columns // 2
    inside_next = has_next[0] > 0
    left, right = [], []
    for y in range(cells):
        e_x = part(field_x, y, columns)
        e_y = part(field_yz, y, columns)
        e_z = part(field_yz, cells + y, columns)
        if y + 1 < cells:
            e_x_up = part(field_x, y + 1, columns)
        else:
            e_x_up = jnp.where(inside_next, ahead_y[half : half + columns, :], 0.0)
        curl_y = forward_z(e_x) - (part(ahead_x, cells + y, columns) - e_z)
        curl_z = (part(ahead_x, y, columns) - e_y) - (e_x_up - e_x)
        mu = material[y : y + 1, :]
        m_y, m_z = mu * curl_y, mu * curl_z
        out_yz[y * columns : (y + 1) * columns, :] = m_y
        out_yz[(cells + y) * columns : (cells + y + 1) * columns, :] = m_z
        if y + 1 == cells:
            out_edge[half + columns :, :] = m_z
        left += [curl_y, curl_z]
        right += [m_y, m_z]
    out_edge[half : half + columns, :] = part(m_x, cells - 1, columns)
    out_edge[:half, :] = near[...] + packed(inner(wide(left), wide(right)))


def add_kernel(left, right, out):
    out[...] = left[...] + right[...]


def join_kernel(gram, edge, edge_other, out):
    half, columns = gram.shape[0], 2 * gram.shape[0]
    proj = edge[:half, :] + edge_other[:half, :]
    out[:, :columns] = unpacked(gram[...])
    out[:, columns:] = unpacked(proj)


def factor(gram):
    columns = gram.shape[0]
    span, tile, width = 2 * columns, 8, 16
    count = columns // tile
    spread = lambda values: jnp.broadcast_to(values, (tile, span))
    sublane = lax.broadcasted_iota(jnp.int32, (tile, span), 0)
    lane = lax.broadcasted_iota(jnp.int32, (tile, span), 1)
    blocks = []
    for b in range(count):
        rows = gram[b * tile : (b + 1) * tile, :]
        rows = jnp.concatenate([rows, jnp.zeros_like(rows)], axis=1)
        blocks.append(jnp.where(lane == sublane + b * tile + columns, 1.0, rows))
    scales = [None] * count
    for start in range(0, columns, width):
        top = start // tile
        panel = [
            {b: spread(blocks[b][:, start + k : start + k + 1]) for b in range(top, count)}
            for k in range(width)
        ]
        for k in range(width):
            at, row = divmod(start + k, tile)
            pivot = spread(panel[k][at][row : row + 1, :])
            inverse = 1.0 / pivot
            ratio = {b: panel[k][b] * inverse for b in range(at, count)}
            ratio[at] = jnp.where(sublane > row, ratio[at], 0.0)
            root = lax.rsqrt(pivot)
            scales[at] = root if row == 0 else jnp.where(sublane == row, root, scales[at])
            for later in range(k + 1, width):
                to, below = divmod(start + later, tile)
                entry = spread(panel[k][to][below : below + 1, :])
                for b in range(at, count):
                    panel[later][b] = panel[later][b] - ratio[b] * entry
            pivot_row = spread(blocks[at][row : row + 1, :])
            for b in range(at, count):
                blocks[b] = blocks[b] - ratio[b] * pivot_row
    kept = []
    for b in range(count):
        row = sublane + b * tile
        kept.append(jnp.where((lane >= row) & (lane <= row + columns), blocks[b] * scales[b], 0.0))
    return jnp.concatenate(kept, axis=0)


def factor_kernel(total, sums, out):
    columns = sums.shape[0]
    out[...] = factor(sums[:, :columns] / total)


def basis_kernel(
    columns, cells, total, has_last, field_x, field_yz, m_x, m_yz, behind_x, behind_y, material,
    factors, proj, proj_other, out_basis, out_image, out_upper, out_proj, basis, image, upper,
    projected, sems,
):
    half = columns // 2
    stride = 3 * cells
    inverse = factors[:, columns:]
    upper[...] = factors[:, :columns]
    third = pltpu.make_async_copy(upper, out_upper, sems.at[2])
    third.start()

    def write(chunks, places, held, target, sem):
        lanes = chunks[0].shape[1]
        whole = product(inverse, wide(chunks))
        for i, k in enumerate(places):
            held[pl.ds(k, columns, stride=stride), :] = whole[:, i * lanes : (i + 1) * lanes]
        copy = pltpu.make_async_copy(held, target, sem)
        copy.start()
        return copy

    fields = [part(field_x, y, columns) for y in range(cells)]
    fields += [part(field_yz, k, columns) for k in range(2 * cells)]
    first = write(fields, range(stride), basis, out_basis, sems.at[0])
    inside_last = has_last[0] > 0
    scaled_eps = material[cells:, :]
    images, places = [], []
    for y in range(cells):
        e = [part(field_x, y, columns), part(field_yz, y, columns), part(field_yz, cells + y, columns)]
        m = [part(m_x, y, columns), part(m_yz, y, columns), part(m_yz, cells + y, columns)]
        if y > 0:
            m_x_down, m_z_down = part(m_x, y - 1, columns), part(m_yz, cells + y - 1, columns)
        else:
            m_x_down = jnp.where(inside_last, behind_y[half : half + columns, :], 0.0)
            m_z_down = jnp.where(inside_last, behind_y[half + columns :, :], 0.0)
        mu_last = behind_x[2 * cells * columns + y : 2 * cells * columns + y + 1, :]
        m_y_last = part(behind_x, y, columns) - mu_last * e[2]
        m_z_last = part(behind_x, cells + y, columns) + mu_last * e[1]
        eps = scaled_eps[y : y + 1, :]
        images += [
            (m[2] - m_z_down) - backward_z(m[1]) - eps * e[0],
            backward_z(m[0]) - (m[2] - m_z_last) - eps * e[1],
            (m[1] - m_y_last) - (m[0] - m_x_down) - eps * e[2],
        ]
        places += [y, cells + y, 2 * cells + y]
    second = write(images, places, image, out_image, sems.at[1])
    raw = unpacked(proj[...] + proj_other[...]) / total
    left = lax.dot_general(
        inverse, raw, (((1,), (0,)), ((), ())), precision=lax.Precision.HIGHEST,
        preferred_element_type=F32,
    )
    projected[...] = inner(left, inverse)
    fourth = pltpu.make_async_copy(projected, out_proj, sems.at[3])
    fourth.start()
    first.wait()
    second.wait()
    third.wait()
    fourth.wait()


def split_kernel(sums, out):
    columns = sums.shape[0]
    out[...] = packed(sums[:, columns:])


SMEM = pl.BlockSpec(memory_space=pltpu.SMEM)
VMEM = pl.BlockSpec(memory_space=pltpu.VMEM)
ANY = pl.BlockSpec(memory_space=pl.ANY)


def call(body, scalars, arrays, outs, flops=None, far=0, scratch=()):
    shapes = [jax.ShapeDtypeStruct(shape, F32) for shape in outs]
    cost = None
    if flops is not None:
        cost = pl.CostEstimate(flops=flops, bytes_accessed=0, transcendentals=0)
    return pl.pallas_call(
        body,
        out_shape=shapes,
        in_specs=[SMEM] * len(scalars) + [VMEM] * len(arrays),
        out_specs=[ANY] * far + [VMEM] * (len(shapes) - far),
        scratch_shapes=scratch,
        cost_estimate=cost,
        compiler_params=pltpu.CompilerParams(vmem_limit_bytes=32 * 1024 * 1024),
    )(*scalars, *arrays)


def swapped(x, axis, step):
    return lax.ppermute(x, axis, [(i, i ^ step) for i in range(lax.axis_size(axis))])


def local(krylov_basis, regions, mu_table, eps_table, shift_value):
    columns, parts, layers, cells, lanes = krylov_basis.shape
    rows, cols = lax.axis_size("row"), lax.axis_size("col")
    assert layers == 1 and parts == 3 and cols == 2 and rows & (rows - 1) == 0
    total = 3 * cells * lanes * rows * cols
    basis = krylov_basis.reshape(-1, lanes)
    labels = regions[0]
    half = columns // 2
    small, large = (cells * columns, lanes), (2 * cells * columns, lanes)
    edge, pair = (half + 2 * columns, lanes), (half, 2 * columns)
    square = (columns, columns)
    place = lax.axis_index("col")
    has_next = jnp.where(place == 0, 1, 0).astype(jnp.int32)[None]
    has_last = 1 - has_next

    (material,) = call(
        material_kernel, (mu_table, eps_table, shift_value), (labels,), ((2 * cells, lanes),),
        flops=0,
    )
    field_x, field_yz = call(
        functools.partial(pack_kernel, columns, cells), (), (basis,), (small, large), flops=0
    )
    ahead_x = shifted(field_yz, "row", -1)
    (gram_edge,) = call(
        functools.partial(gram_kernel, columns, cells), (), (field_x, field_yz), (edge,), flops=0
    )
    ahead_y = swapped(gram_edge, "col", 1)
    sent, gram = call(
        functools.partial(behind_kernel, columns, cells),
        (has_next,),
        (field_x, field_yz, gram_edge, ahead_y, material),
        ((2 * cells * columns + -(-cells // 8) * 8, lanes), pair),
        flops=0,
    )
    gram_other = swapped(gram, "row", 1)
    behind_x = shifted(sent, "row", 1)
    m_x, near = call(
        functools.partial(near_kernel, columns, cells),
        (has_next,),
        (field_x, field_yz, ahead_y, material),
        (small, pair),
        flops=0,
    )
    m_yz, proj_edge = call(
        functools.partial(curl_kernel, columns, cells),
        (has_next,),
        (field_x, field_yz, ahead_x, ahead_y, material, m_x, near),
        (large, edge),
        flops=10**10,
    )
    (gram,) = call(add_kernel, (), (gram, gram_other), (pair,), flops=10**10)
    behind_y = swapped(proj_edge, "col", 1)
    (sums,) = call(
        join_kernel, (), (gram, proj_edge, behind_y), ((columns, 2 * columns),), flops=0
    )
    step = 2
    while step < rows:
        sums = sums + swapped(sums, "row", step)
        step *= 2
    (proj,) = call(split_kernel, (), (sums,), (pair,), flops=0)
    proj_other = swapped(proj, "row", 1)
    (factors,) = call(
        functools.partial(factor_kernel, total), (), (sums,), ((columns, 2 * columns),), flops=0
    )
    basis_out, image_out, upper, projected = call(
        functools.partial(basis_kernel, columns, cells, total),
        (has_last,),
        (
            field_x, field_yz, m_x, m_yz, behind_x, behind_y, material, factors, proj,
            proj_other,
        ),
        (basis.shape, basis.shape, square, square),
        flops=0,
        far=4,
        scratch=[
            pltpu.VMEM(basis.shape, F32),
            pltpu.VMEM(basis.shape, F32),
            pltpu.VMEM(square, F32),
            pltpu.VMEM(square, F32),
            pltpu.SemaphoreType.DMA((4,)),
        ],
    )
    return (
        basis_out.reshape(krylov_basis.shape),
        upper,
        image_out.reshape(krylov_basis.shape),
        projected,
    )


def solution(mesh):
    placed = (P("shift", None, "row", "col", None), P("row", "col", None), P(), P(), P("shift"))
    return jax.shard_map(
        local,
        mesh=mesh,
        in_specs=placed,
        out_specs=(
            P("shift", None, "row", "col", None),
            P("shift", None),
            P("shift", None, "row", "col", None),
            P("shift", None),
        ),
        check_vma=False,
    )
```

```python
import functools

import jax
import jax.numpy as jnp
from jax import lax
from jax.experimental import pallas as pl
from jax.experimental.pallas import tpu as pltpu
from jax.sharding import PartitionSpec as P

F32 = jnp.float32
BF16 = jnp.bfloat16


def shifted(x, axis, by):
    peers = lax.axis_size(axis)
    pairs = [(i, i + by) for i in range(peers) if 0 <= i + by < peers]
    return lax.ppermute(x, axis, pairs)


def wide(chunks):
    return jnp.concatenate(chunks, axis=1)


def three(values):
    high = values.astype(BF16)
    rest = values - high.astype(F32)
    middle = rest.astype(BF16)
    low = (rest - middle.astype(F32)).astype(BF16)
    return [high, middle, low]


def inner(left, right):
    return lax.dot_general(
        left, right, (((1,), (1,)), ((), ())), precision=lax.Precision.HIGHEST,
        preferred_element_type=F32,
    )


def product(left, right):
    rows = left.shape[0]
    high, middle, low = three(left)
    none = jnp.zeros_like(high)
    stacked = jnp.concatenate(
        [wide([high, high, high]), wide([middle, middle, none]), wide([low, none, none])], axis=0
    )
    blocks = lax.dot_general(
        stacked, jnp.concatenate(three(right), axis=0), (((1,), (0,)), ((), ())),
        preferred_element_type=F32,
    )
    return blocks[:rows, :] + (blocks[rows : 2 * rows, :] + blocks[2 * rows :, :])


def table_rows(labels, table_ref):
    result = jnp.zeros(labels.shape, F32)
    for region in range(table_ref.shape[0]):
        result = jnp.where(labels == region, table_ref[region], result)
    return result


def forward_z(values):
    lanes = values.shape[1]
    lane = lax.broadcasted_iota(jnp.int32, values.shape, 1)
    ahead = jnp.where(lane == lanes - 1, 0.0, pltpu.roll(values, lanes - 1, 1))
    return ahead - values


def backward_z(values):
    lane = lax.broadcasted_iota(jnp.int32, values.shape, 1)
    return values - jnp.where(lane == 0, 0.0, pltpu.roll(values, 1, 1))


def part(ref, index, columns):
    return ref[index * columns : (index + 1) * columns, :]


def packed(square):
    half = square.shape[0] // 2
    return jnp.concatenate([square[:half, :], square[half:, :]], axis=1)


def unpacked(pair):
    half = pair.shape[1] // 2
    return jnp.concatenate([pair[:, :half], pair[:, half:]], axis=0)


def pack_kernel(columns, cells, basis, out_x, out_yz):
    stride = 3 * cells
    for k in range(stride):
        ref, at = (out_x, k) if k < cells else (out_yz, k - cells)
        ref[at * columns : (at + 1) * columns, :] = basis[pl.ds(k, columns, stride=stride), :]


def material_kernel(mu_table, eps_table, shift, regions, out):
    labels = regions[...]
    cells = labels.shape[0]
    out[:cells, :] = table_rows(labels, mu_table)
    out[cells:, :] = shift[0] * table_rows(labels, eps_table)


def gram_kernel(columns, cells, field_x, field_yz, out):
    half = columns // 2
    chunks = [part(field_x, k, columns) for k in range(cells)]
    chunks += [part(field_yz, k, columns) for k in range(2 * cells)]
    flat = wide(chunks)
    out[half : half + columns, :] = chunks[0]
    out[half + columns :, :] = chunks[2 * cells]
    out[:half, :] = packed(inner(flat, flat))


def behind_kernel(
    columns, cells, has_next, field_x, field_yz, gram_edge, ahead_y, material, out, out_gram
):
    half = columns // 2
    out_gram[...] = gram_edge[:half, :] + ahead_y[:half, :]
    inside_next = has_next[0] > 0
    mu = material[:cells, :]
    for y in range(cells):
        e_x = part(field_x, y, columns)
        if y + 1 < cells:
            e_x_up = part(field_x, y + 1, columns)
        else:
            e_x_up = jnp.where(inside_next, ahead_y[half : half + columns, :], 0.0)
        e_y, e_z = part(field_yz, y, columns), part(field_yz, cells + y, columns)
        mu_row = mu[y : y + 1, :]
        out[y * columns : (y + 1) * columns, :] = mu_row * (forward_z(e_x) + e_z)
        out[(cells + y) * columns : (cells + y + 1) * columns, :] = -mu_row * (e_y + (e_x_up - e_x))
    out[2 * cells * columns :, :] = jnp.concatenate(
        [mu, jnp.zeros((out.shape[0] - 2 * cells * columns - cells, mu.shape[1]), F32)], axis=0
    )


def near_kernel(columns, cells, has_next, field_x, field_yz, ahead_y, material, out_x, out_proj):
    half = columns // 2
    inside_next = has_next[0] > 0
    left, right = [], []
    for y in range(cells):
        e_x = part(field_x, y, columns)
        e_y = part(field_yz, y, columns)
        e_z = part(field_yz, cells + y, columns)
        if y + 1 < cells:
            e_z_up = part(field_yz, cells + y + 1, columns)
        else:
            e_z_up = jnp.where(inside_next, ahead_y[half + columns :, :], 0.0)
        curl_x = (e_z_up - e_z) - forward_z(e_y)
        m_x = material[y : y + 1, :] * curl_x
        eps = -material[cells + y : cells + y + 1, :]
        out_x[y * columns : (y + 1) * columns, :] = m_x
        left += [curl_x, e_x, e_y, e_z]
        right += [m_x, eps * e_x, eps * e_y, eps * e_z]
    out_proj[...] = packed(inner(wide(left), wide(right)))


def curl_kernel(
    columns, cells, has_next, field_x, field_yz, ahead_x, ahead_y, material, m_x, near, out_yz,
    out_edge,
):
    half = columns // 2
    inside_next = has_next[0] > 0
    left, right = [], []
    for y in range(cells):
        e_x = part(field_x, y, columns)
        e_y = part(field_yz, y, columns)
        e_z = part(field_yz, cells + y, columns)
        if y + 1 < cells:
            e_x_up = part(field_x, y + 1, columns)
        else:
            e_x_up = jnp.where(inside_next, ahead_y[half : half + columns, :], 0.0)
        curl_y = forward_z(e_x) - (part(ahead_x, cells + y, columns) - e_z)
        curl_z = (part(ahead_x, y, columns) - e_y) - (e_x_up - e_x)
        mu = material[y : y + 1, :]
        m_y, m_z = mu * curl_y, mu * curl_z
        out_yz[y * columns : (y + 1) * columns, :] = m_y
        out_yz[(cells + y) * columns : (cells + y + 1) * columns, :] = m_z
        if y + 1 == cells:
            out_edge[half + columns :, :] = m_z
        left += [curl_y, curl_z]
        right += [m_y, m_z]
    out_edge[half : half + columns, :] = part(m_x, cells - 1, columns)
    out_edge[:half, :] = near[...] + packed(inner(wide(left), wide(right)))


def add_kernel(left, right, out):
    out[...] = left[...] + right[...]


def join_kernel(gram, edge, edge_other, out):
    half = gram.shape[0]
    out[:half, :] = gram[...]
    out[half:, :] = edge[:half, :] + edge_other[:half, :]


def sum_kernel(own, both, out, out_proj):
    half = out_proj.shape[0]
    total = own[...] + both[...]
    out[...] = total
    out_proj[...] = total[half:, :]


def factor(gram):
    columns = gram.shape[0]
    span, tile, width = 2 * columns, 8, 16
    count = columns // tile
    spread = lambda values: jnp.broadcast_to(values, (tile, span))
    sublane = lax.broadcasted_iota(jnp.int32, (tile, span), 0)
    lane = lax.broadcasted_iota(jnp.int32, (tile, span), 1)
    blocks = []
    for b in range(count):
        rows = gram[b * tile : (b + 1) * tile, :]
        rows = jnp.concatenate([rows, jnp.zeros_like(rows)], axis=1)
        blocks.append(jnp.where(lane == sublane + b * tile + columns, 1.0, rows))
    scales = [None] * count
    for start in range(0, columns, width):
        top = start // tile
        panel = [
            {b: spread(blocks[b][:, start + k : start + k + 1]) for b in range(top, count)}
            for k in range(width)
        ]
        for k in range(width):
            at, row = divmod(start + k, tile)
            pivot = spread(panel[k][at][row : row + 1, :])
            inverse = 1.0 / pivot
            ratio = {b: panel[k][b] * inverse for b in range(at, count)}
            ratio[at] = jnp.where(sublane > row, ratio[at], 0.0)
            root = lax.rsqrt(pivot)
            scales[at] = root if row == 0 else jnp.where(sublane == row, root, scales[at])
            for later in range(k + 1, width):
                to, below = divmod(start + later, tile)
                entry = spread(panel[k][to][below : below + 1, :])
                for b in range(at, count):
                    panel[later][b] = panel[later][b] - ratio[b] * entry
            pivot_row = spread(blocks[at][row : row + 1, :])
            for b in range(at, count):
                blocks[b] = blocks[b] - ratio[b] * pivot_row
    kept = []
    for b in range(count):
        row = sublane + b * tile
        kept.append(jnp.where((lane >= row) & (lane <= row + columns), blocks[b] * scales[b], 0.0))
    return jnp.concatenate(kept, axis=0)


def factor_kernel(total, sums, far, out):
    half = sums.shape[0] // 2
    out[...] = factor(unpacked(sums[:half, :] + far[:half, :]) / total)


def basis_kernel(
    columns, cells, has_last, field_x, field_yz, m_x, m_yz, behind_x, behind_y, material, factors,
    out_basis, out_image, out_upper, out_inverse, basis, image, upper, sems,
):
    half = columns // 2
    stride = 3 * cells
    inverse = factors[:, columns:]
    out_inverse[...] = inverse
    upper[...] = factors[:, :columns]
    third = pltpu.make_async_copy(upper, out_upper, sems.at[2])
    third.start()

    def write(chunks, places, held, target, sem):
        lanes = chunks[0].shape[1]
        whole = product(inverse, wide(chunks))
        for i, k in enumerate(places):
            held[pl.ds(k, columns, stride=stride), :] = whole[:, i * lanes : (i + 1) * lanes]
        copy = pltpu.make_async_copy(held, target, sem)
        copy.start()
        return copy

    fields = [part(field_x, y, columns) for y in range(cells)]
    fields += [part(field_yz, k, columns) for k in range(2 * cells)]
    first = write(fields, range(stride), basis, out_basis, sems.at[0])
    inside_last = has_last[0] > 0
    scaled_eps = material[cells:, :]
    images, places = [], []
    for y in range(cells):
        e = [part(field_x, y, columns), part(field_yz, y, columns), part(field_yz, cells + y, columns)]
        m = [part(m_x, y, columns), part(m_yz, y, columns), part(m_yz, cells + y, columns)]
        if y > 0:
            m_x_down, m_z_down = part(m_x, y - 1, columns), part(m_yz, cells + y - 1, columns)
        else:
            m_x_down = jnp.where(inside_last, behind_y[half : half + columns, :], 0.0)
            m_z_down = jnp.where(inside_last, behind_y[half + columns :, :], 0.0)
        mu_last = behind_x[2 * cells * columns + y : 2 * cells * columns + y + 1, :]
        m_y_last = part(behind_x, y, columns) - mu_last * e[2]
        m_z_last = part(behind_x, cells + y, columns) + mu_last * e[1]
        eps = scaled_eps[y : y + 1, :]
        images += [
            (m[2] - m_z_down) - backward_z(m[1]) - eps * e[0],
            backward_z(m[0]) - (m[2] - m_z_last) - eps * e[1],
            (m[1] - m_y_last) - (m[0] - m_x_down) - eps * e[2],
        ]
        places += [y, cells + y, 2 * cells + y]
    second = write(images, places, image, out_image, sems.at[1])
    first.wait()
    second.wait()
    third.wait()


def proj_kernel(total, inverse, proj, far_cross, far, near, out):
    half = proj.shape[0]
    raw = (proj[...] + near[...]) + (far[half:, :] + far_cross[...])
    left = lax.dot_general(
        inverse[...], unpacked(raw) / total, (((1,), (0,)), ((), ())),
        precision=lax.Precision.HIGHEST, preferred_element_type=F32,
    )
    out[...] = inner(left, inverse[...])


SMEM = pl.BlockSpec(memory_space=pltpu.SMEM)
VMEM = pl.BlockSpec(memory_space=pltpu.VMEM)
ANY = pl.BlockSpec(memory_space=pl.ANY)


def call(body, scalars, arrays, outs, flops=None, far=0, scratch=()):
    shapes = [jax.ShapeDtypeStruct(shape, F32) for shape in outs]
    cost = None
    if flops is not None:
        cost = pl.CostEstimate(flops=flops, bytes_accessed=0, transcendentals=0)
    return pl.pallas_call(
        body,
        out_shape=shapes,
        in_specs=[SMEM] * len(scalars) + [VMEM] * len(arrays),
        out_specs=[ANY] * far + [VMEM] * (len(shapes) - far),
        scratch_shapes=scratch,
        cost_estimate=cost,
        compiler_params=pltpu.CompilerParams(vmem_limit_bytes=32 * 1024 * 1024),
    )(*scalars, *arrays)


def swapped(x, axis, step):
    return lax.ppermute(x, axis, [(i, i ^ step) for i in range(lax.axis_size(axis))])


def local(krylov_basis, regions, mu_table, eps_table, shift_value):
    columns, parts, layers, cells, lanes = krylov_basis.shape
    rows, cols = lax.axis_size("row"), lax.axis_size("col")
    assert layers == 1 and parts == 3 and cols == 2 and rows >= 8 and rows & (rows - 1) == 0
    total = 3 * cells * lanes * rows * cols
    basis = krylov_basis.reshape(-1, lanes)
    labels = regions[0]
    half, outer = columns // 2, rows // 2
    small, large = (cells * columns, lanes), (2 * cells * columns, lanes)
    edge, pair = (half + 2 * columns, lanes), (half, 2 * columns)
    square = (columns, columns)
    place = lax.axis_index("col")
    has_next = jnp.where(place == 0, 1, 0).astype(jnp.int32)[None]
    has_last = 1 - has_next

    (material,) = call(
        material_kernel, (mu_table, eps_table, shift_value), (labels,), ((2 * cells, lanes),),
        flops=0,
    )
    field_x, field_yz = call(
        functools.partial(pack_kernel, columns, cells), (), (basis,), (small, large), flops=0
    )
    ahead_x = shifted(field_yz, "row", -1)
    (gram_edge,) = call(
        functools.partial(gram_kernel, columns, cells), (), (field_x, field_yz), (edge,), flops=0
    )
    ahead_y = swapped(gram_edge, "col", 1)
    sent, gram = call(
        functools.partial(behind_kernel, columns, cells),
        (has_next,),
        (field_x, field_yz, gram_edge, ahead_y, material),
        ((2 * cells * columns + -(-cells // 8) * 8, lanes), pair),
        flops=0,
    )
    gram_other = swapped(gram, "row", 1)
    behind_x = shifted(sent, "row", 1)
    m_x, near = call(
        functools.partial(near_kernel, columns, cells),
        (has_next,),
        (field_x, field_yz, ahead_y, material),
        (small, pair),
        flops=0,
    )
    m_yz, proj_edge = call(
        functools.partial(curl_kernel, columns, cells),
        (has_next,),
        (field_x, field_yz, ahead_x, ahead_y, material, m_x, near),
        (large, edge),
        flops=10**10,
    )
    both = (2 * half, 2 * columns)
    (gram,) = call(add_kernel, (), (gram, gram_other), (pair,), flops=10**10)
    behind_y = swapped(proj_edge, "col", 1)
    (own,) = call(join_kernel, (), (gram, proj_edge, behind_y), (both,), flops=0)
    next_both = swapped(own, "row", 2)
    sums, proj = call(sum_kernel, (), (own, next_both), (both, pair), flops=0)
    step = 4
    while step < outer:
        sums = sums + swapped(sums, "row", step)
        proj = sums[half:]
        step *= 2
    far = swapped(sums, "row", outer)
    proj_near = swapped(proj, "row", 1)
    far_cross = swapped(proj, "row", outer + 1)
    (factors,) = call(
        functools.partial(factor_kernel, total), (), (sums, far), ((columns, 2 * columns),), flops=0
    )
    basis_out, image_out, upper, inverse = call(
        functools.partial(basis_kernel, columns, cells),
        (has_last,),
        (field_x, field_yz, m_x, m_yz, behind_x, behind_y, material, factors),
        (basis.shape, basis.shape, square, square),
        flops=0,
        far=3,
        scratch=[
            pltpu.VMEM(basis.shape, F32),
            pltpu.VMEM(basis.shape, F32),
            pltpu.VMEM(square, F32),
            pltpu.SemaphoreType.DMA((3,)),
        ],
    )
    (projected,) = call(
        functools.partial(proj_kernel, total),
        (),
        (inverse, proj, far_cross, far, proj_near),
        (square,),
        flops=0,
    )
    return (
        basis_out.reshape(krylov_basis.shape),
        upper,
        image_out.reshape(krylov_basis.shape),
        projected,
    )


def solution(mesh):
    placed = (P("shift", None, "row", "col", None), P("row", "col", None), P(), P(), P("shift"))
    return jax.shard_map(
        local,
        mesh=mesh,
        in_specs=placed,
        out_specs=(
            P("shift", None, "row", "col", None),
            P("shift", None),
            P("shift", None, "row", "col", None),
            P("shift", None),
        ),
        check_vma=False,
    )
```

```python
import functools

import jax
import jax.numpy as jnp
from jax import lax
from jax.experimental import pallas as pl
from jax.experimental.pallas import tpu as pltpu
from jax.sharding import PartitionSpec as P

F32 = jnp.float32
BF16 = jnp.bfloat16


def shifted(x, axis, by):
    peers = lax.axis_size(axis)
    pairs = [(i, i + by) for i in range(peers) if 0 <= i + by < peers]
    return lax.ppermute(x, axis, pairs)


def ringed(x, axis, by):
    peers = lax.axis_size(axis)
    return lax.ppermute(x, axis, [(i, (i + by) % peers) for i in range(peers)])


def wide(chunks):
    return jnp.concatenate(chunks, axis=1)


def three(values):
    high = values.astype(BF16)
    rest = values - high.astype(F32)
    middle = rest.astype(BF16)
    low = (rest - middle.astype(F32)).astype(BF16)
    return [high, middle, low]


def inner(left, right):
    return lax.dot_general(
        left, right, (((1,), (1,)), ((), ())), precision=lax.Precision.HIGHEST,
        preferred_element_type=F32,
    )


def product(left, right):
    rows = left.shape[0]
    high, middle, low = three(left)
    none = jnp.zeros_like(high)
    stacked = jnp.concatenate(
        [wide([high, high, high]), wide([middle, middle, none]), wide([low, none, none])], axis=0
    )
    blocks = lax.dot_general(
        stacked, jnp.concatenate(three(right), axis=0), (((1,), (0,)), ((), ())),
        preferred_element_type=F32,
    )
    return blocks[:rows, :] + (blocks[rows : 2 * rows, :] + blocks[2 * rows :, :])


def table_rows(labels, table_ref):
    result = jnp.zeros(labels.shape, F32)
    for region in range(table_ref.shape[0]):
        result = jnp.where(labels == region, table_ref[region], result)
    return result


def forward_z(values):
    lanes = values.shape[1]
    lane = lax.broadcasted_iota(jnp.int32, values.shape, 1)
    ahead = jnp.where(lane == lanes - 1, 0.0, pltpu.roll(values, lanes - 1, 1))
    return ahead - values


def backward_z(values):
    lane = lax.broadcasted_iota(jnp.int32, values.shape, 1)
    return values - jnp.where(lane == 0, 0.0, pltpu.roll(values, 1, 1))


def part(ref, index, columns):
    return ref[index * columns : (index + 1) * columns, :]


def packed(square):
    half = square.shape[0] // 2
    return jnp.concatenate([square[:half, :], square[half:, :]], axis=1)


def unpacked(pair):
    half = pair.shape[1] // 2
    return jnp.concatenate([pair[:, :half], pair[:, half:]], axis=0)


def pack_kernel(columns, cells, basis, out_x, out_yz):
    stride = 3 * cells
    for k in range(stride):
        ref, at = (out_x, k) if k < cells else (out_yz, k - cells)
        ref[at * columns : (at + 1) * columns, :] = basis[pl.ds(k, columns, stride=stride), :]


def material_kernel(mu_table, eps_table, shift, regions, out):
    labels = regions[...]
    cells = labels.shape[0]
    out[:cells, :] = table_rows(labels, mu_table)
    out[cells:, :] = shift[0] * table_rows(labels, eps_table)


def gram_kernel(columns, cells, field_x, field_yz, out):
    half = columns // 2
    chunks = [part(field_x, k, columns) for k in range(cells)]
    chunks += [part(field_yz, k, columns) for k in range(2 * cells)]
    flat = wide(chunks)
    out[half : half + columns, :] = chunks[0]
    out[half + columns :, :] = chunks[2 * cells]
    out[:half, :] = packed(inner(flat, flat))


def behind_kernel(
    columns, cells, field_x, field_yz, gram_edge, ahead_y, material, out, out_gram
):
    half = columns // 2
    out_gram[...] = gram_edge[:half, :] + ahead_y[:half, :]
    inside_next = lax.axis_index("col") + 1 < lax.axis_size("col")
    mu = material[:cells, :]
    for y in range(cells):
        e_x = part(field_x, y, columns)
        if y + 1 < cells:
            e_x_up = part(field_x, y + 1, columns)
        else:
            e_x_up = jnp.where(inside_next, ahead_y[half : half + columns, :], 0.0)
        e_y, e_z = part(field_yz, y, columns), part(field_yz, cells + y, columns)
        mu_row = mu[y : y + 1, :]
        out[y * columns : (y + 1) * columns, :] = mu_row * (forward_z(e_x) + e_z)
        out[(cells + y) * columns : (cells + y + 1) * columns, :] = -mu_row * (e_y + (e_x_up - e_x))
    out[2 * cells * columns :, :] = jnp.concatenate(
        [mu, jnp.zeros((out.shape[0] - 2 * cells * columns - cells, mu.shape[1]), F32)], axis=0
    )


def near_kernel(columns, cells, field_x, field_yz, ahead_y, material, out_x, out_proj):
    half = columns // 2
    inside_next = lax.axis_index("col") + 1 < lax.axis_size("col")
    left, right = [], []
    for y in range(cells):
        e_x = part(field_x, y, columns)
        e_y = part(field_yz, y, columns)
        e_z = part(field_yz, cells + y, columns)
        if y + 1 < cells:
            e_z_up = part(field_yz, cells + y + 1, columns)
        else:
            e_z_up = jnp.where(inside_next, ahead_y[half + columns :, :], 0.0)
        curl_x = (e_z_up - e_z) - forward_z(e_y)
        m_x = material[y : y + 1, :] * curl_x
        eps = -material[cells + y : cells + y + 1, :]
        out_x[y * columns : (y + 1) * columns, :] = m_x
        left += [curl_x, e_x, e_y, e_z]
        right += [m_x, eps * e_x, eps * e_y, eps * e_z]
    out_proj[...] = packed(inner(wide(left), wide(right)))


def curl_kernel(
    columns, cells, field_x, field_yz, ahead_x, ahead_y, material, m_x, near, out_yz,
    out_edge,
):
    half = columns // 2
    inside_next = lax.axis_index("col") + 1 < lax.axis_size("col")
    left, right = [], []
    for y in range(cells):
        e_x = part(field_x, y, columns)
        e_y = part(field_yz, y, columns)
        e_z = part(field_yz, cells + y, columns)
        if y + 1 < cells:
            e_x_up = part(field_x, y + 1, columns)
        else:
            e_x_up = jnp.where(inside_next, ahead_y[half : half + columns, :], 0.0)
        curl_y = forward_z(e_x) - (part(ahead_x, cells + y, columns) - e_z)
        curl_z = (part(ahead_x, y, columns) - e_y) - (e_x_up - e_x)
        mu = material[y : y + 1, :]
        m_y, m_z = mu * curl_y, mu * curl_z
        out_yz[y * columns : (y + 1) * columns, :] = m_y
        out_yz[(cells + y) * columns : (cells + y + 1) * columns, :] = m_z
        if y + 1 == cells:
            out_edge[half + columns :, :] = m_z
        left += [curl_y, curl_z]
        right += [m_y, m_z]
    out_edge[half : half + columns, :] = part(m_x, cells - 1, columns)
    out_edge[:half, :] = near[...] + packed(inner(wide(left), wide(right)))


def add_kernel(left, right, out):
    out[...] = left[...] + right[...]


def join_kernel(gram, edge, edge_other, out):
    half = gram.shape[0]
    out[:half, :] = gram[...]
    out[half:, :] = edge[:half, :] + edge_other[:half, :]


def sum_kernel(own, both, out, out_proj):
    half = out_proj.shape[0]
    total = own[...] + both[...]
    out[...] = total
    out_proj[...] = total[half:, :]


def factor(gram):
    columns = gram.shape[0]
    span, tile, width = 2 * columns, 8, 16
    count = columns // tile
    spread = lambda values: jnp.broadcast_to(values, (tile, span))
    sublane = lax.broadcasted_iota(jnp.int32, (tile, span), 0)
    lane = lax.broadcasted_iota(jnp.int32, (tile, span), 1)
    blocks = []
    for b in range(count):
        rows = gram[b * tile : (b + 1) * tile, :]
        rows = jnp.concatenate([rows, jnp.zeros_like(rows)], axis=1)
        blocks.append(jnp.where(lane == sublane + b * tile + columns, 1.0, rows))
    scales = [None] * count
    for start in range(0, columns, width):
        top = start // tile
        panel = [
            {b: spread(blocks[b][:, start + k : start + k + 1]) for b in range(top, count)}
            for k in range(width)
        ]
        for k in range(width):
            at, row = divmod(start + k, tile)
            pivot = spread(panel[k][at][row : row + 1, :])
            inverse = 1.0 / pivot
            ratio = {b: panel[k][b] * inverse for b in range(at, count)}
            ratio[at] = jnp.where(sublane > row, ratio[at], 0.0)
            root = lax.rsqrt(pivot)
            scales[at] = root if row == 0 else jnp.where(sublane == row, root, scales[at])
            for later in range(k + 1, width):
                to, below = divmod(start + later, tile)
                entry = spread(panel[k][to][below : below + 1, :])
                for b in range(at, count):
                    panel[later][b] = panel[later][b] - ratio[b] * entry
            pivot_row = spread(blocks[at][row : row + 1, :])
            for b in range(at, count):
                blocks[b] = blocks[b] - ratio[b] * pivot_row
    kept = []
    for b in range(count):
        row = sublane + b * tile
        kept.append(jnp.where((lane >= row) & (lane <= row + columns), blocks[b] * scales[b], 0.0))
    return jnp.concatenate(kept, axis=0)


def factor_kernel(total, sums, far, out):
    half = sums.shape[0] // 2
    out[...] = factor(unpacked(sums[:half, :] + far[:half, :]) / total)


def basis_kernel(
    columns, cells, field_x, field_yz, m_x, m_yz, behind_x, behind_y, material, factors,
    out_basis, out_image, out_upper, out_inverse, basis, image, upper, sems,
):
    half = columns // 2
    stride = 3 * cells
    inverse = factors[:, columns:]
    out_inverse[...] = inverse
    upper[...] = factors[:, :columns]
    third = pltpu.make_async_copy(upper, out_upper, sems.at[2])
    third.start()

    def write(chunks, places, held, target, sem):
        lanes = chunks[0].shape[1]
        whole = product(inverse, wide(chunks))
        for i, k in enumerate(places):
            held[pl.ds(k, columns, stride=stride), :] = whole[:, i * lanes : (i + 1) * lanes]
        copy = pltpu.make_async_copy(held, target, sem)
        copy.start()
        return copy

    fields = [part(field_x, y, columns) for y in range(cells)]
    fields += [part(field_yz, k, columns) for k in range(2 * cells)]
    first = write(fields, range(stride), basis, out_basis, sems.at[0])
    inside_last = lax.axis_index("col") > 0
    scaled_eps = material[cells:, :]
    images, places = [], []
    for y in range(cells):
        e = [part(field_x, y, columns), part(field_yz, y, columns), part(field_yz, cells + y, columns)]
        m = [part(m_x, y, columns), part(m_yz, y, columns), part(m_yz, cells + y, columns)]
        if y > 0:
            m_x_down, m_z_down = part(m_x, y - 1, columns), part(m_yz, cells + y - 1, columns)
        else:
            m_x_down = jnp.where(inside_last, behind_y[half : half + columns, :], 0.0)
            m_z_down = jnp.where(inside_last, behind_y[half + columns :, :], 0.0)
        mu_last = behind_x[2 * cells * columns + y : 2 * cells * columns + y + 1, :]
        m_y_last = part(behind_x, y, columns) - mu_last * e[2]
        m_z_last = part(behind_x, cells + y, columns) + mu_last * e[1]
        eps = scaled_eps[y : y + 1, :]
        images += [
            (m[2] - m_z_down) - backward_z(m[1]) - eps * e[0],
            backward_z(m[0]) - (m[2] - m_z_last) - eps * e[1],
            (m[1] - m_y_last) - (m[0] - m_x_down) - eps * e[2],
        ]
        places += [y, cells + y, 2 * cells + y]
    second = write(images, places, image, out_image, sems.at[1])
    first.wait()
    second.wait()
    third.wait()


def proj_kernel(total, inverse, proj, far_cross, far, near, out):
    half = proj.shape[0]
    raw = (proj[...] + near[...]) + (far[half:, :] + far_cross[...])
    left = lax.dot_general(
        inverse[...], unpacked(raw) / total, (((1,), (0,)), ((), ())),
        precision=lax.Precision.HIGHEST, preferred_element_type=F32,
    )
    out[...] = inner(left, inverse[...])


SMEM = pl.BlockSpec(memory_space=pltpu.SMEM)
VMEM = pl.BlockSpec(memory_space=pltpu.VMEM)
ANY = pl.BlockSpec(memory_space=pl.ANY)


def call(body, scalars, arrays, outs, flops=None, far=0, scratch=()):
    shapes = [jax.ShapeDtypeStruct(shape, F32) for shape in outs]
    cost = None
    if flops is not None:
        cost = pl.CostEstimate(flops=flops, bytes_accessed=0, transcendentals=0)
    return pl.pallas_call(
        body,
        out_shape=shapes,
        in_specs=[SMEM] * len(scalars) + [VMEM] * len(arrays),
        out_specs=[ANY] * far + [VMEM] * (len(shapes) - far),
        scratch_shapes=scratch,
        cost_estimate=cost,
        compiler_params=pltpu.CompilerParams(vmem_limit_bytes=32 * 1024 * 1024),
    )(*scalars, *arrays)


def swapped(x, axis, step):
    return lax.ppermute(x, axis, [(i, i ^ step) for i in range(lax.axis_size(axis))])


def local(krylov_basis, regions, mu_table, eps_table, shift_value):
    columns, parts, layers, cells, lanes = krylov_basis.shape
    rows, cols = lax.axis_size("row"), lax.axis_size("col")
    assert layers == 1 and parts == 3 and cols == 2 and rows >= 8 and rows & (rows - 1) == 0
    total = 3 * cells * lanes * rows * cols
    basis = krylov_basis.reshape(-1, lanes)
    labels = regions[0]
    half, outer = columns // 2, rows // 2
    small, large = (cells * columns, lanes), (2 * cells * columns, lanes)
    edge, pair = (half + 2 * columns, lanes), (half, 2 * columns)
    square = (columns, columns)

    (material,) = call(
        material_kernel, (mu_table, eps_table, shift_value), (labels,), ((2 * cells, lanes),),
        flops=0,
    )
    field_x, field_yz = call(
        functools.partial(pack_kernel, columns, cells), (), (basis,), (small, large), flops=0
    )
    ahead_x = shifted(field_yz, "row", -1)
    (gram_edge,) = call(
        functools.partial(gram_kernel, columns, cells), (), (field_x, field_yz), (edge,), flops=0
    )
    ahead_y = swapped(gram_edge, "col", 1)
    sent, gram = call(
        functools.partial(behind_kernel, columns, cells),
        (),
        (field_x, field_yz, gram_edge, ahead_y, material),
        ((2 * cells * columns + -(-cells // 8) * 8, lanes), pair),
        flops=0,
    )
    gram_other = swapped(gram, "row", 1)
    behind_x = shifted(sent, "row", 1)
    m_x, near = call(
        functools.partial(near_kernel, columns, cells),
        (),
        (field_x, field_yz, ahead_y, material),
        (small, pair),
        flops=0,
    )
    m_yz, proj_edge = call(
        functools.partial(curl_kernel, columns, cells),
        (),
        (field_x, field_yz, ahead_x, ahead_y, material, m_x, near),
        (large, edge),
        flops=10**10,
    )
    both = (2 * half, 2 * columns)
    (gram,) = call(add_kernel, (), (gram, gram_other), (pair,), flops=10**10)
    behind_y = swapped(proj_edge, "col", 1)
    (own,) = call(join_kernel, (), (gram, proj_edge, behind_y), (both,), flops=0)
    next_both = swapped(own, "row", 2)
    sums, proj = call(sum_kernel, (), (own, next_both), (both, pair), flops=0)
    step = 4
    while step < outer:
        sums = sums + swapped(sums, "row", step)
        proj = sums[half:]
        step *= 2
    far = swapped(sums, "row", outer)
    proj_near = swapped(proj, "row", 1)
    far_cross = swapped(proj, "row", outer + 1)
    (factors,) = call(
        functools.partial(factor_kernel, total), (), (sums, far), ((columns, 2 * columns),), flops=0
    )
    basis_out, image_out, upper, inverse = call(
        functools.partial(basis_kernel, columns, cells),
        (),
        (field_x, field_yz, m_x, m_yz, behind_x, behind_y, material, factors),
        (basis.shape, basis.shape, square, square),
        flops=0,
        far=3,
        scratch=[
            pltpu.VMEM(basis.shape, F32),
            pltpu.VMEM(basis.shape, F32),
            pltpu.VMEM(square, F32),
            pltpu.SemaphoreType.DMA((3,)),
        ],
    )
    (projected,) = call(
        functools.partial(proj_kernel, total),
        (),
        (inverse, proj, far_cross, far, proj_near),
        (square,),
        flops=0,
    )
    return (
        basis_out.reshape(krylov_basis.shape),
        upper,
        image_out.reshape(krylov_basis.shape),
        projected,
    )


def solution(mesh):
    placed = (P("shift", None, "row", "col", None), P("row", "col", None), P(), P(), P("shift"))
    return jax.shard_map(
        local,
        mesh=mesh,
        in_specs=placed,
        out_specs=(
            P("shift", None, "row", "col", None),
            P("shift", None),
            P("shift", None, "row", "col", None),
            P("shift", None),
        ),
        check_vma=False,
    )
```

```python
import functools

import jax
import jax.numpy as jnp
from jax import lax
from jax.experimental import pallas as pl
from jax.experimental.pallas import tpu as pltpu
from jax.sharding import PartitionSpec as P

F32 = jnp.float32
BF16 = jnp.bfloat16


def halo_ring(rows, back):
    ahead = [((r, 0), (r - 1, 0)) for r in range(1, rows)] + [((0, 0), (0, 1))]
    ahead += [((r, 1), (r + 1, 1)) for r in range(rows - 1)] + [((rows - 1, 1), (rows - 1, 0))]
    pairs = [(2 * r + c, 2 * to_r + to_c) for (r, c), (to_r, to_c) in ahead]
    return [(j, i) for i, j in pairs] if back else pairs


def wide(chunks):
    return jnp.concatenate(chunks, axis=1)


def three(values):
    high = values.astype(BF16)
    rest = values - high.astype(F32)
    middle = rest.astype(BF16)
    low = (rest - middle.astype(F32)).astype(BF16)
    return [high, middle, low]


def inner(left, right):
    return lax.dot_general(
        left, right, (((1,), (1,)), ((), ())), precision=lax.Precision.HIGHEST,
        preferred_element_type=F32,
    )


def product(left, right):
    rows = left.shape[0]
    high, middle, low = three(left)
    none = jnp.zeros_like(high)
    stacked = jnp.concatenate(
        [wide([high, high, high]), wide([middle, middle, none]), wide([low, none, none])], axis=0
    )
    blocks = lax.dot_general(
        stacked, jnp.concatenate(three(right), axis=0), (((1,), (0,)), ((), ())),
        preferred_element_type=F32,
    )
    return blocks[:rows, :] + (blocks[rows : 2 * rows, :] + blocks[2 * rows :, :])


def table_rows(labels, table_ref):
    result = jnp.zeros(labels.shape, F32)
    for region in range(table_ref.shape[0]):
        result = jnp.where(labels == region, table_ref[region], result)
    return result


def forward_z(values):
    lanes = values.shape[1]
    lane = lax.broadcasted_iota(jnp.int32, values.shape, 1)
    ahead = jnp.where(lane == lanes - 1, 0.0, pltpu.roll(values, lanes - 1, 1))
    return ahead - values


def backward_z(values):
    lane = lax.broadcasted_iota(jnp.int32, values.shape, 1)
    return values - jnp.where(lane == 0, 0.0, pltpu.roll(values, 1, 1))


def part(ref, index, columns):
    return ref[index * columns : (index + 1) * columns, :]


def packed(square):
    half = square.shape[0] // 2
    return jnp.concatenate([square[:half, :], square[half:, :]], axis=1)


def unpacked(pair):
    half = pair.shape[1] // 2
    return jnp.concatenate([pair[:, :half], pair[:, half:]], axis=0)


def first_core():
    return lax.axis_index("col") == 0


def pack_kernel(columns, cells, basis, out_x, out_yz, out_send):
    stride = 3 * cells
    chunks = [basis[pl.ds(k, columns, stride=stride), :] for k in range(stride)]
    down = first_core()
    for y in range(cells):
        e_x, e_y, e_z = chunks[y], chunks[cells + y], chunks[2 * cells + y]
        e_x_up = chunks[y + 1] if y + 1 < cells else jnp.zeros_like(e_x)
        at, other = y * columns, (cells + y) * columns
        out_x[at : at + columns, :] = e_x
        out_yz[at : at + columns, :] = e_y
        out_yz[other : other + columns, :] = e_z
        out_send[at : at + columns, :] = jnp.where(down, e_y, forward_z(e_x) + e_z)
        out_send[other : other + columns, :] = jnp.where(down, e_z, (e_x - e_x_up) - e_y)


def material_kernel(mu_table, eps_table, shift, regions, out):
    labels = regions[...]
    cells = labels.shape[0]
    out[:cells, :] = table_rows(labels, mu_table)
    out[cells:, :] = shift[0] * table_rows(labels, eps_table)


def gram_kernel(columns, cells, field_x, field_yz, out):
    half = columns // 2
    chunks = [part(field_x, k, columns) for k in range(cells)]
    chunks += [part(field_yz, k, columns) for k in range(2 * cells)]
    flat = wide(chunks)
    out[half : half + columns, :] = chunks[0]
    out[half + columns :, :] = chunks[2 * cells]
    out[:half, :] = packed(inner(flat, flat))


def open_kernel(columns, cells, field_x, field_yz, gram_edge, ahead_y, out_open, out_gram):
    half = columns // 2
    out_gram[...] = gram_edge[:half, :] + ahead_y[:half, :]
    inside = first_core()
    for y in range(cells):
        e_x = part(field_x, y, columns)
        if y + 1 < cells:
            e_x_up = part(field_x, y + 1, columns)
        else:
            e_x_up = jnp.where(inside, ahead_y[half : half + columns, :], 0.0)
        e_y, e_z = part(field_yz, y, columns), part(field_yz, cells + y, columns)
        at, other = y * columns, (cells + y) * columns
        out_open[at : at + columns, :] = forward_z(e_x) + e_z
        out_open[other : other + columns, :] = (e_x - e_x_up) - e_y


def near_kernel(columns, cells, field_x, field_yz, ahead_y, material, open_yz, out_x, out_proj):
    half = columns // 2
    inside = first_core()
    left, right = [], []
    for y in range(cells):
        e_x = part(field_x, y, columns)
        e_y = part(field_yz, y, columns)
        e_z = part(field_yz, cells + y, columns)
        if y + 1 < cells:
            e_z_up = part(field_yz, cells + y + 1, columns)
        else:
            e_z_up = jnp.where(inside, ahead_y[half + columns :, :], 0.0)
        curl_x = (e_z_up - e_z) - forward_z(e_y)
        mu = material[y : y + 1, :]
        eps = -material[cells + y : cells + y + 1, :]
        m_x = mu * curl_x
        open_y, open_z = part(open_yz, y, columns), part(open_yz, cells + y, columns)
        out_x[y * columns : (y + 1) * columns, :] = m_x
        left += [curl_x, e_x, e_y, e_z, open_y, open_z]
        right += [m_x, eps * e_x, eps * e_y, eps * e_z, mu * open_y, mu * open_z]
    out_proj[...] = packed(inner(wide(left), wide(right)))


def below_top():
    return lax.axis_index("row") + 1 < lax.axis_size("row")


def above_bottom():
    return lax.axis_index("row") > 0


def curl_kernel(
    columns, cells, field_yz, received, mu_received, open_yz, material, m_x, near, out_edge, out_send
):
    half = columns // 2
    ahead = first_core()
    behind = jnp.logical_and(jnp.logical_not(ahead), above_bottom())
    ahead_here = jnp.logical_and(ahead, below_top())
    left, right = [], []
    for y in range(cells):
        at, other = y * columns, (cells + y) * columns
        got_y, got_z = part(received, y, columns), part(received, cells + y, columns)
        own_y, own_z = part(field_yz, y, columns), part(field_yz, cells + y, columns)
        open_y, open_z = part(open_yz, y, columns), part(open_yz, cells + y, columns)
        mu_got = jnp.where(behind, mu_received[y : y + 1, :], 0.0)
        mu = jnp.where(ahead, material[y : y + 1, :], mu_got)
        out_send[at : at + columns, :] = jnp.where(ahead, open_y, own_y)
        out_send[other : other + columns, :] = jnp.where(ahead, open_z, own_z)
        open_y = jnp.where(ahead, open_y, jnp.where(behind, got_y, 0.0))
        open_z = jnp.where(ahead, open_z, jnp.where(behind, got_z, 0.0))
        e_y = jnp.where(ahead, jnp.where(ahead_here, got_y, 0.0), own_y)
        e_z = jnp.where(ahead, jnp.where(ahead_here, got_z, 0.0), own_z)
        left += [e_z, e_y]
        right += [mu * (0.5 * e_z - open_y), mu * (0.5 * e_y + open_z)]
        if y + 1 == cells:
            out_edge[half + columns :, :] = mu * (open_z + e_y)
    out_send[2 * cells * columns :, :] = material[...]
    out_edge[half : half + columns, :] = part(m_x, cells - 1, columns)
    crossing = inner(wide(left), wide(right))
    out_edge[:half, :] = near[...] + packed(crossing + crossing.T)


def add_kernel(left, right, out):
    out[...] = left[...] + right[...]


def join_kernel(gram, edge, edge_other, out):
    half = gram.shape[0]
    out[:half, :] = gram[...]
    out[half:, :] = edge[:half, :] + edge_other[:half, :]


def sum_kernel(own, both, out, out_proj):
    half = out_proj.shape[0]
    total = own[...] + both[...]
    out[...] = total
    out_proj[...] = total[half:, :]


def factor(gram):
    columns = gram.shape[0]
    span, tile, width = 2 * columns, 8, 16
    count = columns // tile
    spread = lambda values: jnp.broadcast_to(values, (tile, span))
    sublane = lax.broadcasted_iota(jnp.int32, (tile, span), 0)
    lane = lax.broadcasted_iota(jnp.int32, (tile, span), 1)
    blocks = []
    for b in range(count):
        rows = gram[b * tile : (b + 1) * tile, :]
        rows = jnp.concatenate([rows, jnp.zeros_like(rows)], axis=1)
        blocks.append(jnp.where(lane == sublane + b * tile + columns, 1.0, rows))
    scales = [None] * count
    for start in range(0, columns, width):
        top = start // tile
        panel = [
            {b: spread(blocks[b][:, start + k : start + k + 1]) for b in range(top, count)}
            for k in range(width)
        ]
        for k in range(width):
            at, row = divmod(start + k, tile)
            pivot = spread(panel[k][at][row : row + 1, :])
            inverse = 1.0 / pivot
            ratio = {b: panel[k][b] * inverse for b in range(at, count)}
            ratio[at] = jnp.where(sublane > row, ratio[at], 0.0)
            root = lax.rsqrt(pivot)
            scales[at] = root if row == 0 else jnp.where(sublane == row, root, scales[at])
            for later in range(k + 1, width):
                to, below = divmod(start + later, tile)
                entry = spread(panel[k][to][below : below + 1, :])
                for b in range(at, count):
                    panel[later][b] = panel[later][b] - ratio[b] * entry
            pivot_row = spread(blocks[at][row : row + 1, :])
            for b in range(at, count):
                blocks[b] = blocks[b] - ratio[b] * pivot_row
    kept = []
    for b in range(count):
        row = sublane + b * tile
        kept.append(jnp.where((lane >= row) & (lane <= row + columns), blocks[b] * scales[b], 0.0))
    return jnp.concatenate(kept, axis=0)


def factor_kernel(total, sums, far, out):
    half = sums.shape[0] // 2
    out[...] = factor(unpacked(sums[:half, :] + far[:half, :]) / total)


def basis_kernel(
    columns, cells, field_x, field_yz, m_x, open_yz, first_got, mu_received, second_got, behind_y,
    material, factors,
    out_basis, out_image, out_upper, out_inverse, basis, image, upper, sems,
):
    half = columns // 2
    stride = 3 * cells
    inverse = factors[:, columns:]
    out_inverse[...] = inverse
    upper[...] = factors[:, :columns]
    third = pltpu.make_async_copy(upper, out_upper, sems.at[2])
    third.start()

    def write(chunks, places, held, target, sem):
        lanes = chunks[0].shape[1]
        whole = product(inverse, wide(chunks))
        for i, k in enumerate(places):
            held[pl.ds(k, columns, stride=stride), :] = whole[:, i * lanes : (i + 1) * lanes]
        copy = pltpu.make_async_copy(held, target, sem)
        copy.start()
        return copy

    fields = [part(field_x, y, columns) for y in range(cells)]
    fields += [part(field_yz, k, columns) for k in range(2 * cells)]
    first_copy = write(fields, range(stride), basis, out_basis, sems.at[0])
    ahead = first_core()
    top, bottom = below_top(), above_bottom()
    scaled_eps = material[cells:, :]
    images, places = [], []
    m_z_down = None
    for y in range(cells):
        e = [part(field_x, y, columns), part(field_yz, y, columns), part(field_yz, cells + y, columns)]
        last = 2 * cells * columns + y
        mu = material[y : y + 1, :]
        first = part(first_got, y, columns), part(first_got, cells + y, columns)
        second = part(second_got, y, columns), part(second_got, cells + y, columns)
        e_y_next = jnp.where(top, jnp.where(ahead, first[0], second[0]), 0.0)
        e_z_next = jnp.where(top, jnp.where(ahead, first[1], second[1]), 0.0)
        m = [
            part(m_x, y, columns),
            mu * (part(open_yz, y, columns) - e_z_next),
            mu * (part(open_yz, cells + y, columns) + e_y_next),
        ]
        if y > 0:
            m_x_down = part(m_x, y - 1, columns)
        else:
            m_x_down = jnp.where(ahead, 0.0, behind_y[half : half + columns, :])
            m_z_down = jnp.where(ahead, 0.0, behind_y[half + columns :, :])
        mu_last = jnp.where(ahead, second_got[last : last + 1, :], mu_received[y : y + 1, :])
        m_y_last = jnp.where(bottom, mu_last * (jnp.where(ahead, second[0], first[0]) - e[2]), 0.0)
        m_z_last = jnp.where(bottom, mu_last * (jnp.where(ahead, second[1], first[1]) + e[1]), 0.0)
        eps = scaled_eps[y : y + 1, :]
        images += [
            (m[2] - m_z_down) - backward_z(m[1]) - eps * e[0],
            backward_z(m[0]) - (m[2] - m_z_last) - eps * e[1],
            (m[1] - m_y_last) - (m[0] - m_x_down) - eps * e[2],
        ]
        places += [y, cells + y, 2 * cells + y]
        m_z_down = m[2]
    second_copy = write(images, places, image, out_image, sems.at[1])
    first_copy.wait()
    second_copy.wait()
    third.wait()


def proj_kernel(total, inverse, proj, far_cross, far, near, out):
    half = proj.shape[0]
    raw = (proj[...] + near[...]) + (far[half:, :] + far_cross[...])
    left = lax.dot_general(
        inverse[...], unpacked(raw) / total, (((1,), (0,)), ((), ())),
        precision=lax.Precision.HIGHEST, preferred_element_type=F32,
    )
    out[...] = inner(left, inverse[...])


SMEM = pl.BlockSpec(memory_space=pltpu.SMEM)
VMEM = pl.BlockSpec(memory_space=pltpu.VMEM)
ANY = pl.BlockSpec(memory_space=pl.ANY)


def call(body, scalars, arrays, outs, flops=None, far=0, scratch=()):
    shapes = [jax.ShapeDtypeStruct(shape, F32) for shape in outs]
    cost = None
    if flops is not None:
        cost = pl.CostEstimate(flops=flops, bytes_accessed=0, transcendentals=0)
    return pl.pallas_call(
        body,
        out_shape=shapes,
        in_specs=[SMEM] * len(scalars) + [VMEM] * len(arrays),
        out_specs=[ANY] * far + [VMEM] * (len(shapes) - far),
        scratch_shapes=scratch,
        cost_estimate=cost,
        compiler_params=pltpu.CompilerParams(vmem_limit_bytes=32 * 1024 * 1024),
    )(*scalars, *arrays)


def swapped(x, axis, step):
    return lax.ppermute(x, axis, [(i, i ^ step) for i in range(lax.axis_size(axis))])


def local(krylov_basis, regions, mu_table, eps_table, shift_value):
    columns, parts, layers, cells, lanes = krylov_basis.shape
    rows, cols = lax.axis_size("row"), lax.axis_size("col")
    assert layers == 1 and parts == 3 and cols == 2 and rows >= 8 and rows & (rows - 1) == 0
    total = 3 * cells * lanes * rows * cols
    basis = krylov_basis.reshape(-1, lanes)
    labels = regions[0]
    half, outer = columns // 2, rows // 2
    small, large = (cells * columns, lanes), (2 * cells * columns, lanes)
    edge, pair = (half + 2 * columns, lanes), (half, 2 * columns)
    square = (columns, columns)

    (material,) = call(
        material_kernel, (mu_table, eps_table, shift_value), (labels,), ((2 * cells, lanes),),
        flops=0,
    )
    field_x, field_yz, send = call(
        functools.partial(pack_kernel, columns, cells), (), (basis,), (small, large, large), flops=0
    )
    first_got = lax.ppermute(send, ("row", "col"), halo_ring(rows, False))
    (gram_edge,) = call(
        functools.partial(gram_kernel, columns, cells), (), (field_x, field_yz), (edge,), flops=0
    )
    ahead_y = swapped(gram_edge, "col", 1)
    mu_received = lax.ppermute(material, ("row", "col"), halo_ring(rows, False))
    open_yz, gram = call(
        functools.partial(open_kernel, columns, cells),
        (),
        (field_x, field_yz, gram_edge, ahead_y),
        (large, pair),
        flops=0,
    )
    gram_other = swapped(gram, "row", 1)
    m_x, near = call(
        functools.partial(near_kernel, columns, cells),
        (),
        (field_x, field_yz, ahead_y, material, open_yz),
        (small, pair),
        flops=0,
    )
    proj_edge, send = call(
        functools.partial(curl_kernel, columns, cells),
        (),
        (field_yz, first_got, mu_received, open_yz, material, m_x, near),
        (edge, (2 * cells * (columns + 1), lanes)),
        flops=10**10,
    )
    second_got = lax.ppermute(send, ("row", "col"), halo_ring(rows, True))
    (gram,) = call(add_kernel, (), (gram, gram_other), (pair,), flops=10**10)
    behind_y = swapped(proj_edge, "col", 1)
    both = (2 * half, 2 * columns)
    (own,) = call(join_kernel, (), (gram, proj_edge, behind_y), (both,), flops=0)
    next_both = swapped(own, "row", 2)
    sums, proj = call(sum_kernel, (), (own, next_both), (both, pair), flops=0)
    step = 4
    while step < outer:
        sums = sums + swapped(sums, "row", step)
        proj = sums[half:]
        step *= 2
    far = swapped(sums, "row", outer)
    proj_near = swapped(proj, "row", 1)
    far_cross = swapped(proj, "row", outer + 1)
    (factors,) = call(
        functools.partial(factor_kernel, total), (), (sums, far), ((columns, 2 * columns),), flops=0
    )
    basis_out, image_out, upper, inverse = call(
        functools.partial(basis_kernel, columns, cells),
        (),
        (
            field_x, field_yz, m_x, open_yz, first_got, mu_received, second_got, behind_y, material,
            factors,
        ),
        (basis.shape, basis.shape, square, square),
        flops=0,
        far=3,
        scratch=[
            pltpu.VMEM(basis.shape, F32),
            pltpu.VMEM(basis.shape, F32),
            pltpu.VMEM(square, F32),
            pltpu.SemaphoreType.DMA((3,)),
        ],
    )
    (projected,) = call(
        functools.partial(proj_kernel, total),
        (),
        (inverse, proj, far_cross, far, proj_near),
        (square,),
        flops=0,
    )
    return (
        basis_out.reshape(krylov_basis.shape),
        upper,
        image_out.reshape(krylov_basis.shape),
        projected,
    )


def solution(mesh):
    placed = (P("shift", None, "row", "col", None), P("row", "col", None), P(), P(), P("shift"))
    return jax.shard_map(
        local,
        mesh=mesh,
        in_specs=placed,
        out_specs=(
            P("shift", None, "row", "col", None),
            P("shift", None),
            P("shift", None, "row", "col", None),
            P("shift", None),
        ),
        check_vma=False,
    )
```

```python
import functools

import jax
import jax.numpy as jnp
from jax import lax
from jax.experimental import pallas as pl
from jax.experimental.pallas import tpu as pltpu
from jax.sharding import PartitionSpec as P

F32 = jnp.float32
BF16 = jnp.bfloat16


def halo_ring(rows, back):
    ahead = [((r, 0), (r - 1, 0)) for r in range(1, rows)] + [((0, 0), (0, 1))]
    ahead += [((r, 1), (r + 1, 1)) for r in range(rows - 1)] + [((rows - 1, 1), (rows - 1, 0))]
    pairs = [(2 * r + c, 2 * to_r + to_c) for (r, c), (to_r, to_c) in ahead]
    return [(j, i) for i, j in pairs] if back else pairs


def wide(chunks):
    return jnp.concatenate(chunks, axis=1)


def three(values):
    high = values.astype(BF16)
    rest = values - high.astype(F32)
    middle = rest.astype(BF16)
    low = (rest - middle.astype(F32)).astype(BF16)
    return [high, middle, low]


def inner(left, right):
    return lax.dot_general(
        left, right, (((1,), (1,)), ((), ())), precision=lax.Precision.HIGHEST,
        preferred_element_type=F32,
    )


def product(left, right):
    rows = left.shape[0]
    high, middle, low = three(left)
    none = jnp.zeros_like(high)
    stacked = jnp.concatenate(
        [wide([high, high, high]), wide([middle, middle, none]), wide([low, none, none])], axis=0
    )
    blocks = lax.dot_general(
        stacked, jnp.concatenate(three(right), axis=0), (((1,), (0,)), ((), ())),
        preferred_element_type=F32,
    )
    return blocks[:rows, :] + (blocks[rows : 2 * rows, :] + blocks[2 * rows :, :])


def table_rows(labels, table_ref):
    result = jnp.zeros(labels.shape, F32)
    for region in range(table_ref.shape[0]):
        result = jnp.where(labels == region, table_ref[region], result)
    return result


def forward_z(values):
    lanes = values.shape[1]
    lane = lax.broadcasted_iota(jnp.int32, values.shape, 1)
    ahead = jnp.where(lane == lanes - 1, 0.0, pltpu.roll(values, lanes - 1, 1))
    return ahead - values


def backward_z(values):
    lane = lax.broadcasted_iota(jnp.int32, values.shape, 1)
    return values - jnp.where(lane == 0, 0.0, pltpu.roll(values, 1, 1))


def part(ref, index, columns):
    return ref[index * columns : (index + 1) * columns, :]


def packed(square):
    half = square.shape[0] // 2
    return jnp.concatenate([square[:half, :], square[half:, :]], axis=1)


def unpacked(pair):
    half = pair.shape[1] // 2
    return jnp.concatenate([pair[:, :half], pair[:, half:]], axis=0)


def first_core():
    return lax.axis_index("col") == 0


def pack_kernel(columns, cells, basis, out_x, out_yz, out_send):
    stride = 3 * cells
    chunks = [basis[pl.ds(k, columns, stride=stride), :] for k in range(stride)]
    down = first_core()
    for y in range(cells):
        e_x, e_y, e_z = chunks[y], chunks[cells + y], chunks[2 * cells + y]
        e_x_up = chunks[y + 1] if y + 1 < cells else jnp.zeros_like(e_x)
        at, other = y * columns, (cells + y) * columns
        out_x[at : at + columns, :] = e_x
        out_yz[at : at + columns, :] = e_y
        out_yz[other : other + columns, :] = e_z
        out_send[at : at + columns, :] = jnp.where(down, e_y, forward_z(e_x) + e_z)
        out_send[other : other + columns, :] = jnp.where(down, e_z, (e_x - e_x_up) - e_y)


def material_kernel(mu_table, eps_table, shift, regions, out):
    labels = regions[...]
    cells = labels.shape[0]
    out[:cells, :] = table_rows(labels, mu_table)
    out[cells:, :] = shift[0] * table_rows(labels, eps_table)


def gram_kernel(columns, cells, field_x, field_yz, out):
    half = columns // 2
    chunks = [part(field_x, k, columns) for k in range(cells)]
    chunks += [part(field_yz, k, columns) for k in range(2 * cells)]
    flat = wide(chunks)
    out[half : half + columns, :] = chunks[0]
    out[half + columns :, :] = chunks[2 * cells]
    out[:half, :] = packed(inner(flat, flat))


def open_kernel(columns, cells, field_x, field_yz, gram_edge, ahead_y, out_open, out_gram):
    half = columns // 2
    out_gram[...] = gram_edge[:half, :] + ahead_y[:half, :]
    inside = first_core()
    for y in range(cells):
        e_x = part(field_x, y, columns)
        if y + 1 < cells:
            e_x_up = part(field_x, y + 1, columns)
        else:
            e_x_up = jnp.where(inside, ahead_y[half : half + columns, :], 0.0)
        e_y, e_z = part(field_yz, y, columns), part(field_yz, cells + y, columns)
        at, other = y * columns, (cells + y) * columns
        out_open[at : at + columns, :] = forward_z(e_x) + e_z
        out_open[other : other + columns, :] = (e_x - e_x_up) - e_y


def near_kernel(
    columns, cells, field_x, field_yz, ahead_y, material, open_yz, out_x, out_proj, out_send
):
    half = columns // 2
    inside = first_core()
    left, right = [], []
    for y in range(cells):
        e_x = part(field_x, y, columns)
        e_y = part(field_yz, y, columns)
        e_z = part(field_yz, cells + y, columns)
        if y + 1 < cells:
            e_z_up = part(field_yz, cells + y + 1, columns)
        else:
            e_z_up = jnp.where(inside, ahead_y[half + columns :, :], 0.0)
        curl_x = (e_z_up - e_z) - forward_z(e_y)
        mu = material[y : y + 1, :]
        eps = -material[cells + y : cells + y + 1, :]
        m_x = mu * curl_x
        open_y, open_z = part(open_yz, y, columns), part(open_yz, cells + y, columns)
        at, other = y * columns, (cells + y) * columns
        out_x[at : at + columns, :] = m_x
        out_send[at : at + columns, :] = jnp.where(inside, open_y, e_y)
        out_send[other : other + columns, :] = jnp.where(inside, open_z, e_z)
        left += [curl_x, e_x, e_y, e_z, open_y, open_z]
        right += [m_x, eps * e_x, eps * e_y, eps * e_z, mu * open_y, mu * open_z]
    out_send[2 * cells * columns :, :] = material[...]
    out_proj[...] = packed(inner(wide(left), wide(right)))


def below_top():
    return lax.axis_index("row") + 1 < lax.axis_size("row")


def above_bottom():
    return lax.axis_index("row") > 0


def curl_kernel(
    columns, cells, field_yz, received, mu_received, open_yz, material, m_x, near, out_edge
):
    half = columns // 2
    ahead = first_core()
    behind = jnp.logical_and(jnp.logical_not(ahead), above_bottom())
    ahead_here = jnp.logical_and(ahead, below_top())
    left, right = [], []
    for y in range(cells):
        got_y, got_z = part(received, y, columns), part(received, cells + y, columns)
        own_y, own_z = part(field_yz, y, columns), part(field_yz, cells + y, columns)
        open_y, open_z = part(open_yz, y, columns), part(open_yz, cells + y, columns)
        mu_got = jnp.where(behind, mu_received[y : y + 1, :], 0.0)
        mu = jnp.where(ahead, material[y : y + 1, :], mu_got)
        open_y = jnp.where(ahead, open_y, jnp.where(behind, got_y, 0.0))
        open_z = jnp.where(ahead, open_z, jnp.where(behind, got_z, 0.0))
        e_y = jnp.where(ahead, jnp.where(ahead_here, got_y, 0.0), own_y)
        e_z = jnp.where(ahead, jnp.where(ahead_here, got_z, 0.0), own_z)
        left += [e_z, e_y]
        right += [mu * (0.5 * e_z - open_y), mu * (0.5 * e_y + open_z)]
        if y + 1 == cells:
            out_edge[half + columns :, :] = mu * (open_z + e_y)
    out_edge[half : half + columns, :] = part(m_x, cells - 1, columns)
    crossing = inner(wide(left), wide(right))
    out_edge[:half, :] = near[...] + packed(crossing + crossing.T)


def add_kernel(left, right, out):
    out[...] = left[...] + right[...]


def join_kernel(gram, edge, edge_other, out):
    half = gram.shape[0]
    out[:half, :] = gram[...]
    out[half:, :] = edge[:half, :] + edge_other[:half, :]


def sum_kernel(own, both, out, out_proj):
    half = out_proj.shape[0]
    total = own[...] + both[...]
    out[...] = total
    out_proj[...] = total[half:, :]


def factor(gram):
    columns = gram.shape[0]
    span, tile, width = 2 * columns, 8, 16
    count = columns // tile
    spread = lambda values: jnp.broadcast_to(values, (tile, span))
    sublane = lax.broadcasted_iota(jnp.int32, (tile, span), 0)
    lane = lax.broadcasted_iota(jnp.int32, (tile, span), 1)
    blocks = []
    for b in range(count):
        rows = gram[b * tile : (b + 1) * tile, :]
        rows = jnp.concatenate([rows, jnp.zeros_like(rows)], axis=1)
        blocks.append(jnp.where(lane == sublane + b * tile + columns, 1.0, rows))
    scales = [None] * count
    for start in range(0, columns, width):
        top = start // tile
        panel = [
            {b: spread(blocks[b][:, start + k : start + k + 1]) for b in range(top, count)}
            for k in range(width)
        ]
        for k in range(width):
            at, row = divmod(start + k, tile)
            pivot = spread(panel[k][at][row : row + 1, :])
            inverse = 1.0 / pivot
            ratio = {b: panel[k][b] * inverse for b in range(at, count)}
            ratio[at] = jnp.where(sublane > row, ratio[at], 0.0)
            root = lax.rsqrt(pivot)
            scales[at] = root if row == 0 else jnp.where(sublane == row, root, scales[at])
            for later in range(k + 1, width):
                to, below = divmod(start + later, tile)
                entry = spread(panel[k][to][below : below + 1, :])
                for b in range(at, count):
                    panel[later][b] = panel[later][b] - ratio[b] * entry
            pivot_row = spread(blocks[at][row : row + 1, :])
            for b in range(at, count):
                blocks[b] = blocks[b] - ratio[b] * pivot_row
    kept = []
    for b in range(count):
        row = sublane + b * tile
        kept.append(jnp.where((lane >= row) & (lane <= row + columns), blocks[b] * scales[b], 0.0))
    return jnp.concatenate(kept, axis=0)


def factor_kernel(total, sums, far, out):
    half = sums.shape[0] // 2
    out[...] = factor(unpacked(sums[:half, :] + far[:half, :]) / total)


def basis_kernel(
    columns, cells, field_x, field_yz, m_x, open_yz, first_got, mu_received, second_got, behind_y,
    material, factors,
    out_basis, out_image, out_upper, out_inverse, basis, image, upper, sems,
):
    half = columns // 2
    stride = 3 * cells
    inverse = factors[:, columns:]
    out_inverse[...] = inverse
    upper[...] = factors[:, :columns]
    third = pltpu.make_async_copy(upper, out_upper, sems.at[2])
    third.start()

    def write(chunks, places, held, target, sem):
        lanes = chunks[0].shape[1]
        whole = product(inverse, wide(chunks))
        for i, k in enumerate(places):
            held[pl.ds(k, columns, stride=stride), :] = whole[:, i * lanes : (i + 1) * lanes]
        copy = pltpu.make_async_copy(held, target, sem)
        copy.start()
        return copy

    fields = [part(field_x, y, columns) for y in range(cells)]
    fields += [part(field_yz, k, columns) for k in range(2 * cells)]
    first_copy = write(fields, range(stride), basis, out_basis, sems.at[0])
    ahead = first_core()
    top, bottom = below_top(), above_bottom()
    scaled_eps = material[cells:, :]
    images, places = [], []
    m_z_down = None
    for y in range(cells):
        e = [part(field_x, y, columns), part(field_yz, y, columns), part(field_yz, cells + y, columns)]
        last = 2 * cells * columns + y
        mu = material[y : y + 1, :]
        first = part(first_got, y, columns), part(first_got, cells + y, columns)
        second = part(second_got, y, columns), part(second_got, cells + y, columns)
        e_y_next = jnp.where(top, jnp.where(ahead, first[0], second[0]), 0.0)
        e_z_next = jnp.where(top, jnp.where(ahead, first[1], second[1]), 0.0)
        m = [
            part(m_x, y, columns),
            mu * (part(open_yz, y, columns) - e_z_next),
            mu * (part(open_yz, cells + y, columns) + e_y_next),
        ]
        if y > 0:
            m_x_down = part(m_x, y - 1, columns)
        else:
            m_x_down = jnp.where(ahead, 0.0, behind_y[half : half + columns, :])
            m_z_down = jnp.where(ahead, 0.0, behind_y[half + columns :, :])
        mu_last = jnp.where(ahead, second_got[last : last + 1, :], mu_received[y : y + 1, :])
        m_y_last = jnp.where(bottom, mu_last * (jnp.where(ahead, second[0], first[0]) - e[2]), 0.0)
        m_z_last = jnp.where(bottom, mu_last * (jnp.where(ahead, second[1], first[1]) + e[1]), 0.0)
        eps = scaled_eps[y : y + 1, :]
        images += [
            (m[2] - m_z_down) - backward_z(m[1]) - eps * e[0],
            backward_z(m[0]) - (m[2] - m_z_last) - eps * e[1],
            (m[1] - m_y_last) - (m[0] - m_x_down) - eps * e[2],
        ]
        places += [y, cells + y, 2 * cells + y]
        m_z_down = m[2]
    second_copy = write(images, places, image, out_image, sems.at[1])
    first_copy.wait()
    second_copy.wait()
    third.wait()


def proj_kernel(total, inverse, proj, far_cross, far, near, out):
    half = proj.shape[0]
    raw = (proj[...] + near[...]) + (far[half:, :] + far_cross[...])
    left = lax.dot_general(
        inverse[...], unpacked(raw) / total, (((1,), (0,)), ((), ())),
        precision=lax.Precision.HIGHEST, preferred_element_type=F32,
    )
    out[...] = inner(left, inverse[...])


SMEM = pl.BlockSpec(memory_space=pltpu.SMEM)
VMEM = pl.BlockSpec(memory_space=pltpu.VMEM)
ANY = pl.BlockSpec(memory_space=pl.ANY)


def call(body, scalars, arrays, outs, flops=None, far=0, scratch=()):
    shapes = [jax.ShapeDtypeStruct(shape, F32) for shape in outs]
    cost = None
    if flops is not None:
        cost = pl.CostEstimate(flops=flops, bytes_accessed=0, transcendentals=0)
    return pl.pallas_call(
        body,
        out_shape=shapes,
        in_specs=[SMEM] * len(scalars) + [VMEM] * len(arrays),
        out_specs=[ANY] * far + [VMEM] * (len(shapes) - far),
        scratch_shapes=scratch,
        cost_estimate=cost,
        compiler_params=pltpu.CompilerParams(vmem_limit_bytes=32 * 1024 * 1024),
    )(*scalars, *arrays)


def swapped(x, axis, step):
    return lax.ppermute(x, axis, [(i, i ^ step) for i in range(lax.axis_size(axis))])


def local(krylov_basis, regions, mu_table, eps_table, shift_value):
    columns, parts, layers, cells, lanes = krylov_basis.shape
    rows, cols = lax.axis_size("row"), lax.axis_size("col")
    assert layers == 1 and parts == 3 and cols == 2 and rows >= 8 and rows & (rows - 1) == 0
    total = 3 * cells * lanes * rows * cols
    basis = krylov_basis.reshape(-1, lanes)
    labels = regions[0]
    half, outer = columns // 2, rows // 2
    small, large = (cells * columns, lanes), (2 * cells * columns, lanes)
    edge, pair = (half + 2 * columns, lanes), (half, 2 * columns)
    square = (columns, columns)

    (material,) = call(
        material_kernel, (mu_table, eps_table, shift_value), (labels,), ((2 * cells, lanes),),
        flops=0,
    )
    field_x, field_yz, send = call(
        functools.partial(pack_kernel, columns, cells), (), (basis,), (small, large, large), flops=0
    )
    first_got = lax.ppermute(send, ("row", "col"), halo_ring(rows, False))
    (gram_edge,) = call(
        functools.partial(gram_kernel, columns, cells), (), (field_x, field_yz), (edge,), flops=0
    )
    ahead_y = swapped(gram_edge, "col", 1)
    mu_received = lax.ppermute(material, ("row", "col"), halo_ring(rows, False))
    open_yz, gram = call(
        functools.partial(open_kernel, columns, cells),
        (),
        (field_x, field_yz, gram_edge, ahead_y),
        (large, pair),
        flops=0,
    )
    gram_other = swapped(gram, "row", 1)
    m_x, near, send = call(
        functools.partial(near_kernel, columns, cells),
        (),
        (field_x, field_yz, ahead_y, material, open_yz),
        (small, pair, (2 * cells * (columns + 1), lanes)),
        flops=0,
    )
    second_got = lax.ppermute(send, ("row", "col"), halo_ring(rows, True))
    (proj_edge,) = call(
        functools.partial(curl_kernel, columns, cells),
        (),
        (field_yz, first_got, mu_received, open_yz, material, m_x, near),
        (edge,),
        flops=10**10,
    )
    (gram,) = call(add_kernel, (), (gram, gram_other), (pair,), flops=10**10)
    behind_y = swapped(proj_edge, "col", 1)
    both = (2 * half, 2 * columns)
    (own,) = call(join_kernel, (), (gram, proj_edge, behind_y), (both,), flops=0)
    next_both = swapped(own, "row", 2)
    sums, proj = call(sum_kernel, (), (own, next_both), (both, pair), flops=0)
    step = 4
    while step < outer:
        sums = sums + swapped(sums, "row", step)
        proj = sums[half:]
        step *= 2
    far = swapped(sums, "row", outer)
    proj_near = swapped(proj, "row", 1)
    far_cross = swapped(proj, "row", outer + 1)
    (factors,) = call(
        functools.partial(factor_kernel, total), (), (sums, far), ((columns, 2 * columns),), flops=0
    )
    basis_out, image_out, upper, inverse = call(
        functools.partial(basis_kernel, columns, cells),
        (),
        (
            field_x, field_yz, m_x, open_yz, first_got, mu_received, second_got, behind_y, material,
            factors,
        ),
        (basis.shape, basis.shape, square, square),
        flops=0,
        far=3,
        scratch=[
            pltpu.VMEM(basis.shape, F32),
            pltpu.VMEM(basis.shape, F32),
            pltpu.VMEM(square, F32),
            pltpu.SemaphoreType.DMA((3,)),
        ],
    )
    (projected,) = call(
        functools.partial(proj_kernel, total),
        (),
        (inverse, proj, far_cross, far, proj_near),
        (square,),
        flops=0,
    )
    return (
        basis_out.reshape(krylov_basis.shape),
        upper,
        image_out.reshape(krylov_basis.shape),
        projected,
    )


def solution(mesh):
    placed = (P("shift", None, "row", "col", None), P("row", "col", None), P(), P(), P("shift"))
    return jax.shard_map(
        local,
        mesh=mesh,
        in_specs=placed,
        out_specs=(
            P("shift", None, "row", "col", None),
            P("shift", None),
            P("shift", None, "row", "col", None),
            P("shift", None),
        ),
        check_vma=False,
    )
```

```python
import functools

import jax
import jax.numpy as jnp
from jax import lax
from jax.experimental import pallas as pl
from jax.experimental.pallas import tpu as pltpu
from jax.sharding import PartitionSpec as P

F32 = jnp.float32
BF16 = jnp.bfloat16


def halo_ring(rows, back):
    ahead = [((r, 0), (r - 1, 0)) for r in range(1, rows)] + [((0, 0), (0, 1))]
    ahead += [((r, 1), (r + 1, 1)) for r in range(rows - 1)] + [((rows - 1, 1), (rows - 1, 0))]
    pairs = [(2 * r + c, 2 * to_r + to_c) for (r, c), (to_r, to_c) in ahead]
    return [(j, i) for i, j in pairs] if back else pairs


def wide(chunks):
    return jnp.concatenate(chunks, axis=1)


def three(values):
    high = values.astype(BF16)
    rest = values - high.astype(F32)
    middle = rest.astype(BF16)
    low = (rest - middle.astype(F32)).astype(BF16)
    return [high, middle, low]


def inner(left, right):
    return lax.dot_general(
        left, right, (((1,), (1,)), ((), ())), precision=lax.Precision.HIGHEST,
        preferred_element_type=F32,
    )


def product(left, right):
    rows = left.shape[0]
    high, middle, low = three(left)
    none = jnp.zeros_like(high)
    stacked = jnp.concatenate(
        [wide([high, high, high]), wide([middle, middle, none]), wide([low, none, none])], axis=0
    )
    blocks = lax.dot_general(
        stacked, jnp.concatenate(three(right), axis=0), (((1,), (0,)), ((), ())),
        preferred_element_type=F32,
    )
    return blocks[:rows, :] + (blocks[rows : 2 * rows, :] + blocks[2 * rows :, :])


def table_rows(labels, table_ref):
    result = jnp.zeros(labels.shape, F32)
    for region in range(table_ref.shape[0]):
        result = jnp.where(labels == region, table_ref[region], result)
    return result


def forward_z(values):
    lanes = values.shape[1]
    lane = lax.broadcasted_iota(jnp.int32, values.shape, 1)
    ahead = jnp.where(lane == lanes - 1, 0.0, pltpu.roll(values, lanes - 1, 1))
    return ahead - values


def backward_z(values):
    lane = lax.broadcasted_iota(jnp.int32, values.shape, 1)
    return values - jnp.where(lane == 0, 0.0, pltpu.roll(values, 1, 1))


def part(ref, index, columns):
    return ref[index * columns : (index + 1) * columns, :]


def packed(square):
    half = square.shape[0] // 2
    return jnp.concatenate([square[:half, :], square[half:, :]], axis=1)


def unpacked(pair):
    half = pair.shape[1] // 2
    return jnp.concatenate([pair[:, :half], pair[:, half:]], axis=0)


def first_core():
    return lax.axis_index("col") == 0


def pack_kernel(columns, cells, basis, out_x, out_yz, out_send):
    stride = 3 * cells
    chunks = [basis[pl.ds(k, columns, stride=stride), :] for k in range(stride)]
    down = first_core()
    for y in range(cells):
        e_x, e_y, e_z = chunks[y], chunks[cells + y], chunks[2 * cells + y]
        e_x_up = chunks[y + 1] if y + 1 < cells else jnp.zeros_like(e_x)
        at, other = y * columns, (cells + y) * columns
        out_x[at : at + columns, :] = e_x
        out_yz[at : at + columns, :] = e_y
        out_yz[other : other + columns, :] = e_z
        out_send[at : at + columns, :] = jnp.where(down, e_y, forward_z(e_x) + e_z)
        out_send[other : other + columns, :] = jnp.where(down, e_z, (e_x - e_x_up) - e_y)


def material_kernel(mu_table, eps_table, shift, regions, out):
    labels = regions[...]
    cells = labels.shape[0]
    out[:cells, :] = table_rows(labels, mu_table)
    out[cells:, :] = shift[0] * table_rows(labels, eps_table)


def gram_kernel(columns, cells, field_x, field_yz, out):
    half = columns // 2
    chunks = [part(field_x, k, columns) for k in range(cells)]
    chunks += [part(field_yz, k, columns) for k in range(2 * cells)]
    flat = wide(chunks)
    out[half : half + columns, :] = chunks[0]
    out[half + columns :, :] = chunks[2 * cells]
    out[:half, :] = packed(inner(flat, flat))


def open_kernel(columns, cells, field_x, field_yz, gram_edge, ahead_y, out_open, out_gram):
    half = columns // 2
    out_gram[...] = gram_edge[:half, :] + ahead_y[:half, :]
    inside = first_core()
    for y in range(cells):
        e_x = part(field_x, y, columns)
        if y + 1 < cells:
            e_x_up = part(field_x, y + 1, columns)
        else:
            e_x_up = jnp.where(inside, ahead_y[half : half + columns, :], 0.0)
        e_y, e_z = part(field_yz, y, columns), part(field_yz, cells + y, columns)
        at, other = y * columns, (cells + y) * columns
        out_open[at : at + columns, :] = forward_z(e_x) + e_z
        out_open[other : other + columns, :] = (e_x - e_x_up) - e_y


def near_kernel(
    columns, cells, field_x, field_yz, ahead_y, material, open_yz, out_x, out_proj, out_send
):
    half = columns // 2
    inside = first_core()
    left, right = [], []
    for y in range(cells):
        e_x = part(field_x, y, columns)
        e_y = part(field_yz, y, columns)
        e_z = part(field_yz, cells + y, columns)
        if y + 1 < cells:
            e_z_up = part(field_yz, cells + y + 1, columns)
        else:
            e_z_up = jnp.where(inside, ahead_y[half + columns :, :], 0.0)
        curl_x = (e_z_up - e_z) - forward_z(e_y)
        mu = material[y : y + 1, :]
        eps = -material[cells + y : cells + y + 1, :]
        m_x = mu * curl_x
        open_y, open_z = part(open_yz, y, columns), part(open_yz, cells + y, columns)
        at, other = y * columns, (cells + y) * columns
        out_x[at : at + columns, :] = m_x
        out_send[at : at + columns, :] = jnp.where(inside, open_y, e_y)
        out_send[other : other + columns, :] = jnp.where(inside, open_z, e_z)
        left += [curl_x, e_x, e_y, e_z, open_y, open_z]
        right += [m_x, eps * e_x, eps * e_y, eps * e_z, mu * open_y, mu * open_z]
    out_send[2 * cells * columns :, :] = material[...]
    out_proj[...] = packed(inner(wide(left), wide(right)))


def below_top():
    return lax.axis_index("row") + 1 < lax.axis_size("row")


def above_bottom():
    return lax.axis_index("row") > 0


def curl_kernel(
    columns, cells, field_yz, received, mu_received, open_yz, material, m_x, near, out_edge
):
    half = columns // 2
    ahead = first_core()
    behind = jnp.logical_and(jnp.logical_not(ahead), above_bottom())
    ahead_here = jnp.logical_and(ahead, below_top())
    left, right = [], []
    for y in range(cells):
        got_y, got_z = part(received, y, columns), part(received, cells + y, columns)
        own_y, own_z = part(field_yz, y, columns), part(field_yz, cells + y, columns)
        open_y, open_z = part(open_yz, y, columns), part(open_yz, cells + y, columns)
        mu_got = jnp.where(behind, mu_received[y : y + 1, :], 0.0)
        mu = jnp.where(ahead, material[y : y + 1, :], mu_got)
        open_y = jnp.where(ahead, open_y, jnp.where(behind, got_y, 0.0))
        open_z = jnp.where(ahead, open_z, jnp.where(behind, got_z, 0.0))
        e_y = jnp.where(ahead, jnp.where(ahead_here, got_y, 0.0), own_y)
        e_z = jnp.where(ahead, jnp.where(ahead_here, got_z, 0.0), own_z)
        left += [e_z, e_y]
        right += [mu * (0.5 * e_z - open_y), mu * (0.5 * e_y + open_z)]
        if y + 1 == cells:
            out_edge[half + columns :, :] = mu * (open_z + e_y)
    out_edge[half : half + columns, :] = part(m_x, cells - 1, columns)
    crossing = inner(wide(left), wide(right))
    out_edge[:half, :] = near[...] + packed(crossing + crossing.T)


def add_kernel(left, right, out):
    out[...] = left[...] + right[...]


def join_kernel(gram, edge, edge_other, out):
    half = gram.shape[0]
    out[:half, :] = gram[...]
    out[half:, :] = edge[:half, :] + edge_other[:half, :]


def sum_kernel(own, both, out, out_proj):
    half = out_proj.shape[0]
    total = own[...] + both[...]
    out[...] = total
    out_proj[...] = total[half:, :]


def factor(gram):
    columns = gram.shape[0]
    span, tile, width = 2 * columns, 8, 16
    count = columns // tile
    spread = lambda values: jnp.broadcast_to(values, (tile, span))
    sublane = lax.broadcasted_iota(jnp.int32, (tile, span), 0)
    lane = lax.broadcasted_iota(jnp.int32, (tile, span), 1)
    blocks = []
    for b in range(count):
        rows = gram[b * tile : (b + 1) * tile, :]
        rows = jnp.concatenate([rows, jnp.zeros_like(rows)], axis=1)
        blocks.append(jnp.where(lane == sublane + b * tile + columns, 1.0, rows))
    scales = [None] * count
    for start in range(0, columns, width):
        top = start // tile
        panel = [
            {b: spread(blocks[b][:, start + k : start + k + 1]) for b in range(top, count)}
            for k in range(width)
        ]
        for k in range(width):
            at, row = divmod(start + k, tile)
            pivot = spread(panel[k][at][row : row + 1, :])
            inverse = 1.0 / pivot
            ratio = {b: panel[k][b] * inverse for b in range(at, count)}
            ratio[at] = jnp.where(sublane > row, ratio[at], 0.0)
            root = lax.rsqrt(pivot)
            scales[at] = root if row == 0 else jnp.where(sublane == row, root, scales[at])
            for later in range(k + 1, width):
                to, below = divmod(start + later, tile)
                entry = spread(panel[k][to][below : below + 1, :])
                for b in range(at, count):
                    panel[later][b] = panel[later][b] - ratio[b] * entry
            pivot_row = spread(blocks[at][row : row + 1, :])
            for b in range(at, count):
                blocks[b] = blocks[b] - ratio[b] * pivot_row
    kept = []
    for b in range(count):
        row = sublane + b * tile
        kept.append(jnp.where((lane >= row) & (lane <= row + columns), blocks[b] * scales[b], 0.0))
    return jnp.concatenate(kept, axis=0)


def factor_kernel(total, sums, far, out):
    half = sums.shape[0] // 2
    out[...] = factor(unpacked(sums[:half, :] + far[:half, :]) / total)


def basis_kernel(
    columns, cells, field_x, field_yz, m_x, open_yz, first_got, mu_received, second_got, behind_y,
    material, factors,
    out_basis, out_image, out_upper, out_inverse, basis, image, upper, sems,
):
    half = columns // 2
    stride = 3 * cells
    inverse = factors[:, columns:]
    out_inverse[...] = inverse
    upper[...] = factors[:, :columns]
    third = pltpu.make_async_copy(upper, out_upper, sems.at[2])
    third.start()

    def write(chunks, places, held, target, sem):
        lanes = chunks[0].shape[1]
        whole = product(inverse, wide(chunks))
        for i, k in enumerate(places):
            held[pl.ds(k, columns, stride=stride), :] = whole[:, i * lanes : (i + 1) * lanes]
        copy = pltpu.make_async_copy(held, target, sem)
        copy.start()
        return copy

    fields = [part(field_x, y, columns) for y in range(cells)]
    fields += [part(field_yz, k, columns) for k in range(2 * cells)]
    first_copy = write(fields, range(stride), basis, out_basis, sems.at[0])
    ahead = first_core()
    top, bottom = below_top(), above_bottom()
    scaled_eps = material[cells:, :]
    images, places = [], []
    m_z_down = None
    for y in range(cells):
        e = [part(field_x, y, columns), part(field_yz, y, columns), part(field_yz, cells + y, columns)]
        last = 2 * cells * columns + y
        mu = material[y : y + 1, :]
        first = part(first_got, y, columns), part(first_got, cells + y, columns)
        second = part(second_got, y, columns), part(second_got, cells + y, columns)
        e_y_next = jnp.where(top, jnp.where(ahead, first[0], second[0]), 0.0)
        e_z_next = jnp.where(top, jnp.where(ahead, first[1], second[1]), 0.0)
        m = [
            part(m_x, y, columns),
            mu * (part(open_yz, y, columns) - e_z_next),
            mu * (part(open_yz, cells + y, columns) + e_y_next),
        ]
        if y > 0:
            m_x_down = part(m_x, y - 1, columns)
        else:
            m_x_down = jnp.where(ahead, 0.0, behind_y[half : half + columns, :])
            m_z_down = jnp.where(ahead, 0.0, behind_y[half + columns :, :])
        mu_last = jnp.where(ahead, second_got[last : last + 1, :], mu_received[y : y + 1, :])
        m_y_last = jnp.where(bottom, mu_last * (jnp.where(ahead, second[0], first[0]) - e[2]), 0.0)
        m_z_last = jnp.where(bottom, mu_last * (jnp.where(ahead, second[1], first[1]) + e[1]), 0.0)
        eps = scaled_eps[y : y + 1, :]
        images += [
            (m[2] - m_z_down) - backward_z(m[1]) - eps * e[0],
            backward_z(m[0]) - (m[2] - m_z_last) - eps * e[1],
            (m[1] - m_y_last) - (m[0] - m_x_down) - eps * e[2],
        ]
        places += [y, cells + y, 2 * cells + y]
        m_z_down = m[2]
    second_copy = write(images, places, image, out_image, sems.at[1])
    first_copy.wait()
    second_copy.wait()
    third.wait()


def proj_kernel(total, inverse, proj, far_cross, far, near, out):
    half = proj.shape[0]
    raw = (proj[...] + near[...]) + (far[half:, :] + far_cross[...])
    left = lax.dot_general(
        inverse[...], unpacked(raw) / total, (((1,), (0,)), ((), ())),
        precision=lax.Precision.HIGHEST, preferred_element_type=F32,
    )
    out[...] = inner(left, inverse[...])


SMEM = pl.BlockSpec(memory_space=pltpu.SMEM)
VMEM = pl.BlockSpec(memory_space=pltpu.VMEM)
ANY = pl.BlockSpec(memory_space=pl.ANY)


def call(body, scalars, arrays, outs, flops=None, far=0, scratch=()):
    shapes = [jax.ShapeDtypeStruct(shape, F32) for shape in outs]
    cost = None
    if flops is not None:
        cost = pl.CostEstimate(flops=flops, bytes_accessed=0, transcendentals=0)
    return pl.pallas_call(
        body,
        out_shape=shapes,
        in_specs=[SMEM] * len(scalars) + [VMEM] * len(arrays),
        out_specs=[ANY] * far + [VMEM] * (len(shapes) - far),
        scratch_shapes=scratch,
        cost_estimate=cost,
        compiler_params=pltpu.CompilerParams(vmem_limit_bytes=32 * 1024 * 1024),
    )(*scalars, *arrays)


def swapped(x, axis, step):
    return lax.ppermute(x, axis, [(i, i ^ step) for i in range(lax.axis_size(axis))])


def local(krylov_basis, regions, mu_table, eps_table, shift_value):
    columns, parts, layers, cells, lanes = krylov_basis.shape
    rows, cols = lax.axis_size("row"), lax.axis_size("col")
    assert layers == 1 and parts == 3 and cols == 2 and rows >= 8 and rows & (rows - 1) == 0
    total = 3 * cells * lanes * rows * cols
    basis = krylov_basis.reshape(-1, lanes)
    labels = regions[0]
    half, outer = columns // 2, rows // 2
    small, large = (cells * columns, lanes), (2 * cells * columns, lanes)
    edge, pair = (half + 2 * columns, lanes), (half, 2 * columns)
    square = (columns, columns)

    (material,) = call(
        material_kernel, (mu_table, eps_table, shift_value), (labels,), ((2 * cells, lanes),),
        flops=0,
    )
    field_x, field_yz, send = call(
        functools.partial(pack_kernel, columns, cells), (), (basis,), (small, large, large), flops=0
    )
    first_got = lax.ppermute(send, ("row", "col"), halo_ring(rows, False))
    (gram_edge,) = call(
        functools.partial(gram_kernel, columns, cells), (), (field_x, field_yz), (edge,), flops=0
    )
    ahead_y = swapped(gram_edge, "col", 1)
    mu_received = lax.ppermute(material, ("row", "col"), halo_ring(rows, False))
    open_yz, gram = call(
        functools.partial(open_kernel, columns, cells),
        (),
        (field_x, field_yz, gram_edge, ahead_y),
        (large, pair),
        flops=0,
    )
    gram_other = swapped(gram, "row", 1)
    m_x, near, send = call(
        functools.partial(near_kernel, columns, cells),
        (),
        (field_x, field_yz, ahead_y, material, open_yz),
        (small, pair, (2 * cells * (columns + 1), lanes)),
        flops=0,
    )
    second_got = lax.ppermute(send, ("row", "col"), halo_ring(rows, True))
    (proj_edge,) = call(
        functools.partial(curl_kernel, columns, cells),
        (),
        (field_yz, first_got, mu_received, open_yz, material, m_x, near),
        (edge,),
        flops=10**10,
    )
    (gram,) = call(add_kernel, (), (gram, gram_other), (pair,), flops=10**10)
    behind_y = swapped(proj_edge, "col", 1)
    both = (2 * half, 2 * columns)
    (own,) = call(join_kernel, (), (gram, proj_edge, behind_y), (both,), flops=0)
    next_both = swapped(own, "row", outer)
    sums, proj = call(sum_kernel, (), (own, next_both), (both, pair), flops=0)
    step = 4
    while step < outer:
        sums = sums + swapped(sums, "row", step)
        proj = sums[half:]
        step *= 2
    far = swapped(sums, "row", 2)
    proj_near = swapped(proj, "row", 1)
    far_cross = swapped(proj, "row", 3)
    (factors,) = call(
        functools.partial(factor_kernel, total), (), (sums, far), ((columns, 2 * columns),), flops=0
    )
    basis_out, image_out, upper, inverse = call(
        functools.partial(basis_kernel, columns, cells),
        (),
        (
            field_x, field_yz, m_x, open_yz, first_got, mu_received, second_got, behind_y, material,
            factors,
        ),
        (basis.shape, basis.shape, square, square),
        flops=0,
        far=3,
        scratch=[
            pltpu.VMEM(basis.shape, F32),
            pltpu.VMEM(basis.shape, F32),
            pltpu.VMEM(square, F32),
            pltpu.SemaphoreType.DMA((3,)),
        ],
    )
    (projected,) = call(
        functools.partial(proj_kernel, total),
        (),
        (inverse, proj, far_cross, far, proj_near),
        (square,),
        flops=0,
    )
    return (
        basis_out.reshape(krylov_basis.shape),
        upper,
        image_out.reshape(krylov_basis.shape),
        projected,
    )


def solution(mesh):
    placed = (P("shift", None, "row", "col", None), P("row", "col", None), P(), P(), P("shift"))
    return jax.shard_map(
        local,
        mesh=mesh,
        in_specs=placed,
        out_specs=(
            P("shift", None, "row", "col", None),
            P("shift", None),
            P("shift", None, "row", "col", None),
            P("shift", None),
        ),
        check_vma=False,
    )
```

```python
import functools

import jax
import jax.numpy as jnp
from jax import lax
from jax.experimental import pallas as pl
from jax.experimental.pallas import tpu as pltpu
from jax.sharding import PartitionSpec as P

F32 = jnp.float32
BF16 = jnp.bfloat16


def halo_ring(rows, back):
    ahead = [((r, 0), (r - 1, 0)) for r in range(1, rows)] + [((0, 0), (0, 1))]
    ahead += [((r, 1), (r + 1, 1)) for r in range(rows - 1)] + [((rows - 1, 1), (rows - 1, 0))]
    pairs = [(2 * r + c, 2 * to_r + to_c) for (r, c), (to_r, to_c) in ahead]
    return [(j, i) for i, j in pairs] if back else pairs


def wide(chunks):
    return jnp.concatenate(chunks, axis=1)


def three(values):
    high = values.astype(BF16)
    rest = values - high.astype(F32)
    middle = rest.astype(BF16)
    low = (rest - middle.astype(F32)).astype(BF16)
    return [high, middle, low]


def inner(left, right):
    return lax.dot_general(
        left, right, (((1,), (1,)), ((), ())), precision=lax.Precision.HIGHEST,
        preferred_element_type=F32,
    )


def product(left, right_thirds):
    rows = left.shape[0]
    high, middle, low = three(left)
    none = jnp.zeros_like(high)
    stacked = jnp.concatenate(
        [wide([high, high, high]), wide([middle, middle, none]), wide([low, none, none])], axis=0
    )
    blocks = lax.dot_general(
        stacked, right_thirds, (((1,), (0,)), ((), ())), preferred_element_type=F32
    )
    return blocks[:rows, :] + (blocks[rows : 2 * rows, :] + blocks[2 * rows :, :])


def table_rows(labels, table_ref):
    result = jnp.zeros(labels.shape, F32)
    for region in range(table_ref.shape[0]):
        result = jnp.where(labels == region, table_ref[region], result)
    return result


def forward_z(values):
    lanes = values.shape[1]
    lane = lax.broadcasted_iota(jnp.int32, values.shape, 1)
    ahead = jnp.where(lane == lanes - 1, 0.0, pltpu.roll(values, lanes - 1, 1))
    return ahead - values


def backward_z(values):
    lane = lax.broadcasted_iota(jnp.int32, values.shape, 1)
    return values - jnp.where(lane == 0, 0.0, pltpu.roll(values, 1, 1))


def part(ref, index, columns):
    return ref[index * columns : (index + 1) * columns, :]


def packed(square):
    half = square.shape[0] // 2
    return jnp.concatenate([square[:half, :], square[half:, :]], axis=1)


def unpacked(pair):
    half = pair.shape[1] // 2
    return jnp.concatenate([pair[:, :half], pair[:, half:]], axis=0)


def first_core():
    return lax.axis_index("col") == 0


def pack_kernel(columns, cells, basis, out_x, out_yz, out_send):
    stride = 3 * cells
    chunks = [basis[pl.ds(k, columns, stride=stride), :] for k in range(stride)]
    down = first_core()
    for y in range(cells):
        e_x, e_y, e_z = chunks[y], chunks[cells + y], chunks[2 * cells + y]
        e_x_up = chunks[y + 1] if y + 1 < cells else jnp.zeros_like(e_x)
        at, other = y * columns, (cells + y) * columns
        out_x[at : at + columns, :] = e_x
        out_yz[at : at + columns, :] = e_y
        out_yz[other : other + columns, :] = e_z
        out_send[at : at + columns, :] = jnp.where(down, e_y, forward_z(e_x) + e_z)
        out_send[other : other + columns, :] = jnp.where(down, e_z, (e_x - e_x_up) - e_y)


def material_kernel(mu_table, eps_table, shift, regions, out):
    labels = regions[...]
    cells = labels.shape[0]
    out[:cells, :] = table_rows(labels, mu_table)
    out[cells:, :] = shift[0] * table_rows(labels, eps_table)


def gram_kernel(columns, cells, field_x, field_yz, out):
    half = columns // 2
    chunks = [part(field_x, k, columns) for k in range(cells)]
    chunks += [part(field_yz, k, columns) for k in range(2 * cells)]
    flat = wide(chunks)
    out[half : half + columns, :] = chunks[0]
    out[half + columns :, :] = chunks[2 * cells]
    out[:half, :] = packed(inner(flat, flat))


def open_kernel(columns, cells, field_x, field_yz, gram_edge, ahead_y, out_open, out_gram):
    half = columns // 2
    out_gram[...] = gram_edge[:half, :] + ahead_y[:half, :]
    inside = first_core()
    for y in range(cells):
        e_x = part(field_x, y, columns)
        if y + 1 < cells:
            e_x_up = part(field_x, y + 1, columns)
        else:
            e_x_up = jnp.where(inside, ahead_y[half : half + columns, :], 0.0)
        e_y, e_z = part(field_yz, y, columns), part(field_yz, cells + y, columns)
        at, other = y * columns, (cells + y) * columns
        out_open[at : at + columns, :] = forward_z(e_x) + e_z
        out_open[other : other + columns, :] = (e_x - e_x_up) - e_y


def near_kernel(
    columns, cells, field_x, field_yz, ahead_y, material, open_yz, out_x, out_proj, out_send,
    out_thirds,
):
    half = columns // 2
    inside = first_core()
    left, right = [], []
    for y in range(cells):
        e_x = part(field_x, y, columns)
        e_y = part(field_yz, y, columns)
        e_z = part(field_yz, cells + y, columns)
        if y + 1 < cells:
            e_z_up = part(field_yz, cells + y + 1, columns)
        else:
            e_z_up = jnp.where(inside, ahead_y[half + columns :, :], 0.0)
        curl_x = (e_z_up - e_z) - forward_z(e_y)
        mu = material[y : y + 1, :]
        eps = -material[cells + y : cells + y + 1, :]
        m_x = mu * curl_x
        open_y, open_z = part(open_yz, y, columns), part(open_yz, cells + y, columns)
        at, other = y * columns, (cells + y) * columns
        out_x[at : at + columns, :] = m_x
        out_send[at : at + columns, :] = jnp.where(inside, open_y, e_y)
        out_send[other : other + columns, :] = jnp.where(inside, open_z, e_z)
        left += [curl_x, e_x, e_y, e_z, open_y, open_z]
        right += [m_x, eps * e_x, eps * e_y, eps * e_z, mu * open_y, mu * open_z]
    fields = [part(field_x, y, columns) for y in range(cells)]
    fields += [part(field_yz, k, columns) for k in range(2 * cells)]
    for i, values in enumerate(three(wide(fields))):
        out_thirds[i * columns : (i + 1) * columns, :] = values
    out_send[2 * cells * columns :, :] = material[...]
    out_proj[...] = packed(inner(wide(left), wide(right)))


def below_top():
    return lax.axis_index("row") + 1 < lax.axis_size("row")


def above_bottom():
    return lax.axis_index("row") > 0


def curl_kernel(
    columns, cells, field_yz, received, mu_received, open_yz, material, m_x, near, out_edge
):
    half = columns // 2
    ahead = first_core()
    behind = jnp.logical_and(jnp.logical_not(ahead), above_bottom())
    ahead_here = jnp.logical_and(ahead, below_top())
    left, right = [], []
    for y in range(cells):
        got_y, got_z = part(received, y, columns), part(received, cells + y, columns)
        own_y, own_z = part(field_yz, y, columns), part(field_yz, cells + y, columns)
        open_y, open_z = part(open_yz, y, columns), part(open_yz, cells + y, columns)
        mu_got = jnp.where(behind, mu_received[y : y + 1, :], 0.0)
        mu = jnp.where(ahead, material[y : y + 1, :], mu_got)
        open_y = jnp.where(ahead, open_y, jnp.where(behind, got_y, 0.0))
        open_z = jnp.where(ahead, open_z, jnp.where(behind, got_z, 0.0))
        e_y = jnp.where(ahead, jnp.where(ahead_here, got_y, 0.0), own_y)
        e_z = jnp.where(ahead, jnp.where(ahead_here, got_z, 0.0), own_z)
        left += [e_z, e_y]
        right += [mu * (0.5 * e_z - open_y), mu * (0.5 * e_y + open_z)]
        if y + 1 == cells:
            out_edge[half + columns :, :] = mu * (open_z + e_y)
    out_edge[half : half + columns, :] = part(m_x, cells - 1, columns)
    crossing = inner(wide(left), wide(right))
    out_edge[:half, :] = near[...] + packed(crossing + crossing.T)


def add_kernel(left, right, out):
    out[...] = left[...] + right[...]


def join_kernel(gram, edge, edge_other, out):
    half = gram.shape[0]
    out[:half, :] = gram[...]
    out[half:, :] = edge[:half, :] + edge_other[:half, :]


def sum_kernel(own, both, out, out_proj):
    half = out_proj.shape[0]
    total = own[...] + both[...]
    out[...] = total
    out_proj[...] = total[half:, :]


def factor(gram):
    columns = gram.shape[0]
    span, tile, width = 2 * columns, 8, 16
    count = columns // tile
    spread = lambda values: jnp.broadcast_to(values, (tile, span))
    sublane = lax.broadcasted_iota(jnp.int32, (tile, span), 0)
    lane = lax.broadcasted_iota(jnp.int32, (tile, span), 1)
    blocks = []
    for b in range(count):
        rows = gram[b * tile : (b + 1) * tile, :]
        rows = jnp.concatenate([rows, jnp.zeros_like(rows)], axis=1)
        blocks.append(jnp.where(lane == sublane + b * tile + columns, 1.0, rows))
    scales = [None] * count
    for start in range(0, columns, width):
        top = start // tile
        panel = [
            {b: spread(blocks[b][:, start + k : start + k + 1]) for b in range(top, count)}
            for k in range(width)
        ]
        for k in range(width):
            at, row = divmod(start + k, tile)
            pivot = spread(panel[k][at][row : row + 1, :])
            inverse = 1.0 / pivot
            ratio = {b: panel[k][b] * inverse for b in range(at, count)}
            ratio[at] = jnp.where(sublane > row, ratio[at], 0.0)
            root = lax.rsqrt(pivot)
            scales[at] = root if row == 0 else jnp.where(sublane == row, root, scales[at])
            for later in range(k + 1, width):
                to, below = divmod(start + later, tile)
                entry = spread(panel[k][to][below : below + 1, :])
                for b in range(at, count):
                    panel[later][b] = panel[later][b] - ratio[b] * entry
            pivot_row = spread(blocks[at][row : row + 1, :])
            for b in range(at, count):
                blocks[b] = blocks[b] - ratio[b] * pivot_row
    kept = []
    for b in range(count):
        row = sublane + b * tile
        kept.append(jnp.where((lane >= row) & (lane <= row + columns), blocks[b] * scales[b], 0.0))
    return jnp.concatenate(kept, axis=0)


def factor_kernel(total, sums, far, out):
    half = sums.shape[0] // 2
    out[...] = factor(unpacked(sums[:half, :] + far[:half, :]) / total)


def basis_kernel(
    columns, cells, field_x, field_yz, m_x, open_yz, first_got, mu_received, second_got, behind_y,
    material, thirds_ref, factors,
    out_basis, out_image, out_upper, out_inverse, basis, image, upper, sems,
):
    half = columns // 2
    stride = 3 * cells
    inverse = factors[:, columns:]
    out_inverse[...] = inverse
    upper[...] = factors[:, :columns]
    third = pltpu.make_async_copy(upper, out_upper, sems.at[2])
    third.start()

    def write(thirds, places, held, target, sem):
        lanes = held.shape[1]
        whole = product(inverse, thirds)
        for i, k in enumerate(places):
            held[pl.ds(k, columns, stride=stride), :] = whole[:, i * lanes : (i + 1) * lanes]
        copy = pltpu.make_async_copy(held, target, sem)
        copy.start()
        return copy

    first_copy = write(thirds_ref[...], range(stride), basis, out_basis, sems.at[0])
    ahead = first_core()
    top, bottom = below_top(), above_bottom()
    scaled_eps = material[cells:, :]
    images, places = [], []
    m_z_down = None
    for y in range(cells):
        e = [part(field_x, y, columns), part(field_yz, y, columns), part(field_yz, cells + y, columns)]
        last = 2 * cells * columns + y
        mu = material[y : y + 1, :]
        first = part(first_got, y, columns), part(first_got, cells + y, columns)
        second = part(second_got, y, columns), part(second_got, cells + y, columns)
        e_y_next = jnp.where(top, jnp.where(ahead, first[0], second[0]), 0.0)
        e_z_next = jnp.where(top, jnp.where(ahead, first[1], second[1]), 0.0)
        m = [
            part(m_x, y, columns),
            mu * (part(open_yz, y, columns) - e_z_next),
            mu * (part(open_yz, cells + y, columns) + e_y_next),
        ]
        if y > 0:
            m_x_down = part(m_x, y - 1, columns)
        else:
            m_x_down = jnp.where(ahead, 0.0, behind_y[half : half + columns, :])
            m_z_down = jnp.where(ahead, 0.0, behind_y[half + columns :, :])
        mu_last = jnp.where(ahead, second_got[last : last + 1, :], mu_received[y : y + 1, :])
        m_y_last = jnp.where(bottom, mu_last * (jnp.where(ahead, second[0], first[0]) - e[2]), 0.0)
        m_z_last = jnp.where(bottom, mu_last * (jnp.where(ahead, second[1], first[1]) + e[1]), 0.0)
        eps = scaled_eps[y : y + 1, :]
        images += [
            (m[2] - m_z_down) - backward_z(m[1]) - eps * e[0],
            backward_z(m[0]) - (m[2] - m_z_last) - eps * e[1],
            (m[1] - m_y_last) - (m[0] - m_x_down) - eps * e[2],
        ]
        places += [y, cells + y, 2 * cells + y]
        m_z_down = m[2]
    second_copy = write(jnp.concatenate(three(wide(images)), axis=0), places, image, out_image, sems.at[1])
    first_copy.wait()
    second_copy.wait()
    third.wait()


def proj_kernel(total, inverse, proj, far_cross, far, near, out):
    half = proj.shape[0]
    raw = (proj[...] + near[...]) + (far[half:, :] + far_cross[...])
    left = lax.dot_general(
        inverse[...], unpacked(raw) / total, (((1,), (0,)), ((), ())),
        precision=lax.Precision.HIGHEST, preferred_element_type=F32,
    )
    out[...] = inner(left, inverse[...])


SMEM = pl.BlockSpec(memory_space=pltpu.SMEM)
VMEM = pl.BlockSpec(memory_space=pltpu.VMEM)
ANY = pl.BlockSpec(memory_space=pl.ANY)


def call(body, scalars, arrays, outs, flops=None, far=0, scratch=()):
    outs = [out if isinstance(out[0], tuple) else (out, F32) for out in outs]
    shapes = [jax.ShapeDtypeStruct(shape, dtype) for shape, dtype in outs]
    cost = None
    if flops is not None:
        cost = pl.CostEstimate(flops=flops, bytes_accessed=0, transcendentals=0)
    return pl.pallas_call(
        body,
        out_shape=shapes,
        in_specs=[SMEM] * len(scalars) + [VMEM] * len(arrays),
        out_specs=[ANY] * far + [VMEM] * (len(shapes) - far),
        scratch_shapes=scratch,
        cost_estimate=cost,
        compiler_params=pltpu.CompilerParams(vmem_limit_bytes=32 * 1024 * 1024),
    )(*scalars, *arrays)


def swapped(x, axis, step):
    return lax.ppermute(x, axis, [(i, i ^ step) for i in range(lax.axis_size(axis))])


def local(krylov_basis, regions, mu_table, eps_table, shift_value):
    columns, parts, layers, cells, lanes = krylov_basis.shape
    rows, cols = lax.axis_size("row"), lax.axis_size("col")
    assert layers == 1 and parts == 3 and cols == 2 and rows >= 8 and rows & (rows - 1) == 0
    total = 3 * cells * lanes * rows * cols
    basis = krylov_basis.reshape(-1, lanes)
    labels = regions[0]
    half, outer = columns // 2, rows // 2
    small, large = (cells * columns, lanes), (2 * cells * columns, lanes)
    edge, pair = (half + 2 * columns, lanes), (half, 2 * columns)
    square = (columns, columns)

    (material,) = call(
        material_kernel, (mu_table, eps_table, shift_value), (labels,), ((2 * cells, lanes),),
        flops=0,
    )
    field_x, field_yz, send = call(
        functools.partial(pack_kernel, columns, cells), (), (basis,), (small, large, large), flops=0
    )
    first_got = lax.ppermute(send, ("row", "col"), halo_ring(rows, False))
    (gram_edge,) = call(
        functools.partial(gram_kernel, columns, cells), (), (field_x, field_yz), (edge,), flops=0
    )
    ahead_y = swapped(gram_edge, "col", 1)
    mu_received = lax.ppermute(material, ("row", "col"), halo_ring(rows, False))
    open_yz, gram = call(
        functools.partial(open_kernel, columns, cells),
        (),
        (field_x, field_yz, gram_edge, ahead_y),
        (large, pair),
        flops=0,
    )
    gram_other = swapped(gram, "row", 1)
    m_x, near, send, thirds = call(
        functools.partial(near_kernel, columns, cells),
        (),
        (field_x, field_yz, ahead_y, material, open_yz),
        (
            small, pair, (2 * cells * (columns + 1), lanes),
            ((3 * columns, 3 * cells * lanes), BF16),
        ),
        flops=0,
    )
    second_got = lax.ppermute(send, ("row", "col"), halo_ring(rows, True))
    (proj_edge,) = call(
        functools.partial(curl_kernel, columns, cells),
        (),
        (field_yz, first_got, mu_received, open_yz, material, m_x, near),
        (edge,),
        flops=10**10,
    )
    (gram,) = call(add_kernel, (), (gram, gram_other), (pair,), flops=10**10)
    behind_y = swapped(proj_edge, "col", 1)
    both = (2 * half, 2 * columns)
    (own,) = call(join_kernel, (), (gram, proj_edge, behind_y), (both,), flops=0)
    next_both = swapped(own, "row", outer)
    sums, proj = call(sum_kernel, (), (own, next_both), (both, pair), flops=0)
    step = 4
    while step < outer:
        sums = sums + swapped(sums, "row", step)
        proj = sums[half:]
        step *= 2
    far = swapped(sums, "row", 2)
    proj_near = swapped(proj, "row", 1)
    far_cross = swapped(proj, "row", 3)
    (factors,) = call(
        functools.partial(factor_kernel, total), (), (sums, far), ((columns, 2 * columns),), flops=0
    )
    basis_out, image_out, upper, inverse = call(
        functools.partial(basis_kernel, columns, cells),
        (),
        (
            field_x, field_yz, m_x, open_yz, first_got, mu_received, second_got, behind_y, material,
            thirds, factors,
        ),
        (basis.shape, basis.shape, square, square),
        flops=0,
        far=3,
        scratch=[
            pltpu.VMEM(basis.shape, F32),
            pltpu.VMEM(basis.shape, F32),
            pltpu.VMEM(square, F32),
            pltpu.SemaphoreType.DMA((3,)),
        ],
    )
    (projected,) = call(
        functools.partial(proj_kernel, total),
        (),
        (inverse, proj, far_cross, far, proj_near),
        (square,),
        flops=0,
    )
    return (
        basis_out.reshape(krylov_basis.shape),
        upper,
        image_out.reshape(krylov_basis.shape),
        projected,
    )


def solution(mesh):
    placed = (P("shift", None, "row", "col", None), P("row", "col", None), P(), P(), P("shift"))
    return jax.shard_map(
        local,
        mesh=mesh,
        in_specs=placed,
        out_specs=(
            P("shift", None, "row", "col", None),
            P("shift", None),
            P("shift", None, "row", "col", None),
            P("shift", None),
        ),
        check_vma=False,
    )
```

```python
import functools

import jax
import jax.numpy as jnp
from jax import lax
from jax.experimental import pallas as pl
from jax.experimental.pallas import tpu as pltpu
from jax.sharding import PartitionSpec as P

F32 = jnp.float32
BF16 = jnp.bfloat16


def halo_ring(rows, back):
    ahead = [((r, 0), (r - 1, 0)) for r in range(1, rows)] + [((0, 0), (0, 1))]
    ahead += [((r, 1), (r + 1, 1)) for r in range(rows - 1)] + [((rows - 1, 1), (rows - 1, 0))]
    pairs = [(2 * r + c, 2 * to_r + to_c) for (r, c), (to_r, to_c) in ahead]
    return [(j, i) for i, j in pairs] if back else pairs


def wide(chunks):
    return jnp.concatenate(chunks, axis=1)


def three(values):
    high = values.astype(BF16)
    rest = values - high.astype(F32)
    middle = rest.astype(BF16)
    low = (rest - middle.astype(F32)).astype(BF16)
    return [high, middle, low]


def inner(left, right):
    return lax.dot_general(
        left, right, (((1,), (1,)), ((), ())), precision=lax.Precision.HIGHEST,
        preferred_element_type=F32,
    )


def product(left, right_thirds):
    rows = left.shape[0]
    high, middle, low = three(left)
    none = jnp.zeros_like(high)
    stacked = jnp.concatenate(
        [wide([high, high, high]), wide([middle, middle, none]), wide([low, none, none])], axis=0
    )
    blocks = lax.dot_general(
        stacked, right_thirds, (((1,), (0,)), ((), ())), preferred_element_type=F32
    )
    return blocks[:rows, :] + (blocks[rows : 2 * rows, :] + blocks[2 * rows :, :])


def table_rows(labels, table_ref):
    result = jnp.zeros(labels.shape, F32)
    for region in range(table_ref.shape[0]):
        result = jnp.where(labels == region, table_ref[region], result)
    return result


def forward_z(values):
    lanes = values.shape[1]
    lane = lax.broadcasted_iota(jnp.int32, values.shape, 1)
    ahead = jnp.where(lane == lanes - 1, 0.0, pltpu.roll(values, lanes - 1, 1))
    return ahead - values


def backward_z(values):
    lane = lax.broadcasted_iota(jnp.int32, values.shape, 1)
    return values - jnp.where(lane == 0, 0.0, pltpu.roll(values, 1, 1))


def part(ref, index, columns):
    return ref[index * columns : (index + 1) * columns, :]


def packed(square):
    half = square.shape[0] // 2
    return jnp.concatenate([square[:half, :], square[half:, :]], axis=1)


def unpacked(pair):
    half = pair.shape[1] // 2
    return jnp.concatenate([pair[:, :half], pair[:, half:]], axis=0)


def first_core():
    return lax.axis_index("col") == 0


def pack_kernel(columns, cells, basis, out_x, out_yz, out_send):
    stride = 3 * cells
    chunks = [basis[pl.ds(k, columns, stride=stride), :] for k in range(stride)]
    down = first_core()
    for y in range(cells):
        e_x, e_y, e_z = chunks[y], chunks[cells + y], chunks[2 * cells + y]
        e_x_up = chunks[y + 1] if y + 1 < cells else jnp.zeros_like(e_x)
        at, other = y * columns, (cells + y) * columns
        out_x[at : at + columns, :] = e_x
        out_yz[at : at + columns, :] = e_y
        out_yz[other : other + columns, :] = e_z
        out_send[at : at + columns, :] = jnp.where(down, e_y, forward_z(e_x) + e_z)
        out_send[other : other + columns, :] = jnp.where(down, e_z, (e_x - e_x_up) - e_y)


def material_kernel(mu_table, eps_table, shift, regions, out):
    labels = regions[...]
    cells = labels.shape[0]
    out[:cells, :] = table_rows(labels, mu_table)
    out[cells:, :] = shift[0] * table_rows(labels, eps_table)


def gram_kernel(columns, cells, field_x, field_yz, out):
    half = columns // 2
    chunks = [part(field_x, k, columns) for k in range(cells)]
    chunks += [part(field_yz, k, columns) for k in range(2 * cells)]
    flat = wide(chunks)
    out[half : half + columns, :] = chunks[0]
    out[half + columns :, :] = chunks[2 * cells]
    out[:half, :] = packed(inner(flat, flat))


def open_kernel(columns, cells, field_x, field_yz, gram_edge, ahead_y, out_open, out_gram):
    half = columns // 2
    out_gram[...] = gram_edge[:half, :] + ahead_y[:half, :]
    inside = first_core()
    for y in range(cells):
        e_x = part(field_x, y, columns)
        if y + 1 < cells:
            e_x_up = part(field_x, y + 1, columns)
        else:
            e_x_up = jnp.where(inside, ahead_y[half : half + columns, :], 0.0)
        e_y, e_z = part(field_yz, y, columns), part(field_yz, cells + y, columns)
        at, other = y * columns, (cells + y) * columns
        out_open[at : at + columns, :] = forward_z(e_x) + e_z
        out_open[other : other + columns, :] = (e_x - e_x_up) - e_y


def near_kernel(
    columns, cells, field_x, field_yz, ahead_y, material, open_yz, out_x, out_proj, out_send,
    out_thirds,
):
    half = columns // 2
    inside = first_core()
    left, right = [], []
    for y in range(cells):
        e_x = part(field_x, y, columns)
        e_y = part(field_yz, y, columns)
        e_z = part(field_yz, cells + y, columns)
        if y + 1 < cells:
            e_z_up = part(field_yz, cells + y + 1, columns)
        else:
            e_z_up = jnp.where(inside, ahead_y[half + columns :, :], 0.0)
        curl_x = (e_z_up - e_z) - forward_z(e_y)
        mu = material[y : y + 1, :]
        eps = -material[cells + y : cells + y + 1, :]
        m_x = mu * curl_x
        open_y, open_z = part(open_yz, y, columns), part(open_yz, cells + y, columns)
        at, other = y * columns, (cells + y) * columns
        out_x[at : at + columns, :] = m_x
        out_send[at : at + columns, :] = jnp.where(inside, open_y, e_y)
        out_send[other : other + columns, :] = jnp.where(inside, open_z, e_z)
        left += [curl_x, e_x, e_y, e_z, open_y, open_z]
        right += [m_x, eps * e_x, eps * e_y, eps * e_z, mu * open_y, mu * open_z]
    fields = [part(field_x, y, columns) for y in range(cells)]
    fields += [part(field_yz, k, columns) for k in range(2 * cells)]
    for i, values in enumerate(three(wide(fields))):
        out_thirds[i * columns : (i + 1) * columns, :] = values
    out_send[2 * cells * columns :, :] = material[...]
    out_proj[...] = packed(inner(wide(left), wide(right)))


def below_top():
    return lax.axis_index("row") + 1 < lax.axis_size("row")


def above_bottom():
    return lax.axis_index("row") > 0


def curl_kernel(
    columns, cells, field_yz, received, mu_received, open_yz, material, m_x, near, out_edge,
    out_proj,
):
    ahead = first_core()
    behind = jnp.logical_and(jnp.logical_not(ahead), above_bottom())
    ahead_here = jnp.logical_and(ahead, below_top())
    left, right = [], []
    for y in range(cells):
        got_y, got_z = part(received, y, columns), part(received, cells + y, columns)
        own_y, own_z = part(field_yz, y, columns), part(field_yz, cells + y, columns)
        open_y, open_z = part(open_yz, y, columns), part(open_yz, cells + y, columns)
        mu_got = jnp.where(behind, mu_received[y : y + 1, :], 0.0)
        mu = jnp.where(ahead, material[y : y + 1, :], mu_got)
        open_y = jnp.where(ahead, open_y, jnp.where(behind, got_y, 0.0))
        open_z = jnp.where(ahead, open_z, jnp.where(behind, got_z, 0.0))
        e_y = jnp.where(ahead, jnp.where(ahead_here, got_y, 0.0), own_y)
        e_z = jnp.where(ahead, jnp.where(ahead_here, got_z, 0.0), own_z)
        left += [e_z, e_y]
        right += [mu * (0.5 * e_z - open_y), mu * (0.5 * e_y + open_z)]
        if y + 1 == cells:
            out_edge[columns:, :] = mu * (open_z + e_y)
    out_edge[:columns, :] = part(m_x, cells - 1, columns)
    crossing = inner(wide(left), wide(right))
    out_proj[...] = near[...] + packed(crossing + crossing.T)


def add_kernel(left, right, out):
    out[...] = left[...] + right[...]


def join_kernel(gram, proj, proj_other, out):
    half = gram.shape[0]
    out[:half, :] = gram[...]
    out[half:, :] = proj[...] + proj_other[...]


def sum_kernel(own, both, out, out_proj):
    half = out_proj.shape[0]
    total = own[...] + both[...]
    out[...] = total
    out_proj[...] = total[half:, :]


def factor(gram):
    columns = gram.shape[0]
    span, tile, width = 2 * columns, 8, 16
    count = columns // tile
    spread = lambda values: jnp.broadcast_to(values, (tile, span))
    sublane = lax.broadcasted_iota(jnp.int32, (tile, span), 0)
    lane = lax.broadcasted_iota(jnp.int32, (tile, span), 1)
    blocks = []
    for b in range(count):
        rows = gram[b * tile : (b + 1) * tile, :]
        rows = jnp.concatenate([rows, jnp.zeros_like(rows)], axis=1)
        blocks.append(jnp.where(lane == sublane + b * tile + columns, 1.0, rows))
    scales = [None] * count
    for start in range(0, columns, width):
        top = start // tile
        panel = [
            {b: spread(blocks[b][:, start + k : start + k + 1]) for b in range(top, count)}
            for k in range(width)
        ]
        for k in range(width):
            at, row = divmod(start + k, tile)
            pivot = spread(panel[k][at][row : row + 1, :])
            inverse = 1.0 / pivot
            ratio = {b: panel[k][b] * inverse for b in range(at, count)}
            ratio[at] = jnp.where(sublane > row, ratio[at], 0.0)
            root = lax.rsqrt(pivot)
            scales[at] = root if row == 0 else jnp.where(sublane == row, root, scales[at])
            for later in range(k + 1, width):
                to, below = divmod(start + later, tile)
                entry = spread(panel[k][to][below : below + 1, :])
                for b in range(at, count):
                    panel[later][b] = panel[later][b] - ratio[b] * entry
            pivot_row = spread(blocks[at][row : row + 1, :])
            for b in range(at, count):
                blocks[b] = blocks[b] - ratio[b] * pivot_row
    kept = []
    for b in range(count):
        row = sublane + b * tile
        kept.append(jnp.where((lane >= row) & (lane <= row + columns), blocks[b] * scales[b], 0.0))
    return jnp.concatenate(kept, axis=0)


def factor_kernel(total, sums, far, out):
    half = sums.shape[0] // 2
    out[...] = factor(unpacked(sums[:half, :] + far[:half, :]) / total)


def basis_kernel(
    columns, cells, field_x, field_yz, m_x, open_yz, first_got, mu_received, second_got, behind_y,
    material, thirds_ref, factors,
    out_basis, out_image, out_upper, out_inverse, basis, image, upper, sems,
):
    stride = 3 * cells
    inverse = factors[:, columns:]
    out_inverse[...] = inverse
    upper[...] = factors[:, :columns]
    third = pltpu.make_async_copy(upper, out_upper, sems.at[2])
    third.start()

    def write(thirds, places, held, target, sem):
        lanes = held.shape[1]
        whole = product(inverse, thirds)
        for i, k in enumerate(places):
            held[pl.ds(k, columns, stride=stride), :] = whole[:, i * lanes : (i + 1) * lanes]
        copy = pltpu.make_async_copy(held, target, sem)
        copy.start()
        return copy

    first_copy = write(thirds_ref[...], range(stride), basis, out_basis, sems.at[0])
    ahead = first_core()
    top, bottom = below_top(), above_bottom()
    scaled_eps = material[cells:, :]
    images, places = [], []
    m_z_down = None
    for y in range(cells):
        e = [part(field_x, y, columns), part(field_yz, y, columns), part(field_yz, cells + y, columns)]
        last = 2 * cells * columns + y
        mu = material[y : y + 1, :]
        first = part(first_got, y, columns), part(first_got, cells + y, columns)
        second = part(second_got, y, columns), part(second_got, cells + y, columns)
        e_y_next = jnp.where(top, jnp.where(ahead, first[0], second[0]), 0.0)
        e_z_next = jnp.where(top, jnp.where(ahead, first[1], second[1]), 0.0)
        m = [
            part(m_x, y, columns),
            mu * (part(open_yz, y, columns) - e_z_next),
            mu * (part(open_yz, cells + y, columns) + e_y_next),
        ]
        if y > 0:
            m_x_down = part(m_x, y - 1, columns)
        else:
            m_x_down = jnp.where(ahead, 0.0, behind_y[:columns, :])
            m_z_down = jnp.where(ahead, 0.0, behind_y[columns:, :])
        mu_last = jnp.where(ahead, second_got[last : last + 1, :], mu_received[y : y + 1, :])
        m_y_last = jnp.where(bottom, mu_last * (jnp.where(ahead, second[0], first[0]) - e[2]), 0.0)
        m_z_last = jnp.where(bottom, mu_last * (jnp.where(ahead, second[1], first[1]) + e[1]), 0.0)
        eps = scaled_eps[y : y + 1, :]
        images += [
            (m[2] - m_z_down) - backward_z(m[1]) - eps * e[0],
            backward_z(m[0]) - (m[2] - m_z_last) - eps * e[1],
            (m[1] - m_y_last) - (m[0] - m_x_down) - eps * e[2],
        ]
        places += [y, cells + y, 2 * cells + y]
        m_z_down = m[2]
    second_copy = write(jnp.concatenate(three(wide(images)), axis=0), places, image, out_image, sems.at[1])
    first_copy.wait()
    second_copy.wait()
    third.wait()


def proj_kernel(total, inverse, proj, near, far, far_cross, out):
    half = proj.shape[0]
    raw = (proj[...] + near[...]) + (far[half:, :] + far_cross[...])
    left = lax.dot_general(
        inverse[...], unpacked(raw) / total, (((1,), (0,)), ((), ())),
        precision=lax.Precision.HIGHEST, preferred_element_type=F32,
    )
    out[...] = inner(left, inverse[...])


SMEM = pl.BlockSpec(memory_space=pltpu.SMEM)
VMEM = pl.BlockSpec(memory_space=pltpu.VMEM)
ANY = pl.BlockSpec(memory_space=pl.ANY)


def call(body, scalars, arrays, outs, flops=None, far=0, scratch=()):
    outs = [out if isinstance(out[0], tuple) else (out, F32) for out in outs]
    shapes = [jax.ShapeDtypeStruct(shape, dtype) for shape, dtype in outs]
    cost = None
    if flops is not None:
        cost = pl.CostEstimate(flops=flops, bytes_accessed=0, transcendentals=0)
    return pl.pallas_call(
        body,
        out_shape=shapes,
        in_specs=[SMEM] * len(scalars) + [VMEM] * len(arrays),
        out_specs=[ANY] * far + [VMEM] * (len(shapes) - far),
        scratch_shapes=scratch,
        cost_estimate=cost,
        compiler_params=pltpu.CompilerParams(vmem_limit_bytes=32 * 1024 * 1024),
    )(*scalars, *arrays)


def swapped(x, axis, step):
    return lax.ppermute(x, axis, [(i, i ^ step) for i in range(lax.axis_size(axis))])


def local(krylov_basis, regions, mu_table, eps_table, shift_value):
    columns, parts, layers, cells, lanes = krylov_basis.shape
    rows, cols = lax.axis_size("row"), lax.axis_size("col")
    assert layers == 1 and parts == 3 and cols == 2 and rows >= 8 and rows & (rows - 1) == 0
    total = 3 * cells * lanes * rows * cols
    basis = krylov_basis.reshape(-1, lanes)
    labels = regions[0]
    half, outer = columns // 2, rows // 2
    small, large = (cells * columns, lanes), (2 * cells * columns, lanes)
    edge, pair = (half + 2 * columns, lanes), (half, 2 * columns)
    square = (columns, columns)

    (material,) = call(
        material_kernel, (mu_table, eps_table, shift_value), (labels,), ((2 * cells, lanes),),
        flops=0,
    )
    field_x, field_yz, send = call(
        functools.partial(pack_kernel, columns, cells), (), (basis,), (small, large, large), flops=0
    )
    first_got = lax.ppermute(send, ("row", "col"), halo_ring(rows, False))
    (gram_edge,) = call(
        functools.partial(gram_kernel, columns, cells), (), (field_x, field_yz), (edge,), flops=0
    )
    ahead_y = swapped(gram_edge, "col", 1)
    mu_received = lax.ppermute(material, ("row", "col"), halo_ring(rows, False))
    open_yz, gram = call(
        functools.partial(open_kernel, columns, cells),
        (),
        (field_x, field_yz, gram_edge, ahead_y),
        (large, pair),
        flops=0,
    )
    gram_other = swapped(gram, "row", 1)
    m_x, near, send, thirds = call(
        functools.partial(near_kernel, columns, cells),
        (),
        (field_x, field_yz, ahead_y, material, open_yz),
        (
            small, pair, (2 * cells * (columns + 1), lanes),
            ((3 * columns, 3 * cells * lanes), BF16),
        ),
        flops=0,
    )
    second_got = lax.ppermute(send, ("row", "col"), halo_ring(rows, True))
    edge_m, proj = call(
        functools.partial(curl_kernel, columns, cells),
        (),
        (field_yz, first_got, mu_received, open_yz, material, m_x, near),
        ((2 * columns, lanes), pair),
        flops=10**10,
    )
    (gram,) = call(add_kernel, (), (gram, gram_other), (pair,), flops=10**10)
    proj_other = swapped(proj, "col", 1)
    behind_y = swapped(edge_m, "col", 1)
    both = (2 * half, 2 * columns)
    (own,) = call(join_kernel, (), (gram, proj, proj_other), (both,), flops=0)
    next_both = swapped(own, "row", outer)
    sums, proj = call(sum_kernel, (), (own, next_both), (both, pair), flops=0)
    step = 4
    while step < outer:
        sums = sums + swapped(sums, "row", step)
        proj = sums[half:]
        step *= 2
    far = swapped(sums, "row", 2)
    proj_near = swapped(proj, "row", 1)
    far_cross = swapped(proj, "row", 3)
    (factors,) = call(
        functools.partial(factor_kernel, total), (), (sums, far), ((columns, 2 * columns),), flops=0
    )
    basis_out, image_out, upper, inverse = call(
        functools.partial(basis_kernel, columns, cells),
        (),
        (
            field_x, field_yz, m_x, open_yz, first_got, mu_received, second_got, behind_y, material,
            thirds, factors,
        ),
        (basis.shape, basis.shape, square, square),
        flops=0,
        far=3,
        scratch=[
            pltpu.VMEM(basis.shape, F32),
            pltpu.VMEM(basis.shape, F32),
            pltpu.VMEM(square, F32),
            pltpu.SemaphoreType.DMA((3,)),
        ],
    )
    (projected,) = call(
        functools.partial(proj_kernel, total),
        (),
        (inverse, proj, proj_near, far, far_cross),
        (square,),
        flops=0,
    )
    return (
        basis_out.reshape(krylov_basis.shape),
        upper,
        image_out.reshape(krylov_basis.shape),
        projected,
    )


def solution(mesh):
    placed = (P("shift", None, "row", "col", None), P("row", "col", None), P(), P(), P("shift"))
    return jax.shard_map(
        local,
        mesh=mesh,
        in_specs=placed,
        out_specs=(
            P("shift", None, "row", "col", None),
            P("shift", None),
            P("shift", None, "row", "col", None),
            P("shift", None),
        ),
        check_vma=False,
    )
```

```python
import functools

import jax
import jax.numpy as jnp
from jax import lax
from jax.experimental import pallas as pl
from jax.experimental.pallas import tpu as pltpu
from jax.sharding import PartitionSpec as P

F32 = jnp.float32
BF16 = jnp.bfloat16


def halo_ring(rows, back):
    ahead = [((r, 0), (r - 1, 0)) for r in range(1, rows)] + [((0, 0), (0, 1))]
    ahead += [((r, 1), (r + 1, 1)) for r in range(rows - 1)] + [((rows - 1, 1), (rows - 1, 0))]
    pairs = [(2 * r + c, 2 * to_r + to_c) for (r, c), (to_r, to_c) in ahead]
    return [(j, i) for i, j in pairs] if back else pairs


def wide(chunks):
    return jnp.concatenate(chunks, axis=1)


def three(values):
    high = values.astype(BF16)
    rest = values - high.astype(F32)
    middle = rest.astype(BF16)
    low = (rest - middle.astype(F32)).astype(BF16)
    return [high, middle, low]


def inner(left, right):
    return lax.dot_general(
        left, right, (((1,), (1,)), ((), ())), precision=lax.Precision.HIGHEST,
        preferred_element_type=F32,
    )


def product(left, right_thirds):
    rows = left.shape[0]
    high, middle, low = three(left)
    none = jnp.zeros_like(high)
    stacked = jnp.concatenate(
        [wide([high, high, high]), wide([middle, middle, none]), wide([low, none, none])], axis=0
    )
    blocks = lax.dot_general(
        stacked, right_thirds, (((1,), (0,)), ((), ())), preferred_element_type=F32
    )
    return blocks[:rows, :] + (blocks[rows : 2 * rows, :] + blocks[2 * rows :, :])


def table_rows(labels, table_ref):
    result = jnp.zeros(labels.shape, F32)
    for region in range(table_ref.shape[0]):
        result = jnp.where(labels == region, table_ref[region], result)
    return result


def forward_z(values):
    lanes = values.shape[1]
    lane = lax.broadcasted_iota(jnp.int32, values.shape, 1)
    ahead = jnp.where(lane == lanes - 1, 0.0, pltpu.roll(values, lanes - 1, 1))
    return ahead - values


def backward_z(values):
    lane = lax.broadcasted_iota(jnp.int32, values.shape, 1)
    return values - jnp.where(lane == 0, 0.0, pltpu.roll(values, 1, 1))


def part(ref, index, columns):
    return ref[index * columns : (index + 1) * columns, :]


def packed(square):
    half = square.shape[0] // 2
    return jnp.concatenate([square[:half, :], square[half:, :]], axis=1)


def unpacked(pair):
    half = pair.shape[1] // 2
    return jnp.concatenate([pair[:, :half], pair[:, half:]], axis=0)


def first_core():
    return lax.axis_index("col") == 0


def pack_kernel(columns, cells, basis, out_x, out_yz, out_send):
    stride = 3 * cells
    chunks = [basis[pl.ds(k, columns, stride=stride), :] for k in range(stride)]
    down = first_core()
    for y in range(cells):
        e_x, e_y, e_z = chunks[y], chunks[cells + y], chunks[2 * cells + y]
        e_x_up = chunks[y + 1] if y + 1 < cells else jnp.zeros_like(e_x)
        at, other = y * columns, (cells + y) * columns
        out_x[at : at + columns, :] = e_x
        out_yz[at : at + columns, :] = e_y
        out_yz[other : other + columns, :] = e_z
        out_send[at : at + columns, :] = jnp.where(down, e_y, forward_z(e_x) + e_z)
        out_send[other : other + columns, :] = jnp.where(down, e_z, (e_x - e_x_up) - e_y)


def material_kernel(mu_table, eps_table, shift, regions, out):
    labels = regions[...]
    cells = labels.shape[0]
    out[:cells, :] = table_rows(labels, mu_table)
    out[cells:, :] = shift[0] * table_rows(labels, eps_table)


def gram_kernel(columns, cells, field_x, field_yz, out):
    half = columns // 2
    chunks = [part(field_x, k, columns) for k in range(cells)]
    chunks += [part(field_yz, k, columns) for k in range(2 * cells)]
    flat = wide(chunks)
    out[half : half + columns, :] = chunks[0]
    out[half + columns :, :] = chunks[2 * cells]
    out[:half, :] = packed(inner(flat, flat))


def open_kernel(columns, cells, field_x, field_yz, gram_edge, ahead_y, out_open, out_gram):
    half = columns // 2
    out_gram[...] = gram_edge[:half, :] + ahead_y[:half, :]
    inside = first_core()
    for y in range(cells):
        e_x = part(field_x, y, columns)
        if y + 1 < cells:
            e_x_up = part(field_x, y + 1, columns)
        else:
            e_x_up = jnp.where(inside, ahead_y[half : half + columns, :], 0.0)
        e_y, e_z = part(field_yz, y, columns), part(field_yz, cells + y, columns)
        at, other = y * columns, (cells + y) * columns
        out_open[at : at + columns, :] = forward_z(e_x) + e_z
        out_open[other : other + columns, :] = (e_x - e_x_up) - e_y


def near_kernel(
    columns, cells, field_x, field_yz, ahead_y, material, open_yz, out_x, out_proj, out_send,
    out_thirds,
):
    half = columns // 2
    inside = first_core()
    left, right = [], []
    for y in range(cells):
        e_x = part(field_x, y, columns)
        e_y = part(field_yz, y, columns)
        e_z = part(field_yz, cells + y, columns)
        if y + 1 < cells:
            e_z_up = part(field_yz, cells + y + 1, columns)
        else:
            e_z_up = jnp.where(inside, ahead_y[half + columns :, :], 0.0)
        curl_x = (e_z_up - e_z) - forward_z(e_y)
        mu = material[y : y + 1, :]
        eps = -material[cells + y : cells + y + 1, :]
        m_x = mu * curl_x
        open_y, open_z = part(open_yz, y, columns), part(open_yz, cells + y, columns)
        at, other = y * columns, (cells + y) * columns
        out_x[at : at + columns, :] = m_x
        out_send[at : at + columns, :] = jnp.where(inside, open_y, e_y)
        out_send[other : other + columns, :] = jnp.where(inside, open_z, e_z)
        left += [curl_x, e_x, e_y, e_z, open_y, open_z]
        right += [m_x, eps * e_x, eps * e_y, eps * e_z, mu * open_y, mu * open_z]
    fields = [part(field_x, y, columns) for y in range(cells)]
    fields += [part(field_yz, k, columns) for k in range(2 * cells)]
    for i, values in enumerate(three(wide(fields))):
        out_thirds[i * columns : (i + 1) * columns, :] = values
    out_send[2 * cells * columns :, :] = material[...]
    out_proj[...] = packed(inner(wide(left), wide(right)))


def below_top():
    return lax.axis_index("row") + 1 < lax.axis_size("row")


def above_bottom():
    return lax.axis_index("row") > 0


def curl_kernel(
    columns, cells, field_yz, received, mu_received, open_yz, material, m_x, near, out_edge,
    out_proj,
):
    ahead = first_core()
    behind = jnp.logical_and(jnp.logical_not(ahead), above_bottom())
    ahead_here = jnp.logical_and(ahead, below_top())
    left, right = [], []
    for y in range(cells):
        got_y, got_z = part(received, y, columns), part(received, cells + y, columns)
        own_y, own_z = part(field_yz, y, columns), part(field_yz, cells + y, columns)
        open_y, open_z = part(open_yz, y, columns), part(open_yz, cells + y, columns)
        mu_got = jnp.where(behind, mu_received[y : y + 1, :], 0.0)
        mu = jnp.where(ahead, material[y : y + 1, :], mu_got)
        open_y = jnp.where(ahead, open_y, jnp.where(behind, got_y, 0.0))
        open_z = jnp.where(ahead, open_z, jnp.where(behind, got_z, 0.0))
        e_y = jnp.where(ahead, jnp.where(ahead_here, got_y, 0.0), own_y)
        e_z = jnp.where(ahead, jnp.where(ahead_here, got_z, 0.0), own_z)
        left += [e_z, e_y]
        right += [mu * (0.5 * e_z - open_y), mu * (0.5 * e_y + open_z)]
        if y + 1 == cells:
            out_edge[columns:, :] = mu * (open_z + e_y)
    out_edge[:columns, :] = part(m_x, cells - 1, columns)
    crossing = inner(wide(left), wide(right))
    out_proj[...] = near[...] + packed(crossing + crossing.T)


def add_kernel(left, right, out):
    out[...] = left[...] + right[...]


def join_kernel(gram, proj, proj_other, out):
    half = gram.shape[0]
    out[:half, :] = gram[...]
    out[half:, :] = proj[...] + proj_other[...]


def sum_kernel(own, both, out, out_proj):
    half = out_proj.shape[0]
    total = own[...] + both[...]
    out[...] = total
    out_proj[...] = total[half:, :]


def factor(gram):
    columns = gram.shape[0]
    span, tile, width = 2 * columns, 8, 16
    count = columns // tile
    spread = lambda values: jnp.broadcast_to(values, (tile, span))
    sublane = lax.broadcasted_iota(jnp.int32, (tile, span), 0)
    lane = lax.broadcasted_iota(jnp.int32, (tile, span), 1)
    blocks = []
    for b in range(count):
        rows = gram[b * tile : (b + 1) * tile, :]
        rows = jnp.concatenate([rows, jnp.zeros_like(rows)], axis=1)
        blocks.append(jnp.where(lane == sublane + b * tile + columns, 1.0, rows))
    scales = [None] * count
    for start in range(0, columns, width):
        top = start // tile
        panel = [
            {b: spread(blocks[b][:, start + k : start + k + 1]) for b in range(top, count)}
            for k in range(width)
        ]
        for k in range(width):
            at, row = divmod(start + k, tile)
            pivot = spread(panel[k][at][row : row + 1, :])
            inverse = 1.0 / pivot
            ratio = {b: panel[k][b] * inverse for b in range(at, count)}
            ratio[at] = jnp.where(sublane > row, ratio[at], 0.0)
            root = lax.rsqrt(pivot)
            scales[at] = root if row == 0 else jnp.where(sublane == row, root, scales[at])
            for later in range(k + 1, width):
                to, below = divmod(start + later, tile)
                entry = spread(panel[k][to][below : below + 1, :])
                for b in range(at, count):
                    panel[later][b] = panel[later][b] - ratio[b] * entry
            pivot_row = spread(blocks[at][row : row + 1, :])
            for b in range(at, count):
                blocks[b] = blocks[b] - ratio[b] * pivot_row
    kept = []
    for b in range(count):
        row = sublane + b * tile
        kept.append(jnp.where((lane >= row) & (lane <= row + columns), blocks[b] * scales[b], 0.0))
    return jnp.concatenate(kept, axis=0)


def factor_kernel(total, sums, far, out):
    half = sums.shape[0] // 2
    out[...] = factor(unpacked(sums[:half, :] + far[:half, :]) / total)


def basis_kernel(
    columns, cells, field_x, field_yz, m_x, open_yz, first_got, mu_received, second_got, behind_y,
    material, thirds_ref, factors,
    out_basis, out_image, out_upper, out_inverse, basis, image, upper, sems,
):
    stride = 3 * cells
    inverse = factors[:, columns:]
    out_inverse[...] = inverse
    upper[...] = factors[:, :columns]
    third = pltpu.make_async_copy(upper, out_upper, sems.at[2])
    third.start()

    def write(thirds, places, held, target, sem):
        lanes = held.shape[1]
        whole = product(inverse, thirds)
        for i, k in enumerate(places):
            held[pl.ds(k, columns, stride=stride), :] = whole[:, i * lanes : (i + 1) * lanes]
        copy = pltpu.make_async_copy(held, target, sem)
        copy.start()
        return copy

    first_copy = write(thirds_ref[...], range(stride), basis, out_basis, sems.at[0])
    ahead = first_core()
    top, bottom = below_top(), above_bottom()
    scaled_eps = material[cells:, :]
    images, places = [], []
    m_z_down = None
    for y in range(cells):
        e = [part(field_x, y, columns), part(field_yz, y, columns), part(field_yz, cells + y, columns)]
        last = 2 * cells * columns + y
        mu = material[y : y + 1, :]
        first = part(first_got, y, columns), part(first_got, cells + y, columns)
        second = part(second_got, y, columns), part(second_got, cells + y, columns)
        e_y_next = jnp.where(top, jnp.where(ahead, first[0], second[0]), 0.0)
        e_z_next = jnp.where(top, jnp.where(ahead, first[1], second[1]), 0.0)
        m = [
            part(m_x, y, columns),
            mu * (part(open_yz, y, columns) - e_z_next),
            mu * (part(open_yz, cells + y, columns) + e_y_next),
        ]
        if y > 0:
            m_x_down = part(m_x, y - 1, columns)
        else:
            m_x_down = jnp.where(ahead, 0.0, behind_y[:columns, :])
            m_z_down = jnp.where(ahead, 0.0, behind_y[columns:, :])
        mu_last = jnp.where(ahead, second_got[last : last + 1, :], mu_received[y : y + 1, :])
        m_y_last = jnp.where(bottom, mu_last * (jnp.where(ahead, second[0], first[0]) - e[2]), 0.0)
        m_z_last = jnp.where(bottom, mu_last * (jnp.where(ahead, second[1], first[1]) + e[1]), 0.0)
        eps = scaled_eps[y : y + 1, :]
        images += [
            (m[2] - m_z_down) - backward_z(m[1]) - eps * e[0],
            backward_z(m[0]) - (m[2] - m_z_last) - eps * e[1],
            (m[1] - m_y_last) - (m[0] - m_x_down) - eps * e[2],
        ]
        places += [y, cells + y, 2 * cells + y]
        m_z_down = m[2]
    second_copy = write(jnp.concatenate(three(wide(images)), axis=0), places, image, out_image, sems.at[1])
    first_copy.wait()
    second_copy.wait()
    third.wait()


def proj_kernel(total, inverse, proj, near, far, far_cross, out):
    half = proj.shape[0]
    raw = (proj[...] + near[...]) + (far[half:, :] + far_cross[...])
    left = lax.dot_general(
        inverse[...], unpacked(raw) / total, (((1,), (0,)), ((), ())),
        precision=lax.Precision.HIGHEST, preferred_element_type=F32,
    )
    out[...] = inner(left, inverse[...])


SMEM = pl.BlockSpec(memory_space=pltpu.SMEM)
VMEM = pl.BlockSpec(memory_space=pltpu.VMEM)
ANY = pl.BlockSpec(memory_space=pl.ANY)


def call(body, scalars, arrays, outs, flops=None, far=0, scratch=()):
    outs = [out if isinstance(out[0], tuple) else (out, F32) for out in outs]
    shapes = [jax.ShapeDtypeStruct(shape, dtype) for shape, dtype in outs]
    cost = None
    if flops is not None:
        cost = pl.CostEstimate(flops=flops, bytes_accessed=0, transcendentals=0)
    return pl.pallas_call(
        body,
        out_shape=shapes,
        in_specs=[SMEM] * len(scalars) + [VMEM] * len(arrays),
        out_specs=[ANY] * far + [VMEM] * (len(shapes) - far),
        scratch_shapes=scratch,
        cost_estimate=cost,
        compiler_params=pltpu.CompilerParams(vmem_limit_bytes=32 * 1024 * 1024),
    )(*scalars, *arrays)


def swapped(x, axis, step):
    return lax.ppermute(x, axis, [(i, i ^ step) for i in range(lax.axis_size(axis))])


def local(krylov_basis, regions, mu_table, eps_table, shift_value):
    columns, parts, layers, cells, lanes = krylov_basis.shape
    rows, cols = lax.axis_size("row"), lax.axis_size("col")
    assert layers == 1 and parts == 3 and cols == 2 and rows >= 8 and rows & (rows - 1) == 0
    total = 3 * cells * lanes * rows * cols
    basis = krylov_basis.reshape(-1, lanes)
    labels = regions[0]
    half, outer = columns // 2, rows // 2
    small, large = (cells * columns, lanes), (2 * cells * columns, lanes)
    edge, pair = (half + 2 * columns, lanes), (half, 2 * columns)
    square = (columns, columns)

    (material,) = call(
        material_kernel, (mu_table, eps_table, shift_value), (labels,), ((2 * cells, lanes),),
        flops=0,
    )
    field_x, field_yz, send = call(
        functools.partial(pack_kernel, columns, cells), (), (basis,), (small, large, large), flops=0
    )
    first_got = lax.ppermute(send, ("row", "col"), halo_ring(rows, False))
    (gram_edge,) = call(
        functools.partial(gram_kernel, columns, cells), (), (field_x, field_yz), (edge,), flops=0
    )
    ahead_y = swapped(gram_edge, "col", 1)
    mu_received = lax.ppermute(material, ("row", "col"), halo_ring(rows, False))
    open_yz, gram = call(
        functools.partial(open_kernel, columns, cells),
        (),
        (field_x, field_yz, gram_edge, ahead_y),
        (large, pair),
        flops=0,
    )
    gram_other = swapped(gram, "row", 2)
    m_x, near, send, thirds = call(
        functools.partial(near_kernel, columns, cells),
        (),
        (field_x, field_yz, ahead_y, material, open_yz),
        (
            small, pair, (2 * cells * (columns + 1), lanes),
            ((3 * columns, 3 * cells * lanes), BF16),
        ),
        flops=0,
    )
    second_got = lax.ppermute(send, ("row", "col"), halo_ring(rows, True))
    edge_m, proj = call(
        functools.partial(curl_kernel, columns, cells),
        (),
        (field_yz, first_got, mu_received, open_yz, material, m_x, near),
        ((2 * columns, lanes), pair),
        flops=10**10,
    )
    (gram,) = call(add_kernel, (), (gram, gram_other), (pair,), flops=10**10)
    proj_other = swapped(proj, "col", 1)
    behind_y = swapped(edge_m, "col", 1)
    both = (2 * half, 2 * columns)
    (own,) = call(join_kernel, (), (gram, proj, proj_other), (both,), flops=0)
    next_both = swapped(own, "row", outer)
    sums, proj = call(sum_kernel, (), (own, next_both), (both, pair), flops=0)
    step = 4
    while step < outer:
        sums = sums + swapped(sums, "row", step)
        proj = sums[half:]
        step *= 2
    far = swapped(sums, "row", 1)
    proj_near = swapped(proj, "row", 2)
    far_cross = swapped(proj, "row", 3)
    (factors,) = call(
        functools.partial(factor_kernel, total), (), (sums, far), ((columns, 2 * columns),), flops=0
    )
    basis_out, image_out, upper, inverse = call(
        functools.partial(basis_kernel, columns, cells),
        (),
        (
            field_x, field_yz, m_x, open_yz, first_got, mu_received, second_got, behind_y, material,
            thirds, factors,
        ),
        (basis.shape, basis.shape, square, square),
        flops=0,
        far=3,
        scratch=[
            pltpu.VMEM(basis.shape, F32),
            pltpu.VMEM(basis.shape, F32),
            pltpu.VMEM(square, F32),
            pltpu.SemaphoreType.DMA((3,)),
        ],
    )
    (projected,) = call(
        functools.partial(proj_kernel, total),
        (),
        (inverse, proj, proj_near, far, far_cross),
        (square,),
        flops=0,
    )
    return (
        basis_out.reshape(krylov_basis.shape),
        upper,
        image_out.reshape(krylov_basis.shape),
        projected,
    )


def solution(mesh):
    placed = (P("shift", None, "row", "col", None), P("row", "col", None), P(), P(), P("shift"))
    return jax.shard_map(
        local,
        mesh=mesh,
        in_specs=placed,
        out_specs=(
            P("shift", None, "row", "col", None),
            P("shift", None),
            P("shift", None, "row", "col", None),
            P("shift", None),
        ),
        check_vma=False,
    )
```

```python
import functools

import jax
import jax.numpy as jnp
from jax import lax
from jax.experimental import pallas as pl
from jax.experimental.pallas import tpu as pltpu
from jax.sharding import PartitionSpec as P

F32 = jnp.float32
BF16 = jnp.bfloat16


def halo_ring(rows, back):
    ahead = [((r, 0), (r - 1, 0)) for r in range(1, rows)] + [((0, 0), (0, 1))]
    ahead += [((r, 1), (r + 1, 1)) for r in range(rows - 1)] + [((rows - 1, 1), (rows - 1, 0))]
    pairs = [(2 * r + c, 2 * to_r + to_c) for (r, c), (to_r, to_c) in ahead]
    return [(j, i) for i, j in pairs] if back else pairs


def wide(chunks):
    return jnp.concatenate(chunks, axis=1)


def three(values):
    high = values.astype(BF16)
    rest = values - high.astype(F32)
    middle = rest.astype(BF16)
    low = (rest - middle.astype(F32)).astype(BF16)
    return [high, middle, low]


def inner(left, right):
    return lax.dot_general(
        left, right, (((1,), (1,)), ((), ())), precision=lax.Precision.HIGHEST,
        preferred_element_type=F32,
    )


def product(left, right_thirds):
    rows = left.shape[0]
    high, middle, low = three(left)
    none = jnp.zeros_like(high)
    stacked = jnp.concatenate(
        [wide([high, high, high]), wide([middle, middle, none]), wide([low, none, none])], axis=0
    )
    blocks = lax.dot_general(
        stacked, right_thirds, (((1,), (0,)), ((), ())), preferred_element_type=F32
    )
    return blocks[:rows, :] + (blocks[rows : 2 * rows, :] + blocks[2 * rows :, :])


def table_rows(labels, table_ref):
    result = jnp.zeros(labels.shape, F32)
    for region in range(table_ref.shape[0]):
        result = jnp.where(labels == region, table_ref[region], result)
    return result


def forward_z(values):
    lanes = values.shape[1]
    lane = lax.broadcasted_iota(jnp.int32, values.shape, 1)
    ahead = jnp.where(lane == lanes - 1, 0.0, pltpu.roll(values, lanes - 1, 1))
    return ahead - values


def backward_z(values):
    lane = lax.broadcasted_iota(jnp.int32, values.shape, 1)
    return values - jnp.where(lane == 0, 0.0, pltpu.roll(values, 1, 1))


def part(ref, index, columns):
    return ref[index * columns : (index + 1) * columns, :]


def packed(square):
    half = square.shape[0] // 2
    return jnp.concatenate([square[:half, :], square[half:, :]], axis=1)


def unpacked(pair):
    half = pair.shape[1] // 2
    return jnp.concatenate([pair[:, :half], pair[:, half:]], axis=0)


def first_core():
    return lax.axis_index("col") == 0


def pack_kernel(columns, cells, basis, out_x, out_yz, out_send):
    stride = 3 * cells
    chunks = [basis[pl.ds(k, columns, stride=stride), :] for k in range(stride)]
    down = first_core()
    for y in range(cells):
        e_x, e_y, e_z = chunks[y], chunks[cells + y], chunks[2 * cells + y]
        e_x_up = chunks[y + 1] if y + 1 < cells else jnp.zeros_like(e_x)
        at, other = y * columns, (cells + y) * columns
        out_x[at : at + columns, :] = e_x
        out_yz[at : at + columns, :] = e_y
        out_yz[other : other + columns, :] = e_z
        out_send[at : at + columns, :] = jnp.where(down, e_y, forward_z(e_x) + e_z)
        out_send[other : other + columns, :] = jnp.where(down, e_z, (e_x - e_x_up) - e_y)


def material_kernel(mu_table, eps_table, shift, regions, out):
    labels = regions[...]
    cells = labels.shape[0]
    out[:cells, :] = table_rows(labels, mu_table)
    out[cells:, :] = shift[0] * table_rows(labels, eps_table)


def gram_kernel(columns, cells, field_x, field_yz, out):
    half = columns // 2
    chunks = [part(field_x, k, columns) for k in range(cells)]
    chunks += [part(field_yz, k, columns) for k in range(2 * cells)]
    flat = wide(chunks)
    out[half : half + columns, :] = chunks[0]
    out[half + columns :, :] = chunks[2 * cells]
    out[:half, :] = packed(inner(flat, flat))


def open_kernel(columns, cells, field_x, field_yz, gram_edge, ahead_y, out_open, out_gram):
    half = columns // 2
    out_gram[...] = gram_edge[:half, :] + ahead_y[:half, :]
    inside = first_core()
    for y in range(cells):
        e_x = part(field_x, y, columns)
        if y + 1 < cells:
            e_x_up = part(field_x, y + 1, columns)
        else:
            e_x_up = jnp.where(inside, ahead_y[half : half + columns, :], 0.0)
        e_y, e_z = part(field_yz, y, columns), part(field_yz, cells + y, columns)
        at, other = y * columns, (cells + y) * columns
        out_open[at : at + columns, :] = forward_z(e_x) + e_z
        out_open[other : other + columns, :] = (e_x - e_x_up) - e_y


def near_kernel(
    columns, cells, field_x, field_yz, ahead_y, material, open_yz, out_x, out_proj, out_send,
    out_thirds,
):
    half = columns // 2
    inside = first_core()
    left, right = [], []
    for y in range(cells):
        e_x = part(field_x, y, columns)
        e_y = part(field_yz, y, columns)
        e_z = part(field_yz, cells + y, columns)
        if y + 1 < cells:
            e_z_up = part(field_yz, cells + y + 1, columns)
        else:
            e_z_up = jnp.where(inside, ahead_y[half + columns :, :], 0.0)
        curl_x = (e_z_up - e_z) - forward_z(e_y)
        mu = material[y : y + 1, :]
        eps = -material[cells + y : cells + y + 1, :]
        m_x = mu * curl_x
        open_y, open_z = part(open_yz, y, columns), part(open_yz, cells + y, columns)
        at, other = y * columns, (cells + y) * columns
        out_x[at : at + columns, :] = m_x
        out_send[at : at + columns, :] = jnp.where(inside, open_y, e_y)
        out_send[other : other + columns, :] = jnp.where(inside, open_z, e_z)
        left += [curl_x, e_x, e_y, e_z, open_y, open_z]
        right += [m_x, eps * e_x, eps * e_y, eps * e_z, mu * open_y, mu * open_z]
    fields = [part(field_x, y, columns) for y in range(cells)]
    fields += [part(field_yz, k, columns) for k in range(2 * cells)]
    for i, values in enumerate(three(wide(fields))):
        out_thirds[i * columns : (i + 1) * columns, :] = values
    out_send[2 * cells * columns :, :] = material[...]
    out_proj[...] = packed(inner(wide(left), wide(right)))


def below_top():
    return lax.axis_index("row") + 1 < lax.axis_size("row")


def above_bottom():
    return lax.axis_index("row") > 0


def curl_kernel(
    columns, cells, field_yz, received, mu_received, open_yz, material, m_x, near, out_edge,
    out_proj,
):
    ahead = first_core()
    behind = jnp.logical_and(jnp.logical_not(ahead), above_bottom())
    ahead_here = jnp.logical_and(ahead, below_top())
    left, right = [], []
    for y in range(cells):
        got_y, got_z = part(received, y, columns), part(received, cells + y, columns)
        own_y, own_z = part(field_yz, y, columns), part(field_yz, cells + y, columns)
        open_y, open_z = part(open_yz, y, columns), part(open_yz, cells + y, columns)
        mu_got = jnp.where(behind, mu_received[y : y + 1, :], 0.0)
        mu = jnp.where(ahead, material[y : y + 1, :], mu_got)
        open_y = jnp.where(ahead, open_y, jnp.where(behind, got_y, 0.0))
        open_z = jnp.where(ahead, open_z, jnp.where(behind, got_z, 0.0))
        e_y = jnp.where(ahead, jnp.where(ahead_here, got_y, 0.0), own_y)
        e_z = jnp.where(ahead, jnp.where(ahead_here, got_z, 0.0), own_z)
        left += [e_z, e_y]
        right += [mu * (0.5 * e_z - open_y), mu * (0.5 * e_y + open_z)]
        if y + 1 == cells:
            out_edge[columns:, :] = mu * (open_z + e_y)
    out_edge[:columns, :] = part(m_x, cells - 1, columns)
    crossing = inner(wide(left), wide(right))
    out_proj[...] = near[...] + packed(crossing + crossing.T)


def add_kernel(left, right, out):
    out[...] = left[...] + right[...]


def join_kernel(gram, proj, proj_other, out):
    half = gram.shape[0]
    out[:half, :] = gram[...]
    out[half:, :] = proj[...] + proj_other[...]


def sum_kernel(own, both, out, out_proj):
    half = out_proj.shape[0]
    total = own[...] + both[...]
    out[...] = total
    out_proj[...] = total[half:, :]


def factor(gram):
    columns = gram.shape[0]
    span, tile, width = 2 * columns, 8, 16
    count = columns // tile
    spread = lambda values: jnp.broadcast_to(values, (tile, span))
    sublane = lax.broadcasted_iota(jnp.int32, (tile, span), 0)
    lane = lax.broadcasted_iota(jnp.int32, (tile, span), 1)
    blocks = []
    for b in range(count):
        rows = gram[b * tile : (b + 1) * tile, :]
        rows = jnp.concatenate([rows, jnp.zeros_like(rows)], axis=1)
        blocks.append(jnp.where(lane == sublane + b * tile + columns, 1.0, rows))
    scales = [None] * count
    for start in range(0, columns, width):
        top = start // tile
        panel = [
            {b: spread(blocks[b][:, start + k : start + k + 1]) for b in range(top, count)}
            for k in range(width)
        ]
        for k in range(width):
            at, row = divmod(start + k, tile)
            pivot = spread(panel[k][at][row : row + 1, :])
            inverse = 1.0 / pivot
            ratio = {b: panel[k][b] * inverse for b in range(at, count)}
            ratio[at] = jnp.where(sublane > row, ratio[at], 0.0)
            root = lax.rsqrt(pivot)
            scales[at] = root if row == 0 else jnp.where(sublane == row, root, scales[at])
            for later in range(k + 1, width):
                to, below = divmod(start + later, tile)
                entry = spread(panel[k][to][below : below + 1, :])
                for b in range(at, count):
                    panel[later][b] = panel[later][b] - ratio[b] * entry
            pivot_row = spread(blocks[at][row : row + 1, :])
            for b in range(at, count):
                blocks[b] = blocks[b] - ratio[b] * pivot_row
    kept = []
    for b in range(count):
        row = sublane + b * tile
        kept.append(jnp.where((lane >= row) & (lane <= row + columns), blocks[b] * scales[b], 0.0))
    return jnp.concatenate(kept, axis=0)


def factor_kernel(total, sums, far, out):
    half = sums.shape[0] // 2
    out[...] = factor(unpacked(sums[:half, :] + far[:half, :]) / total)


def basis_kernel(
    columns, cells, total, field_x, field_yz, m_x, open_yz, first_got, mu_received, second_got, behind_y,
    material, thirds_ref, factors,
    out_basis, out_image, out_upper, out_inverse, out_turned, basis, image, upper, sems,
):
    stride = 3 * cells
    inverse = factors[:, columns:]
    out_inverse[...] = inverse
    out_turned[...] = inverse.T / total
    upper[...] = factors[:, :columns]
    third = pltpu.make_async_copy(upper, out_upper, sems.at[2])
    third.start()

    def write(thirds, places, held, target, sem):
        lanes = held.shape[1]
        whole = product(inverse, thirds)
        for i, k in enumerate(places):
            held[pl.ds(k, columns, stride=stride), :] = whole[:, i * lanes : (i + 1) * lanes]
        copy = pltpu.make_async_copy(held, target, sem)
        copy.start()
        return copy

    first_copy = write(thirds_ref[...], range(stride), basis, out_basis, sems.at[0])
    ahead = first_core()
    top, bottom = below_top(), above_bottom()
    scaled_eps = material[cells:, :]
    images, places = [], []
    m_z_down = None
    for y in range(cells):
        e = [part(field_x, y, columns), part(field_yz, y, columns), part(field_yz, cells + y, columns)]
        last = 2 * cells * columns + y
        mu = material[y : y + 1, :]
        first = part(first_got, y, columns), part(first_got, cells + y, columns)
        second = part(second_got, y, columns), part(second_got, cells + y, columns)
        e_y_next = jnp.where(top, jnp.where(ahead, first[0], second[0]), 0.0)
        e_z_next = jnp.where(top, jnp.where(ahead, first[1], second[1]), 0.0)
        m = [
            part(m_x, y, columns),
            mu * (part(open_yz, y, columns) - e_z_next),
            mu * (part(open_yz, cells + y, columns) + e_y_next),
        ]
        if y > 0:
            m_x_down = part(m_x, y - 1, columns)
        else:
            m_x_down = jnp.where(ahead, 0.0, behind_y[:columns, :])
            m_z_down = jnp.where(ahead, 0.0, behind_y[columns:, :])
        mu_last = jnp.where(ahead, second_got[last : last + 1, :], mu_received[y : y + 1, :])
        m_y_last = jnp.where(bottom, mu_last * (jnp.where(ahead, second[0], first[0]) - e[2]), 0.0)
        m_z_last = jnp.where(bottom, mu_last * (jnp.where(ahead, second[1], first[1]) + e[1]), 0.0)
        eps = scaled_eps[y : y + 1, :]
        images += [
            (m[2] - m_z_down) - backward_z(m[1]) - eps * e[0],
            backward_z(m[0]) - (m[2] - m_z_last) - eps * e[1],
            (m[1] - m_y_last) - (m[0] - m_x_down) - eps * e[2],
        ]
        places += [y, cells + y, 2 * cells + y]
        m_z_down = m[2]
    second_copy = write(jnp.concatenate(three(wide(images)), axis=0), places, image, out_image, sems.at[1])
    first_copy.wait()
    second_copy.wait()
    third.wait()


def proj_kernel(inverse, turned, proj, near, far, far_cross, out):
    half = proj.shape[0]
    raw = (proj[...] + near[...]) + (far[half:, :] + far_cross[...])
    left = lax.dot_general(
        inverse[...], unpacked(raw), (((1,), (0,)), ((), ())),
        precision=lax.Precision.HIGHEST, preferred_element_type=F32,
    )
    out[...] = lax.dot_general(
        left, turned[...], (((1,), (0,)), ((), ())), precision=lax.Precision.HIGHEST,
        preferred_element_type=F32,
    )


SMEM = pl.BlockSpec(memory_space=pltpu.SMEM)
VMEM = pl.BlockSpec(memory_space=pltpu.VMEM)
ANY = pl.BlockSpec(memory_space=pl.ANY)


def call(body, scalars, arrays, outs, flops=None, far=0, scratch=()):
    outs = [out if isinstance(out[0], tuple) else (out, F32) for out in outs]
    shapes = [jax.ShapeDtypeStruct(shape, dtype) for shape, dtype in outs]
    cost = None
    if flops is not None:
        cost = pl.CostEstimate(flops=flops, bytes_accessed=0, transcendentals=0)
    return pl.pallas_call(
        body,
        out_shape=shapes,
        in_specs=[SMEM] * len(scalars) + [VMEM] * len(arrays),
        out_specs=[ANY] * far + [VMEM] * (len(shapes) - far),
        scratch_shapes=scratch,
        cost_estimate=cost,
        compiler_params=pltpu.CompilerParams(vmem_limit_bytes=32 * 1024 * 1024),
    )(*scalars, *arrays)


def swapped(x, axis, step):
    return lax.ppermute(x, axis, [(i, i ^ step) for i in range(lax.axis_size(axis))])


def local(krylov_basis, regions, mu_table, eps_table, shift_value):
    columns, parts, layers, cells, lanes = krylov_basis.shape
    rows, cols = lax.axis_size("row"), lax.axis_size("col")
    assert layers == 1 and parts == 3 and cols == 2 and rows >= 8 and rows & (rows - 1) == 0
    total = 3 * cells * lanes * rows * cols
    basis = krylov_basis.reshape(-1, lanes)
    labels = regions[0]
    half, outer = columns // 2, rows // 2
    small, large = (cells * columns, lanes), (2 * cells * columns, lanes)
    edge, pair = (half + 2 * columns, lanes), (half, 2 * columns)
    square = (columns, columns)

    (material,) = call(
        material_kernel, (mu_table, eps_table, shift_value), (labels,), ((2 * cells, lanes),),
        flops=0,
    )
    field_x, field_yz, send = call(
        functools.partial(pack_kernel, columns, cells), (), (basis,), (small, large, large), flops=0
    )
    first_got = lax.ppermute(send, ("row", "col"), halo_ring(rows, False))
    (gram_edge,) = call(
        functools.partial(gram_kernel, columns, cells), (), (field_x, field_yz), (edge,), flops=0
    )
    ahead_y = swapped(gram_edge, "col", 1)
    mu_received = lax.ppermute(material, ("row", "col"), halo_ring(rows, False))
    open_yz, gram = call(
        functools.partial(open_kernel, columns, cells),
        (),
        (field_x, field_yz, gram_edge, ahead_y),
        (large, pair),
        flops=0,
    )
    gram_other = swapped(gram, "row", 2)
    m_x, near, send, thirds = call(
        functools.partial(near_kernel, columns, cells),
        (),
        (field_x, field_yz, ahead_y, material, open_yz),
        (
            small, pair, (2 * cells * (columns + 1), lanes),
            ((3 * columns, 3 * cells * lanes), BF16),
        ),
        flops=0,
    )
    second_got = lax.ppermute(send, ("row", "col"), halo_ring(rows, True))
    edge_m, proj = call(
        functools.partial(curl_kernel, columns, cells),
        (),
        (field_yz, first_got, mu_received, open_yz, material, m_x, near),
        ((2 * columns, lanes), pair),
        flops=10**10,
    )
    (gram,) = call(add_kernel, (), (gram, gram_other), (pair,), flops=10**10)
    proj_other = swapped(proj, "col", 1)
    behind_y = swapped(edge_m, "col", 1)
    both = (2 * half, 2 * columns)
    (own,) = call(join_kernel, (), (gram, proj, proj_other), (both,), flops=0)
    next_both = swapped(own, "row", outer)
    sums, proj = call(sum_kernel, (), (own, next_both), (both, pair), flops=0)
    step = 4
    while step < outer:
        sums = sums + swapped(sums, "row", step)
        proj = sums[half:]
        step *= 2
    far = swapped(sums, "row", 1)
    proj_near = swapped(proj, "row", 2)
    far_cross = swapped(proj, "row", 3)
    (factors,) = call(
        functools.partial(factor_kernel, total), (), (sums, far), ((columns, 2 * columns),), flops=0
    )
    basis_out, image_out, upper, inverse, turned = call(
        functools.partial(basis_kernel, columns, cells, total),
        (),
        (
            field_x, field_yz, m_x, open_yz, first_got, mu_received, second_got, behind_y, material,
            thirds, factors,
        ),
        (basis.shape, basis.shape, square, square, square),
        flops=0,
        far=3,
        scratch=[
            pltpu.VMEM(basis.shape, F32),
            pltpu.VMEM(basis.shape, F32),
            pltpu.VMEM(square, F32),
            pltpu.SemaphoreType.DMA((3,)),
        ],
    )
    (projected,) = call(
        proj_kernel,
        (),
        (inverse, turned, proj, proj_near, far, far_cross),
        (square,),
        flops=0,
    )
    return (
        basis_out.reshape(krylov_basis.shape),
        upper,
        image_out.reshape(krylov_basis.shape),
        projected,
    )


def solution(mesh):
    placed = (P("shift", None, "row", "col", None), P("row", "col", None), P(), P(), P("shift"))
    return jax.shard_map(
        local,
        mesh=mesh,
        in_specs=placed,
        out_specs=(
            P("shift", None, "row", "col", None),
            P("shift", None),
            P("shift", None, "row", "col", None),
            P("shift", None),
        ),
        check_vma=False,
    )
```

```python
import functools

import jax
import jax.numpy as jnp
from jax import lax
from jax.experimental import pallas as pl
from jax.experimental.pallas import tpu as pltpu
from jax.sharding import PartitionSpec as P

F32 = jnp.float32
BF16 = jnp.bfloat16


def halo_ring(rows, back):
    ahead = [((r, 0), (r - 1, 0)) for r in range(1, rows)] + [((0, 0), (0, 1))]
    ahead += [((r, 1), (r + 1, 1)) for r in range(rows - 1)] + [((rows - 1, 1), (rows - 1, 0))]
    pairs = [(2 * r + c, 2 * to_r + to_c) for (r, c), (to_r, to_c) in ahead]
    return [(j, i) for i, j in pairs] if back else pairs


def wide(chunks):
    return jnp.concatenate(chunks, axis=1)


def three(values):
    high = values.astype(BF16)
    rest = values - high.astype(F32)
    middle = rest.astype(BF16)
    low = (rest - middle.astype(F32)).astype(BF16)
    return [high, middle, low]


def inner(left, right):
    return lax.dot_general(
        left, right, (((1,), (1,)), ((), ())), precision=lax.Precision.HIGHEST,
        preferred_element_type=F32,
    )


def product(left, right_thirds):
    rows = left.shape[0]
    high, middle, low = three(left)
    none = jnp.zeros_like(high)
    stacked = jnp.concatenate(
        [wide([high, high, high]), wide([middle, middle, none]), wide([low, none, none])], axis=0
    )
    blocks = lax.dot_general(
        stacked, right_thirds, (((1,), (0,)), ((), ())), preferred_element_type=F32
    )
    return blocks[:rows, :] + (blocks[rows : 2 * rows, :] + blocks[2 * rows :, :])


def table_rows(labels, table_ref):
    result = jnp.zeros(labels.shape, F32)
    for region in range(table_ref.shape[0]):
        result = jnp.where(labels == region, table_ref[region], result)
    return result


def forward_z(values):
    lanes = values.shape[1]
    lane = lax.broadcasted_iota(jnp.int32, values.shape, 1)
    ahead = jnp.where(lane == lanes - 1, 0.0, pltpu.roll(values, lanes - 1, 1))
    return ahead - values


def backward_z(values):
    lane = lax.broadcasted_iota(jnp.int32, values.shape, 1)
    return values - jnp.where(lane == 0, 0.0, pltpu.roll(values, 1, 1))


def part(ref, index, columns):
    return ref[index * columns : (index + 1) * columns, :]


def packed(square):
    half = square.shape[0] // 2
    return jnp.concatenate([square[:half, :], square[half:, :]], axis=1)


def unpacked(pair):
    half = pair.shape[1] // 2
    return jnp.concatenate([pair[:, :half], pair[:, half:]], axis=0)


def first_core():
    return lax.axis_index("col") == 0


def pack_kernel(columns, cells, basis, out_x, out_yz, out_send):
    stride = 3 * cells
    chunks = [basis[pl.ds(k, columns, stride=stride), :] for k in range(stride)]
    down = first_core()
    for y in range(cells):
        e_x, e_y, e_z = chunks[y], chunks[cells + y], chunks[2 * cells + y]
        e_x_up = chunks[y + 1] if y + 1 < cells else jnp.zeros_like(e_x)
        at, other = y * columns, (cells + y) * columns
        out_x[at : at + columns, :] = e_x
        out_yz[at : at + columns, :] = e_y
        out_yz[other : other + columns, :] = e_z
        out_send[at : at + columns, :] = jnp.where(down, e_y, forward_z(e_x) + e_z)
        out_send[other : other + columns, :] = jnp.where(down, e_z, (e_x - e_x_up) - e_y)


def material_kernel(mu_table, eps_table, shift, regions, out):
    labels = regions[...]
    cells = labels.shape[0]
    out[:cells, :] = table_rows(labels, mu_table)
    out[cells:, :] = shift[0] * table_rows(labels, eps_table)


def gram_kernel(columns, cells, field_x, field_yz, out):
    half = columns // 2
    chunks = [part(field_x, k, columns) for k in range(cells)]
    chunks += [part(field_yz, k, columns) for k in range(2 * cells)]
    flat = wide(chunks)
    out[half : half + columns, :] = chunks[0]
    out[half + columns :, :] = chunks[2 * cells]
    out[:half, :] = packed(inner(flat, flat))


def open_kernel(columns, cells, field_x, field_yz, gram_edge, ahead_y, out_open, out_gram):
    half = columns // 2
    out_gram[...] = gram_edge[:half, :] + ahead_y[:half, :]
    inside = first_core()
    for y in range(cells):
        e_x = part(field_x, y, columns)
        if y + 1 < cells:
            e_x_up = part(field_x, y + 1, columns)
        else:
            e_x_up = jnp.where(inside, ahead_y[half : half + columns, :], 0.0)
        e_y, e_z = part(field_yz, y, columns), part(field_yz, cells + y, columns)
        at, other = y * columns, (cells + y) * columns
        out_open[at : at + columns, :] = forward_z(e_x) + e_z
        out_open[other : other + columns, :] = (e_x - e_x_up) - e_y


def near_kernel(
    columns, cells, field_x, field_yz, ahead_y, material, open_yz, out_x, out_proj, out_send,
    out_thirds,
):
    half = columns // 2
    inside = first_core()
    left, right = [], []
    for y in range(cells):
        e_x = part(field_x, y, columns)
        e_y = part(field_yz, y, columns)
        e_z = part(field_yz, cells + y, columns)
        if y + 1 < cells:
            e_z_up = part(field_yz, cells + y + 1, columns)
        else:
            e_z_up = jnp.where(inside, ahead_y[half + columns :, :], 0.0)
        curl_x = (e_z_up - e_z) - forward_z(e_y)
        mu = material[y : y + 1, :]
        eps = -material[cells + y : cells + y + 1, :]
        m_x = mu * curl_x
        open_y, open_z = part(open_yz, y, columns), part(open_yz, cells + y, columns)
        at, other = y * columns, (cells + y) * columns
        out_x[at : at + columns, :] = m_x
        out_send[at : at + columns, :] = jnp.where(inside, open_y, e_y)
        out_send[other : other + columns, :] = jnp.where(inside, open_z, e_z)
        left += [curl_x, e_x, e_y, e_z, open_y, open_z]
        right += [m_x, eps * e_x, eps * e_y, eps * e_z, mu * open_y, mu * open_z]
    fields = [part(field_x, y, columns) for y in range(cells)]
    fields += [part(field_yz, k, columns) for k in range(2 * cells)]
    for i, values in enumerate(three(wide(fields))):
        out_thirds[i * columns : (i + 1) * columns, :] = values
    out_send[2 * cells * columns :, :] = material[...]
    out_proj[...] = packed(inner(wide(left), wide(right)))


def below_top():
    return lax.axis_index("row") + 1 < lax.axis_size("row")


def above_bottom():
    return lax.axis_index("row") > 0


def curl_kernel(
    columns, cells, field_yz, received, mu_received, open_yz, material, m_x, near, out_edge,
    out_proj,
):
    ahead = first_core()
    behind = jnp.logical_and(jnp.logical_not(ahead), above_bottom())
    ahead_here = jnp.logical_and(ahead, below_top())
    left, right = [], []
    for y in range(cells):
        got_y, got_z = part(received, y, columns), part(received, cells + y, columns)
        own_y, own_z = part(field_yz, y, columns), part(field_yz, cells + y, columns)
        open_y, open_z = part(open_yz, y, columns), part(open_yz, cells + y, columns)
        mu_got = jnp.where(behind, mu_received[y : y + 1, :], 0.0)
        mu = jnp.where(ahead, material[y : y + 1, :], mu_got)
        open_y = jnp.where(ahead, open_y, jnp.where(behind, got_y, 0.0))
        open_z = jnp.where(ahead, open_z, jnp.where(behind, got_z, 0.0))
        e_y = jnp.where(ahead, jnp.where(ahead_here, got_y, 0.0), own_y)
        e_z = jnp.where(ahead, jnp.where(ahead_here, got_z, 0.0), own_z)
        left += [e_z, e_y]
        right += [mu * (0.5 * e_z - open_y), mu * (0.5 * e_y + open_z)]
        if y + 1 == cells:
            out_edge[columns:, :] = mu * (open_z + e_y)
    out_edge[:columns, :] = part(m_x, cells - 1, columns)
    crossing = inner(wide(left), wide(right))
    out_proj[...] = near[...] + packed(crossing + crossing.T)


def add_kernel(left, right, out):
    out[...] = left[...] + right[...]


def join_kernel(gram, proj, proj_other, out):
    half = gram.shape[0]
    out[:half, :] = gram[...]
    out[half:, :] = proj[...] + proj_other[...]


def sum_kernel(own, both, out, out_proj):
    half = out_proj.shape[0]
    total = own[...] + both[...]
    out[...] = total
    out_proj[...] = total[half:, :]


def factor(gram):
    columns = gram.shape[0]
    span, tile, width = 2 * columns, 8, 16
    count = columns // tile
    spread = lambda values: jnp.broadcast_to(values, (tile, span))
    sublane = lax.broadcasted_iota(jnp.int32, (tile, span), 0)
    lane = lax.broadcasted_iota(jnp.int32, (tile, span), 1)
    blocks = []
    for b in range(count):
        rows = gram[b * tile : (b + 1) * tile, :]
        rows = jnp.concatenate([rows, jnp.zeros_like(rows)], axis=1)
        blocks.append(jnp.where(lane == sublane + b * tile + columns, 1.0, rows))
    scales = [None] * count
    for start in range(0, columns, width):
        top = start // tile
        panel = [
            {b: spread(blocks[b][:, start + k : start + k + 1]) for b in range(top, count)}
            for k in range(width)
        ]
        for k in range(width):
            at, row = divmod(start + k, tile)
            pivot = spread(panel[k][at][row : row + 1, :])
            inverse = 1.0 / pivot
            ratio = {b: panel[k][b] * inverse for b in range(at, count)}
            ratio[at] = jnp.where(sublane > row, ratio[at], 0.0)
            root = lax.rsqrt(pivot)
            scales[at] = root if row == 0 else jnp.where(sublane == row, root, scales[at])
            for later in range(k + 1, width):
                to, below = divmod(start + later, tile)
                entry = spread(panel[k][to][below : below + 1, :])
                for b in range(at, count):
                    panel[later][b] = panel[later][b] - ratio[b] * entry
            pivot_row = spread(blocks[at][row : row + 1, :])
            for b in range(at, count):
                blocks[b] = blocks[b] - ratio[b] * pivot_row
    kept = []
    for b in range(count):
        row = sublane + b * tile
        kept.append(jnp.where((lane >= row) & (lane <= row + columns), blocks[b] * scales[b], 0.0))
    return jnp.concatenate(kept, axis=0)


def factor_kernel(total, sums, far, out):
    half = sums.shape[0] // 2
    both = factor(unpacked(sums[:half, :] + far[:half, :]))
    lane = lax.broadcasted_iota(jnp.int32, both.shape, 1)
    root = float(total) ** 0.5
    out[...] = both * jnp.where(lane < both.shape[0], 1.0 / root, root)


def basis_kernel(
    columns, cells, field_x, field_yz, m_x, open_yz, first_got, mu_received, second_got, behind_y,
    material, thirds_ref, factors,
    out_basis, out_image, out_upper, out_inverse, basis, image, upper, sems,
):
    stride = 3 * cells
    inverse = factors[:, columns:]
    out_inverse[...] = inverse
    upper[...] = factors[:, :columns]
    third = pltpu.make_async_copy(upper, out_upper, sems.at[2])
    third.start()

    def write(thirds, places, held, target, sem):
        lanes = held.shape[1]
        whole = product(inverse, thirds)
        for i, k in enumerate(places):
            held[pl.ds(k, columns, stride=stride), :] = whole[:, i * lanes : (i + 1) * lanes]
        copy = pltpu.make_async_copy(held, target, sem)
        copy.start()
        return copy

    first_copy = write(thirds_ref[...], range(stride), basis, out_basis, sems.at[0])
    ahead = first_core()
    top, bottom = below_top(), above_bottom()
    scaled_eps = material[cells:, :]
    images, places = [], []
    m_z_down = None
    for y in range(cells):
        e = [part(field_x, y, columns), part(field_yz, y, columns), part(field_yz, cells + y, columns)]
        last = 2 * cells * columns + y
        mu = material[y : y + 1, :]
        first = part(first_got, y, columns), part(first_got, cells + y, columns)
        second = part(second_got, y, columns), part(second_got, cells + y, columns)
        e_y_next = jnp.where(top, jnp.where(ahead, first[0], second[0]), 0.0)
        e_z_next = jnp.where(top, jnp.where(ahead, first[1], second[1]), 0.0)
        m = [
            part(m_x, y, columns),
            mu * (part(open_yz, y, columns) - e_z_next),
            mu * (part(open_yz, cells + y, columns) + e_y_next),
        ]
        if y > 0:
            m_x_down = part(m_x, y - 1, columns)
        else:
            m_x_down = jnp.where(ahead, 0.0, behind_y[:columns, :])
            m_z_down = jnp.where(ahead, 0.0, behind_y[columns:, :])
        mu_last = jnp.where(ahead, second_got[last : last + 1, :], mu_received[y : y + 1, :])
        m_y_last = jnp.where(bottom, mu_last * (jnp.where(ahead, second[0], first[0]) - e[2]), 0.0)
        m_z_last = jnp.where(bottom, mu_last * (jnp.where(ahead, second[1], first[1]) + e[1]), 0.0)
        eps = scaled_eps[y : y + 1, :]
        images += [
            (m[2] - m_z_down) - backward_z(m[1]) - eps * e[0],
            backward_z(m[0]) - (m[2] - m_z_last) - eps * e[1],
            (m[1] - m_y_last) - (m[0] - m_x_down) - eps * e[2],
        ]
        places += [y, cells + y, 2 * cells + y]
        m_z_down = m[2]
    second_copy = write(jnp.concatenate(three(wide(images)), axis=0), places, image, out_image, sems.at[1])
    first_copy.wait()
    second_copy.wait()
    third.wait()


def proj_kernel(total, inverse, proj, near, far, far_cross, out):
    half = proj.shape[0]
    raw = (proj[...] + near[...]) + (far[half:, :] + far_cross[...])
    left = lax.dot_general(
        inverse[...], unpacked(raw) / total, (((1,), (0,)), ((), ())),
        precision=lax.Precision.HIGHEST, preferred_element_type=F32,
    )
    out[...] = inner(left, inverse[...])


SMEM = pl.BlockSpec(memory_space=pltpu.SMEM)
VMEM = pl.BlockSpec(memory_space=pltpu.VMEM)
ANY = pl.BlockSpec(memory_space=pl.ANY)


def call(body, scalars, arrays, outs, flops=None, far=0, scratch=()):
    outs = [out if isinstance(out[0], tuple) else (out, F32) for out in outs]
    shapes = [jax.ShapeDtypeStruct(shape, dtype) for shape, dtype in outs]
    cost = None
    if flops is not None:
        cost = pl.CostEstimate(flops=flops, bytes_accessed=0, transcendentals=0)
    return pl.pallas_call(
        body,
        out_shape=shapes,
        in_specs=[SMEM] * len(scalars) + [VMEM] * len(arrays),
        out_specs=[ANY] * far + [VMEM] * (len(shapes) - far),
        scratch_shapes=scratch,
        cost_estimate=cost,
        compiler_params=pltpu.CompilerParams(vmem_limit_bytes=32 * 1024 * 1024),
    )(*scalars, *arrays)


def swapped(x, axis, step):
    return lax.ppermute(x, axis, [(i, i ^ step) for i in range(lax.axis_size(axis))])


def local(krylov_basis, regions, mu_table, eps_table, shift_value):
    columns, parts, layers, cells, lanes = krylov_basis.shape
    rows, cols = lax.axis_size("row"), lax.axis_size("col")
    assert layers == 1 and parts == 3 and cols == 2 and rows >= 8 and rows & (rows - 1) == 0
    total = 3 * cells * lanes * rows * cols
    basis = krylov_basis.reshape(-1, lanes)
    labels = regions[0]
    half, outer = columns // 2, rows // 2
    small, large = (cells * columns, lanes), (2 * cells * columns, lanes)
    edge, pair = (half + 2 * columns, lanes), (half, 2 * columns)
    square = (columns, columns)

    (material,) = call(
        material_kernel, (mu_table, eps_table, shift_value), (labels,), ((2 * cells, lanes),),
        flops=0,
    )
    field_x, field_yz, send = call(
        functools.partial(pack_kernel, columns, cells), (), (basis,), (small, large, large), flops=0
    )
    first_got = lax.ppermute(send, ("row", "col"), halo_ring(rows, False))
    (gram_edge,) = call(
        functools.partial(gram_kernel, columns, cells), (), (field_x, field_yz), (edge,), flops=0
    )
    ahead_y = swapped(gram_edge, "col", 1)
    mu_received = lax.ppermute(material, ("row", "col"), halo_ring(rows, False))
    open_yz, gram = call(
        functools.partial(open_kernel, columns, cells),
        (),
        (field_x, field_yz, gram_edge, ahead_y),
        (large, pair),
        flops=0,
    )
    gram_other = swapped(gram, "row", 2)
    m_x, near, send, thirds = call(
        functools.partial(near_kernel, columns, cells),
        (),
        (field_x, field_yz, ahead_y, material, open_yz),
        (
            small, pair, (2 * cells * (columns + 1), lanes),
            ((3 * columns, 3 * cells * lanes), BF16),
        ),
        flops=0,
    )
    second_got = lax.ppermute(send, ("row", "col"), halo_ring(rows, True))
    edge_m, proj = call(
        functools.partial(curl_kernel, columns, cells),
        (),
        (field_yz, first_got, mu_received, open_yz, material, m_x, near),
        ((2 * columns, lanes), pair),
        flops=10**10,
    )
    (gram,) = call(add_kernel, (), (gram, gram_other), (pair,), flops=10**10)
    proj_other = swapped(proj, "col", 1)
    behind_y = swapped(edge_m, "col", 1)
    both = (2 * half, 2 * columns)
    (own,) = call(join_kernel, (), (gram, proj, proj_other), (both,), flops=0)
    next_both = swapped(own, "row", outer)
    sums, proj = call(sum_kernel, (), (own, next_both), (both, pair), flops=0)
    step = 4
    while step < outer:
        sums = sums + swapped(sums, "row", step)
        proj = sums[half:]
        step *= 2
    far = swapped(sums, "row", 1)
    proj_near = swapped(proj, "row", 2)
    far_cross = swapped(proj, "row", 3)
    (factors,) = call(
        functools.partial(factor_kernel, total), (), (sums, far), ((columns, 2 * columns),), flops=0
    )
    basis_out, image_out, upper, inverse = call(
        functools.partial(basis_kernel, columns, cells),
        (),
        (
            field_x, field_yz, m_x, open_yz, first_got, mu_received, second_got, behind_y, material,
            thirds, factors,
        ),
        (basis.shape, basis.shape, square, square),
        flops=0,
        far=3,
        scratch=[
            pltpu.VMEM(basis.shape, F32),
            pltpu.VMEM(basis.shape, F32),
            pltpu.VMEM(square, F32),
            pltpu.SemaphoreType.DMA((3,)),
        ],
    )
    (projected,) = call(
        functools.partial(proj_kernel, total),
        (),
        (inverse, proj, proj_near, far, far_cross),
        (square,),
        flops=0,
    )
    return (
        basis_out.reshape(krylov_basis.shape),
        upper,
        image_out.reshape(krylov_basis.shape),
        projected,
    )


def solution(mesh):
    placed = (P("shift", None, "row", "col", None), P("row", "col", None), P(), P(), P("shift"))
    return jax.shard_map(
        local,
        mesh=mesh,
        in_specs=placed,
        out_specs=(
            P("shift", None, "row", "col", None),
            P("shift", None),
            P("shift", None, "row", "col", None),
            P("shift", None),
        ),
        check_vma=False,
    )
```
